32 devices in a mesh: dp: 8 (over z, y), mp: 4 (over x, core).
Axes of the slice: x: 2, y: 2, z: 4, core: 2. Of those that a mesh axis runs over, the one named last changes fastest.
Arguments:
- inputs: bfloat16 [9216, 2304], P('dp', 'mp'), may hold values from -6 to 6
- lengths: int32 [8], P('dp'), may hold values from 896 to 1152, as said below
- start_cell: float32 [8, 2304], P('dp', 'mp'), may hold values from -6 to 6
- weight: bfloat16 [2, 2304, 3, 2304], P(None, None, None, 'mp'), may hold values from -0.09375 to 0.09375
- bias: bfloat16 [3, 2304], P(None, 'mp'), may hold values from -1 to 7
- out_grad: bfloat16 [9216, 2304], P('dp', 'mp'), may hold values from -6 to 6
- cell_grad: float32 [8, 2304], P('dp', 'mp'), may hold values from -6 to 6
Outputs:
- hidden: bfloat16 [9216, 2304], P('dp', 'mp')
- last_cell: float32 [8, 2304], P('dp', 'mp')
- input_grad: bfloat16 [9216, 2304], P('dp', 'mp')
- start_grad: float32 [8, 2304], P('dp', 'mp')
- weight_grad: float32 [2, 2304, 3, 2304], P(None, None, None, 'mp')
- bias_grad: float32 [3, 2304], P(None, 'mp')
The draws below stay inside these ranges and needn't reach their ends.
Inputs may be any that keep to these rules, and one draw needn't show every extreme that they name: `lengths`: each length is 896, 1024 or 1152; every draw has a window of 1152 and one of 896.
All inputs are finite; a program needn't handle non-finite values.
Results may differ from the reference program's by a relative error of at most 0.0049.
Values may be sent and summed in bfloat16 or wider, within the bound.
No kernel may reach another device: no remote copies, remote signals or barrier semaphores. Data moves between devices by JAX's collectives and lax.ppermute only.
A program may use at most 192 MiB of HBM per device.

```python
import jax
import jax.numpy as jnp
from jax import lax

D = 2304
LMAX = 1152
STEP = 128
WINDOWS = 8
TOKENS = 9216


def draw_lengths(key, part):
    key = jax.random.fold_in(key, 11)
    key_list = jax.random.split(key, 3)
    level_index = jax.random.randint(key_list[0], (WINDOWS,), 0, 3)
    window_lengths = LMAX - STEP * (2 - level_index)
    longest = jax.random.randint(key_list[1], (), 0, WINDOWS)
    gap_length = jax.random.randint(key_list[2], (), 1, WINDOWS)
    shortest = (longest + gap_length) % WINDOWS
    window_lengths = window_lengths.at[longest].set(LMAX).at[shortest].set(LMAX - 2 * STEP)
    return window_lengths.astype(jnp.int32)


def draw_bias(key, part):
    key = jax.random.fold_in(key, 12)
    key_list = jax.random.split(key, 2)
    others = jax.random.uniform(key_list[0], (3, D), jnp.float32, -1.0, 1.0)
    forget_bias = jax.random.uniform(key_list[1], (D,), jnp.float32, 1.0, 7.0)
    return others.at[1].set(forget_bias).astype(jnp.bfloat16)


def levels(rng, extent, cuts, low, largest):
    def one(position, parts):
        draws = jax.random.uniform(jax.random.fold_in(jax.random.fold_in(rng, 6), position), (parts,), jnp.float32, low / len(cuts), largest / len(cuts))
        return jnp.repeat(jnp.exp(draws), extent[position] // parts).reshape((-1,) + (1,) * (len(extent) - position - 1))

    loudness = one(*cuts[0])
    for cut in cuts[1:]:
        loudness = loudness * one(*cut)
    return loudness


def noise(rng, dims, deviation, most, cuts=(), held_as=jnp.bfloat16):
    values = jax.random.normal(rng, dims, jnp.float32) * deviation
    if len(cuts) > 0:
        values = levels(rng, dims, cuts, -0.22, 0.18) * values
    return jnp.clip(values, min=-most, max=most).astype(held_as)


def setup_inputs(seed: int = 0) -> dict:
    keys = jax.random.split(jax.random.key(seed), 8)
    return {
        "inputs": noise(keys[0], (TOKENS, D), 1.0, 6.0, ((0, 8), (1, 4))),
        "lengths": draw_lengths(jax.random.fold_in(keys[7], 71), 0),
        "start_cell": noise(keys[2], (WINDOWS, D), 1.0, 6.0, ((0, 8), (1, 4)), jnp.float32),
        "weight": noise(keys[3], (2, D, 3, D), (2 * D) ** -0.5, 0.09375, ((3, 4),)),
        "bias": draw_bias(jax.random.fold_in(keys[7], 71), 0),
        "out_grad": noise(keys[5], (TOKENS, D), 1.0, 6.0, ((0, 8), (1, 4))),
        "cell_grad": noise(keys[6], (WINDOWS, D), 1.0, 6.0, ((0, 8), (1, 4)), jnp.float32),
    }


@jax.custom_vjp
def low(v):
    return lax.optimization_barrier(v.astype(jnp.bfloat16)).astype(jnp.float32)

@jax.custom_vjp
def low_back(v):
    return v

def low_keep(v):
    return (low(v), None)

def low_pass(kept, grad):
    return (grad,)

def back_keep(v):
    return (v, None)

def back_low(kept, grad):
    return (low(grad),)
low.defvjp(low_keep, low_pass)
low_back.defvjp(back_keep, back_low)

def block_run(cell_value, pair_block):

    def single_step(state_now, pair_now):
        updated = pair_now[0] * state_now + pair_now[1]
        return (updated, updated)
    return lax.scan(single_step, cell_value, pair_block)

def pooled(input_block, weight_full, bias_full, start_block, live_block):
    shifted = jnp.concatenate([jnp.zeros_like(input_block[:, :1]), input_block[:, :-1]], axis=1)
    gates = jnp.einsum('gld,dke->glke', input_block, weight_full[0], precision=lax.Precision.HIGHEST)
    gates = gates + jnp.einsum('gld,dke->glke', shifted, weight_full[1], precision=lax.Precision.HIGHEST)
    gates = low_back(gates + bias_full)
    candidate = jnp.tanh(gates[:, :, 0])
    forget_gate = jax.nn.sigmoid(gates[:, :, 1])
    output_gate = jax.nn.sigmoid(gates[:, :, 2])
    live_mask = live_block[:, :, None]
    decay_rate = 1.0 - live_mask * (1.0 - forget_gate)
    new_input = live_mask * (1.0 - forget_gate) * candidate
    group_count, win_span, width_all = candidate.shape
    decay_time = jnp.transpose(decay_rate, (1, 0, 2)).reshape(9, win_span // 9, group_count, width_all)
    input_time = jnp.transpose(new_input, (1, 0, 2)).reshape(9, win_span // 9, group_count, width_all)
    final_cell, cell_states = lax.scan(jax.checkpoint(block_run), start_block, (decay_time, input_time))
    cell_states = jnp.transpose(cell_states.reshape(win_span, group_count, width_all), (1, 0, 2))
    return (live_mask * output_gate * cell_states, final_cell)

def reference(inputs, lengths, start_cell, weight, bias, out_grad, cell_grad):
    pair_count = WINDOWS // 2
    input_float = inputs.astype(jnp.float32).reshape(pair_count, 2, LMAX, D)
    weight_float = weight.astype(jnp.float32)
    bias_float = bias.astype(jnp.float32)
    positions = jnp.arange(LMAX, dtype=jnp.int32)
    live_all = (positions[None, :] < lengths[:, None]).astype(jnp.float32).reshape(pair_count, 2, LMAX)
    start_pairs = start_cell.astype(jnp.float32).reshape(pair_count, 2, D)
    hidden_grads = out_grad.astype(jnp.float32).reshape(pair_count, 2, LMAX, D)
    final_grads = cell_grad.astype(jnp.float32).reshape(pair_count, 2, D)

    def group_pass(totals, group_data):
        input_block, live_block, start_block, hidden_block, final_block = group_data

        def forward(input_value, weight_value, bias_value, start_value):
            return pooled(input_value, weight_value, bias_value, start_value, live_block)
        results, pull_back = jax.vjp(forward, input_block, weight_float, bias_float, start_block)
        grad_input, grad_weight, grad_bias, grad_start = pull_back((hidden_block, final_block))
        new_totals = (totals[0] + grad_weight, totals[1] + grad_bias)
        return (new_totals, (results[0].astype(jnp.bfloat16), results[1], grad_input.astype(jnp.bfloat16), grad_start))
    init_totals = (jnp.zeros((2, D, 3, D), jnp.float32), jnp.zeros((3, D), jnp.float32))
    grad_totals, outputs = lax.scan(group_pass, init_totals, (input_float, live_all, start_pairs, hidden_grads, final_grads))
    hidden_out, final_out, input_out, start_out = outputs
    return (hidden_out.reshape(TOKENS, D), final_out.reshape(WINDOWS, D), input_out.reshape(TOKENS, D), start_out.reshape(WINDOWS, D), grad_totals[0], grad_totals[1])
```

```python
import functools

import jax
import jax.numpy as jnp
from jax import lax
from jax.experimental import pallas as pl
from jax.experimental.pallas import tpu as pltpu
from jax.sharding import PartitionSpec as P

LANES = 128
ROWS = 16


def pool_kernel(length_ref, gates_ref, small_ref, grad_ref, hidden_ref, sums_ref, gg_ref):
    span = grad_ref.shape[-1]
    tiles = span // LANES
    length = length_ref[0]
    lane = lax.broadcasted_iota(jnp.int32, (ROWS, LANES), 1)
    zero = jnp.zeros((ROWS, LANES), jnp.float32)

    def block(step, unused):
        row = pl.multiple_of(step * ROWS, ROWS)
        rows = pl.ds(row, ROWS)
        small = small_ref[rows, :]

        def column(index):
            return jnp.broadcast_to(small[:, index : index + 1], (ROWS, LANES))

        bias = [column(k) for k in range(3)]
        carry = column(3)
        ahead_last = [zero] * 3
        cand, forget, keep, out_gate, live, decay, cell, before = ([] for _ in range(8))
        for j in range(tiles):
            cols = pl.ds(j * LANES, LANES)
            gates = []
            for k in range(3):
                later = pltpu.roll(gates_ref[1, k, rows, cols], 1, 1)
                gates.append(
                    gates_ref[0, k, rows, cols]
                    + jnp.where(lane == 0, ahead_last[k], later)
                    + bias[k]
                )
                ahead_last[k] = later
            alive = (lane + j * LANES < length).astype(jnp.float32)
            c = jnp.tanh(gates[0])
            f = jax.nn.sigmoid(gates[1])
            o = jax.nn.sigmoid(gates[2])
            kept = alive * (1.0 - f)
            d = 1.0 - kept
            product, total = d, kept * c
            for k in (1, 2, 4, 8, 16, 32, 64):
                inside = lane >= k
                total = total + product * jnp.where(inside, pltpu.roll(total, k, 1), 0.0)
                product = product * jnp.where(inside, pltpu.roll(product, k, 1), 1.0)
            total = total + product * carry
            moved = pltpu.roll(total, 1, 1)
            before.append(jnp.where(lane == 0, carry, moved))
            carry = jnp.broadcast_to(total[:, LANES - 1 :], (ROWS, LANES))
            cand.append(c)
            forget.append(f)
            keep.append(kept)
            out_gate.append(o)
            live.append(alive)
            decay.append(d)
            cell.append(total)
        last_cell = carry[:, :1]
        carry = zero
        decay_next = zero
        first_next = [zero] * 3
        bias_sum = [zero] * 3
        for j in range(tiles - 1, -1, -1):
            cols = pl.ds(j * LANES, LANES)
            grad = grad_ref[rows, cols].astype(jnp.float32)
            lo = live[j] * out_gate[j]
            emitted = lo * grad
            if j == tiles - 1:
                emitted = emitted + jnp.where(lane == LANES - 1, column(4), 0.0)
            hidden_ref[rows, cols] = (lo * cell[j]).astype(jnp.bfloat16)
            back = pltpu.roll(decay[j], LANES - 1, 1)
            product = jnp.where(lane == LANES - 1, decay_next, back)
            decay_next = back
            total = emitted
            for k in (1, 2, 4, 8, 16, 32, 64):
                inside = lane < LANES - k
                total = total + product * jnp.where(inside, pltpu.roll(total, LANES - k, 1), 0.0)
                product = product * jnp.where(inside, pltpu.roll(product, LANES - k, 1), 1.0)
            total = total + product * carry
            carry = jnp.broadcast_to(total[:, :1], (ROWS, LANES))
            shared = total * keep[j]
            outs = [
                shared * (1.0 - cand[j] * cand[j]),
                shared * (before[j] - cand[j]) * forget[j],
                emitted * cell[j] * (1.0 - out_gate[j])
                if j < tiles - 1
                else lo * grad * cell[j] * (1.0 - out_gate[j]),
            ]
            for k in range(3):
                rounded = outs[k].astype(jnp.bfloat16)
                gg_ref[0, k, rows, cols] = rounded
                wide = rounded.astype(jnp.float32)
                bias_sum[k] = bias_sum[k] + wide
                moved = pltpu.roll(wide, LANES - 1, 1)
                gg_ref[1, k, rows, cols] = jnp.where(
                    lane == LANES - 1, first_next[k], moved
                ).astype(jnp.bfloat16)
                first_next[k] = moved
        start_grad = decay[0][:, :1] * carry[:, :1]
        columns = [last_cell, start_grad] + [
            jnp.sum(s, axis=1, keepdims=True) for s in bias_sum
        ]
        answer = zero
        for index, value in enumerate(columns):
            answer = jnp.where(lane == index, jnp.broadcast_to(value, (ROWS, LANES)), answer)
        sums_ref[rows, :] = answer
        return unused

    lax.fori_loop(0, grad_ref.shape[0] // ROWS, block, 0)


def pool(length, gates, small, grad):
    taps, kinds, width, span = gates.shape
    part = 48
    return pl.pallas_call(
        pool_kernel,
        grid=(width // part,),
        in_specs=[
            pl.BlockSpec(memory_space=pltpu.SMEM),
            pl.BlockSpec((2, 3, part, span), lambda i: (0, 0, i, 0)),
            pl.BlockSpec((part, LANES), lambda i: (i, 0)),
            pl.BlockSpec((part, span), lambda i: (i, 0)),
        ],
        out_specs=[
            pl.BlockSpec((part, span), lambda i: (i, 0)),
            pl.BlockSpec((part, LANES), lambda i: (i, 0)),
            pl.BlockSpec((2, 3, part, span), lambda i: (0, 0, i, 0)),
        ],
        out_shape=[
            jax.ShapeDtypeStruct((width, span), jnp.bfloat16),
            jax.ShapeDtypeStruct((width, LANES), jnp.float32),
            jax.ShapeDtypeStruct((2, 3, width, span), jnp.bfloat16),
        ],
        compiler_params=pltpu.CompilerParams(vmem_limit_bytes=40 * 2**20),
        cost_estimate=pl.CostEstimate(
            flops=150 * width * span, bytes_accessed=48 * width * span, transcendentals=6 * width * span
        ),
        name="pool",
    )(length, gates, small, grad)


def small_columns(bias, start_cell, cell_grad):
    stacked = jnp.concatenate([bias.astype(jnp.float32), start_cell, cell_grad], axis=0)
    return jnp.pad(stacked.T, ((0, 0), (0, LANES - 5)))


def on_device(inputs, lengths, start_cell, weight, bias, out_grad, cell_grad):
    span, width = inputs.shape
    depth = weight.shape[1]
    x_own = inputs.T
    w_rows = jnp.transpose(weight, (0, 2, 3, 1))
    x_all = lax.all_gather(x_own, "mp", axis=0, tiled=True)
    w_flat = w_rows.reshape(6 * width, depth)
    gates = jnp.dot(w_flat, x_all, preferred_element_type=jnp.float32)
    small = small_columns(bias, start_cell, cell_grad)
    hidden, sums, gg = pool(lengths, gates.reshape(2, 3, width, span), small, out_grad.T)
    gg = gg.reshape(6 * width, span)
    back = lax.dot_general(w_flat, gg, (((0,), (0,)), ((), ())), preferred_element_type=jnp.float32)
    input_grad = lax.psum_scatter(
        back.astype(jnp.bfloat16), "mp", scatter_dimension=0, tiled=True
    )
    wgrad = lax.dot_general(gg, x_all, (((1,), (1,)), ((), ())), preferred_element_type=jnp.float32)
    wgrad = lax.psum(wgrad.astype(jnp.bfloat16), "dp").astype(jnp.float32)
    bias_grad = lax.psum(sums[:, 2:5].T, "dp")
    return (
        hidden.T,
        sums[:, 0:1].T,
        input_grad.T,
        sums[:, 1:2].T,
        jnp.transpose(wgrad.reshape(2, 3, width, depth), (0, 3, 1, 2)),
        bias_grad,
    )


def solution(mesh):
    in_specs = (
        P("dp", "mp"),
        P("dp"),
        P("dp", "mp"),
        P(None, None, None, "mp"),
        P(None, "mp"),
        P("dp", "mp"),
        P("dp", "mp"),
    )
    out_specs = (
        P("dp", "mp"),
        P("dp", "mp"),
        P("dp", "mp"),
        P("dp", "mp"),
        P(None, None, None, "mp"),
        P(None, "mp"),
    )
    return jax.shard_map(
        on_device, mesh=mesh, in_specs=in_specs, out_specs=out_specs, check_vma=False
    )
```

```python
import functools

import jax
import jax.numpy as jnp
from jax import lax
from jax.experimental import pallas as pl
from jax.experimental.pallas import tpu as pltpu
from jax.sharding import PartitionSpec as P

LANES = 128
ROWS = 16
CHUNKS = 18
LAG = 4
HIDDEN_COST = pl.CostEstimate(flops=1, bytes_accessed=1, transcendentals=0)


def pool_kernel(length_ref, gates_ref, small_ref, grad_ref, hidden_ref, sums_ref, gg_ref, held):
    part, span = grad_ref.shape
    tiles = span // LANES
    length = length_ref[0]
    lane = lax.broadcasted_iota(jnp.int32, (ROWS, LANES), 1)
    zero = jnp.zeros((ROWS, LANES), jnp.float32)
    one = zero + 1.0
    first_lane = lane == 0
    last_lane = lane == LANES - 1
    cand_at, forget_at, out_at = 0, 1, 2
    run_at, back_at, decay_at = 0, 1, 2
    held_gates, held_runs = held

    def tile_of(j):
        return pl.ds(j * LANES, LANES)

    def is_live(j):
        return lane * tiles + j < length

    def local(step, unused):
        rows = pl.ds(pl.multiple_of(step * ROWS, ROWS), ROWS)
        small = small_ref[rows, :]
        bias = [jnp.broadcast_to(small[:, k : k + 1], (ROWS, LANES)) for k in range(3)]
        end_grad = jnp.where(last_lane, jnp.broadcast_to(small[:, 4:5], (ROWS, LANES)), 0.0)
        earlier = [
            jnp.where(first_lane, 0.0, pltpu.roll(gates_ref[1, k, rows, tile_of(tiles - 1)], 1, 1))
            for k in range(3)
        ]
        run, product, back = zero, one, zero
        for j in range(tiles):
            gates = []
            for k in range(3):
                gates.append(gates_ref[0, k, rows, tile_of(j)] + earlier[k] + bias[k])
                earlier[k] = gates_ref[1, k, rows, tile_of(j)]
            live = is_live(j)
            cand = jnp.tanh(gates[0])
            forget = jax.nn.sigmoid(gates[1])
            out_gate = jnp.where(live, jax.nn.sigmoid(gates[2]), 0.0)
            kept = jnp.where(live, 1.0 - forget, 0.0)
            decay = 1.0 - kept
            emitted = out_gate * grad_ref[rows, tile_of(j)].astype(jnp.float32)
            if j == tiles - 1:
                emitted = emitted + end_grad
            run = decay * run + kept * cand
            product = product * decay
            back = back + product * emitted
            held_gates[cand_at, rows, tile_of(j)] = cand
            held_gates[forget_at, rows, tile_of(j)] = forget
            held_gates[out_at, rows, tile_of(j)] = out_gate
        held_runs[run_at, rows, :] = run
        held_runs[back_at, rows, :] = back
        held_runs[decay_at, rows, :] = product
        return unused

    lax.fori_loop(0, part // ROWS, local, 0)

    wide = lax.broadcasted_iota(jnp.int32, (part, LANES), 1)
    begin = jnp.broadcast_to(small_ref[:, 3:4], (part, LANES))
    run, back, product = held_runs[run_at], held_runs[back_at], held_runs[decay_at]
    run = jnp.where(wide == 0, run + product * begin, run)
    up = product
    for k in (1, 2, 4, 8, 16, 32, 64):
        inside = wide >= k
        run = run + up * jnp.where(inside, pltpu.roll(run, k, 1), 0.0)
        up = up * jnp.where(inside, pltpu.roll(up, k, 1), 1.0)
        inside = wide < LANES - k
        back = back + product * jnp.where(inside, pltpu.roll(back, LANES - k, 1), 0.0)
        product = product * jnp.where(inside, pltpu.roll(product, LANES - k, 1), 1.0)
    held_runs[run_at] = jnp.where(wide == 0, begin, pltpu.roll(run, 1, 1))
    held_runs[decay_at] = jnp.where(wide == LANES - 1, 0.0, pltpu.roll(back, LANES - 1, 1))
    last_cell = jnp.broadcast_to(run[:, LANES - 1 :], (part, LANES))
    sums_ref[...] = jnp.where(wide == 0, last_cell, 0.0) + jnp.where(
        wide == 1, jnp.broadcast_to(back[:, :1], (part, LANES)), 0.0
    )

    def final(step, unused):
        rows = pl.ds(pl.multiple_of(step * ROWS, ROWS), ROWS)
        small = small_ref[rows, :]
        end_grad = jnp.where(last_lane, jnp.broadcast_to(small[:, 4:5], (ROWS, LANES)), 0.0)
        before = held_runs[run_at, rows, :]
        cells, befores = [], []
        for j in range(tiles):
            cand = held_gates[cand_at, rows, tile_of(j)]
            kept = jnp.where(is_live(j), 1.0 - held_gates[forget_at, rows, tile_of(j)], 0.0)
            cell = (1.0 - kept) * before + kept * cand
            befores.append(before)
            cells.append(cell)
            before = cell
        follow = held_runs[decay_at, rows, :]
        bias_sum = [zero] * 3
        for j in range(tiles - 1, -1, -1):
            cand = held_gates[cand_at, rows, tile_of(j)]
            forget = held_gates[forget_at, rows, tile_of(j)]
            out_gate = held_gates[out_at, rows, tile_of(j)]
            kept = jnp.where(is_live(j), 1.0 - forget, 0.0)
            emitted = out_gate * grad_ref[rows, tile_of(j)].astype(jnp.float32)
            hidden_ref[rows, tile_of(j)] = (out_gate * cells[j]).astype(jnp.bfloat16)
            out_part = emitted * cells[j] * (1.0 - out_gate)
            if j == tiles - 1:
                emitted = emitted + end_grad
            cell_grad = emitted + follow
            follow = (1.0 - kept) * cell_grad
            shared = cell_grad * kept
            parts = [
                shared * (1.0 - cand * cand),
                shared * (befores[j] - cand) * forget,
                out_part,
            ]
            for k in range(3):
                rounded = parts[k].astype(jnp.bfloat16)
                gg_ref[0, k, rows, tile_of(j)] = rounded
                wide_part = rounded.astype(jnp.float32)
                bias_sum[k] = bias_sum[k] + wide_part
                if j > 0:
                    gg_ref[1, k, rows, tile_of(j - 1)] = rounded
                else:
                    moved = jnp.where(last_lane, 0.0, pltpu.roll(wide_part, LANES - 1, 1))
                    gg_ref[1, k, rows, tile_of(tiles - 1)] = moved.astype(jnp.bfloat16)
        answer = sums_ref[rows, :]
        for k in range(3):
            total = jnp.sum(bias_sum[k], axis=1, keepdims=True)
            answer = jnp.where(lane == 2 + k, jnp.broadcast_to(total, (ROWS, LANES)), answer)
        sums_ref[rows, :] = answer
        return unused

    lax.fori_loop(0, part // ROWS, final, 0)


def pool(length, gates, small, grad):
    taps, kinds, width, span = gates.shape
    part = next(p for p in (96, 48, 16) if width % p == 0)
    return pl.pallas_call(
        lambda *refs: pool_kernel(*refs[:-2], refs[-2:]),
        grid=(width // part,),
        in_specs=[
            pl.BlockSpec(memory_space=pltpu.SMEM),
            pl.BlockSpec((2, 3, part, span), lambda i: (0, 0, i, 0)),
            pl.BlockSpec((part, LANES), lambda i: (i, 0)),
            pl.BlockSpec((part, span), lambda i: (i, 0)),
        ],
        out_specs=[
            pl.BlockSpec((part, span), lambda i: (i, 0)),
            pl.BlockSpec((part, LANES), lambda i: (i, 0)),
            pl.BlockSpec((2, 3, part, span), lambda i: (0, 0, i, 0)),
        ],
        out_shape=[
            jax.ShapeDtypeStruct((width, span), jnp.bfloat16),
            jax.ShapeDtypeStruct((width, LANES), jnp.float32),
            jax.ShapeDtypeStruct((2, 3, width, span), jnp.bfloat16),
        ],
        scratch_shapes=[
            pltpu.VMEM((3, part, span), jnp.float32),
            pltpu.VMEM((3, part, LANES), jnp.float32),
        ],
        compiler_params=pltpu.CompilerParams(vmem_limit_bytes=40 * 2**20),
        cost_estimate=HIDDEN_COST,
        name="pool",
    )(length, gates, small, grad)


def small_columns(bias, start_cell, cell_grad):
    stacked = jnp.concatenate([bias.astype(jnp.float32), start_cell, cell_grad], axis=0)
    return jnp.pad(stacked.T, ((0, 0), (0, LANES - 5)))


def slot_order(span):
    tiles = span // LANES
    slot = lax.broadcasted_iota(jnp.int32, (span, span), 0)
    place = lax.broadcasted_iota(jnp.int32, (span, span), 1)
    return (place == (slot % tiles) * LANES + slot // tiles).astype(jnp.bfloat16)


def mix(block, order, back=False):
    dims = (((1,), (1 if back else 0,)), ((), ()))
    return lax.dot_general(block, order, dims, preferred_element_type=jnp.float32).astype(jnp.bfloat16)


def times(left, right):
    return jnp.dot(left, right, preferred_element_type=jnp.float32)


def rows_dot(left, right):
    return lax.dot_general(left, right, (((0,), (0,)), ((), ())), preferred_element_type=jnp.float32)


def cols_dot(left, right):
    return lax.dot_general(left, right, (((1,), (1,)), ((), ())), preferred_element_type=jnp.float32)


def once(shape):
    zeros = (0,) * len(shape)
    return pl.BlockSpec(shape, lambda *at: zeros, pipeline_mode=pl.Buffered(1))


def gates_kernel(pick_ref, low_ref, high_ref, w_ref, *refs):
    base_ref = refs[0] if len(refs) == 3 else None
    out_ref, x_ref = refs[-2:]
    half_rows = low_ref.shape[0]

    @pl.when(pl.program_id(0) == 0)
    def _():
        at = pl.multiple_of(pick_ref[2] * half_rows, 64)
        x_ref[pl.ds(at, half_rows), :] = low_ref[...]
        at = pl.multiple_of((1 - pick_ref[2]) * half_rows, 64)
        x_ref[pl.ds(at, half_rows), :] = high_ref[...]

    kinds, width = w_ref.shape[1:3]
    weights = w_ref[0].reshape(kinds * width, w_ref.shape[3])
    total = jnp.dot(weights, x_ref[...], preferred_element_type=jnp.float32)
    total = total.reshape(out_ref.shape)
    if base_ref is not None:
        total = total + base_ref[...]
    out_ref[...] = total


def gates_step(pick, w_rows, own, sibling, base=None):
    taps, kinds, width, depth = w_rows.shape
    rows, span = own.shape
    block = lambda: pl.BlockSpec((1, kinds, width // 2, span), lambda g, p: (g, 0, 0, 0))
    specs = [
        once((rows, span)),
        once((rows, span)),
        pl.BlockSpec((1, kinds, width // 2, 2 * rows), lambda g, p: (g, 0, p[0], p[1])),
    ]
    operands = [own, sibling, w_rows]
    if base is not None:
        specs.append(block())
        operands.append(base)
    return pl.pallas_call(
        gates_kernel,
        grid_spec=pltpu.PrefetchScalarGridSpec(
            num_scalar_prefetch=1,
            grid=(taps,),
            in_specs=specs,
            out_specs=[block(), pl.BlockSpec((2 * rows, span), lambda g, p: (0, 0))],
        ),
        out_shape=[
            jax.ShapeDtypeStruct((taps, kinds, width // 2, span), jnp.float32),
            jax.ShapeDtypeStruct((2 * rows, span), jnp.bfloat16),
        ],
        compiler_params=pltpu.CompilerParams(vmem_limit_bytes=48 * 2**20),
        cost_estimate=HIDDEN_COST,
        name="gates_step",
    )(pick, *operands)


def gates_both_kernel(pick_ref, near_ref, far_ref, w_near_ref, w_far_ref, out_ref):
    kinds, width, rows = w_near_ref.shape[1:]

    def product(w_ref, x_ref):
        weights = w_ref[0].reshape(kinds * width, rows)
        return jnp.dot(weights, x_ref[...], preferred_element_type=jnp.float32)

    total = product(w_near_ref, near_ref) + product(w_far_ref, far_ref)
    out_ref[...] = total.reshape(out_ref.shape)


def gates_both(pick, w_rows, near, far):
    taps, kinds, width, depth = w_rows.shape
    rows, span = near.shape
    return pl.pallas_call(
        gates_both_kernel,
        grid_spec=pltpu.PrefetchScalarGridSpec(
            num_scalar_prefetch=1,
            grid=(taps,),
            in_specs=[
                once((rows, span)),
                once((rows, span)),
                pl.BlockSpec((1, kinds, width // 2, rows), lambda g, p: (g, 0, p[0], p[1])),
                pl.BlockSpec((1, kinds, width // 2, rows), lambda g, p: (g, 0, p[0], 1 - p[1])),
            ],
            out_specs=pl.BlockSpec((1, kinds, width // 2, span), lambda g, p: (g, 0, 0, 0)),
        ),
        out_shape=jax.ShapeDtypeStruct((taps, kinds, width // 2, span), jnp.float32),
        compiler_params=pltpu.CompilerParams(vmem_limit_bytes=48 * 2**20),
        cost_estimate=HIDDEN_COST,
        name="gates_both",
    )(pick, near, far, w_rows, w_rows)


def back_kernel(pick_ref, w_ref, mine_ref, other_ref, keep_ref, give_ref, total_ref):
    step = pl.program_id(0)
    kinds, width, columns = w_ref.shape[1:]
    weights = w_ref[0].reshape(kinds * width, columns)

    def add(grads):
        product = lax.dot_general(
            weights, grads, (((0,), (0,)), ((), ())), preferred_element_type=jnp.float32
        )

        @pl.when(step == 0)
        def _():
            total_ref[...] = product

        @pl.when(step > 0)
        def _():
            total_ref[...] += product

    @pl.when(step % 2 == 0)
    def _():
        add(mine_ref[0].reshape(kinds * width, mine_ref.shape[-1]))

    @pl.when(step % 2 == 1)
    def _():
        add(other_ref[0].reshape(kinds * width, other_ref.shape[-1]))

    @pl.when(step == pl.num_programs(0) - 1)
    def _():
        rows = keep_ref.shape[0]
        keep_ref[...] = total_ref[pl.ds(pl.multiple_of(pick_ref[2] * rows, 64), rows), :]
        give_ref[...] = total_ref[
            pl.ds(pl.multiple_of((1 - pick_ref[2]) * rows, 64), rows), :
        ].astype(jnp.bfloat16)


def back_products(pick, w_rows, mine, other):
    taps, kinds, width, depth = w_rows.shape
    span = mine.shape[-1]
    columns = depth // 2
    grads = pl.BlockSpec((1, kinds, width // 2, span), lambda i, p: (i // 2, 0, 0, 0))
    return pl.pallas_call(
        back_kernel,
        grid_spec=pltpu.PrefetchScalarGridSpec(
            num_scalar_prefetch=1,
            grid=(2 * taps,),
            in_specs=[
                pl.BlockSpec(
                    (1, kinds, width // 2, columns),
                    lambda i, p: (i // 2, 0, jnp.where(i % 2 == 0, p[0], 1 - p[0]), p[1]),
                ),
                grads,
                grads,
            ],
            out_specs=[
                pl.BlockSpec((columns // 2, span), lambda i, p: (0, 0)),
                pl.BlockSpec((columns // 2, span), lambda i, p: (0, 0)),
            ],
            scratch_shapes=[pltpu.VMEM((columns, span), jnp.float32)],
        ),
        out_shape=[
            jax.ShapeDtypeStruct((columns // 2, span), jnp.float32),
            jax.ShapeDtypeStruct((columns // 2, span), jnp.bfloat16),
        ],
        compiler_params=pltpu.CompilerParams(vmem_limit_bytes=48 * 2**20),
        cost_estimate=HIDDEN_COST,
        name="back_products",
    )(pick, w_rows, mine, other)


def weight_kernel(mine_ref, pair_ref, near_ref, far_ref, pair_near_ref, pair_far_ref, out_ref):
    def product(gg_ref, x_ref):
        return lax.dot_general(
            gg_ref[...], x_ref[...], (((1,), (1,)), ((), ())), preferred_element_type=jnp.float32
        )

    middle = near_ref.shape[0]
    out_ref[:, :middle] = (
        product(mine_ref, near_ref) + product(pair_ref, pair_near_ref)
    ).astype(jnp.bfloat16)
    out_ref[:, middle:] = (
        product(mine_ref, far_ref) + product(pair_ref, pair_far_ref)
    ).astype(jnp.bfloat16)


def weight_products(gg_mine, gg_pair, near, far, pair_near, pair_far, block, first, last):
    rows, span = gg_mine.shape
    columns = near.shape[0]
    grads = pl.BlockSpec((block, span), lambda i: (i + first, 0))
    return pl.pallas_call(
        weight_kernel,
        grid=(last - first,),
        in_specs=[grads, grads] + [once((columns, span))] * 4,
        out_specs=pl.BlockSpec((block, 2 * columns), lambda i: (i, 0)),
        out_shape=jax.ShapeDtypeStruct(((last - first) * block, 2 * columns), jnp.bfloat16),
        compiler_params=pltpu.CompilerParams(vmem_limit_bytes=48 * 2**20),
        cost_estimate=HIDDEN_COST,
        name="weight_products",
    )(gg_mine, gg_pair, near, far, pair_near, pair_far)


def even_odd(count):
    return [(i, i ^ 1) for i in range(count)]


def line_pairs(moves):
    return [(2 * a + s, 2 * b + s) for a, b in moves for s in range(2)]


class Order:
    def __init__(self, token):
        self.token = token

    def __call__(self, values):
        values, self.token = lax.optimization_barrier((values, self.token))
        return values


def line_sum(part, length):
    if length & (length - 1) == 0:
        step = 1
        while step < length:
            part = part + lax.ppermute(part, "dp", line_pairs([(i, i ^ step) for i in range(length)]))
            step *= 2
        return part
    total = part
    for _ in range(length - 1):
        part = lax.ppermute(part, "dp", line_pairs([(i, (i + 1) % length) for i in range(length)]))
        total = total + part
    return total


def half(array, axis, which):
    size = array.shape[axis] // 2
    return lax.dynamic_slice_in_dim(array, which * size, size, axis)


def join(low_first, mine, other, axis):
    return jnp.where(
        low_first,
        jnp.concatenate([mine, other], axis=axis),
        jnp.concatenate([other, mine], axis=axis),
    )


def write_kernel(count, flags_ref, *refs):
    out_ref = refs[-1]
    size = refs[0].shape[0]
    middle = refs[0].shape[1] // 2
    mine = flags_ref[0] == pl.program_id(0)
    straight = flags_ref[1] == 0
    for j in range(count):
        at = pl.ds(j * size, size)
        block = jnp.where(mine, refs[j][...], refs[count + j][...]).astype(jnp.float32)
        left, right = block[:, :middle], block[:, middle:]
        out_ref[at, :middle] = jnp.where(straight, left, right)
        out_ref[at, middle:] = jnp.where(straight, right, left)


def write_chunks(flags, mine, theirs, group, whole, shape):
    count = len(mine)
    size, depth = mine[0].shape
    specs = [pl.BlockSpec(memory_space=pltpu.SMEM)]
    specs += [pl.BlockSpec((size, depth), lambda i: (0, 0))] * (2 * count)
    operands = [flags, *mine, *theirs]
    aliases = {}
    if whole is not None:
        specs.append(pl.BlockSpec(memory_space=pl.ANY))
        operands.append(whole)
        aliases = {len(operands) - 1: 0}
    return pl.pallas_call(
        functools.partial(write_kernel, count),
        grid=(2,),
        in_specs=specs,
        out_specs=pl.BlockSpec((count * size, depth), lambda i: (2 * group + i, 0)),
        out_shape=jax.ShapeDtypeStruct(shape, jnp.float32),
        input_output_aliases=aliases,
        compiler_params=pltpu.CompilerParams(vmem_limit_bytes=40 * 2**20),
        cost_estimate=HIDDEN_COST,
        name="write_chunks",
    )(*operands)


def add_times(total, left, right):
    return total + times(left, right)


def add_rounded(left, right):
    return (left.astype(jnp.float32) + right.astype(jnp.float32)).astype(jnp.bfloat16)


def piped_sums(order, chunks, pairs, fillers, arrived):
    position = lax.axis_index("dp") // 2
    inner = (position == 1) | (position == 2)
    edge = line_pairs([(0, 1), (1, 0), (2, 3), (3, 2)])
    middle = line_pairs([(1, 2), (2, 1)])
    sums, totals, finals, swapped = {}, {}, {}, {}
    got_edge, got_middle, got_pair = {}, {}, {}
    for n in range(CHUNKS + LAG + 3):
        k = n - 3
        if 0 <= k < CHUNKS:
            got = order(got_middle.pop(k))
            totals[k] = order(add_rounded(sums.pop(k), got))
        k = n - LAG
        if n < CHUNKS and 0 <= k < CHUNKS:
            payload = jnp.where(inner, totals[k], chunks[n])
        elif n < CHUNKS:
            payload = chunks[n]
        elif 0 <= k < CHUNKS:
            payload = totals[k]
        else:
            payload = None
        if payload is not None:
            got_edge[n] = lax.ppermute(order(payload), "dp", edge)
        if n in fillers:
            fillers[n]()
        k = n - 1
        if k in got_edge:
            got = order(got_edge.pop(k))
            if k < CHUNKS:
                sums[k] = order(add_rounded(chunks.pop(k), got))
                got_middle[k] = lax.ppermute(sums[k], "dp", middle)
            k = k - LAG
            if 0 <= k < CHUNKS:
                finals[k] = order(jnp.where(inner, totals.pop(k), got))
                got_pair[k] = lax.ppermute(finals[k], "dp", pairs)
        k = n - LAG - 3
        if 0 <= k < CHUNKS:
            swapped[k] = order(got_pair.pop(k))
            arrived(k, finals, swapped)
    for k in sorted(got_pair):
        swapped[k] = order(got_pair.pop(k))
        arrived(k, finals, swapped)


def on_device(line, channel_parts, inputs, lengths, start_cell, weight, bias, out_grad, cell_grad):
    span, width = inputs.shape
    depth = weight.shape[1]
    own = width // 2
    rows = 6 * own
    side = lax.axis_index("dp") % 2
    other_side = 1 - side
    is_low = side == 0
    pairs = even_odd(2 * line)
    slots = slot_order(span)

    place = lax.axis_index("mp")
    core_low = place % 2 == 0
    near_low = place < 2
    core_pairs = even_odd(channel_parts)
    chip_pairs = [(i, i ^ 2) for i in range(4)]

    def split(array, axis):
        return half(array, axis, place // 2), half(array, axis, 1 - place // 2)

    small = small_columns(bias, start_cell, cell_grad)
    lane = lax.broadcasted_iota(jnp.int32, small.shape, 1)
    small = jnp.where(lane == 5, lengths[0].astype(jnp.float32), small)
    small_mine, small_other = half(small, 0, side), half(small, 0, other_side)
    w_rows = jnp.transpose(weight, (0, 2, 3, 1))

    def pooled(total, length, small_part, grad_part):
        hidden, sums, gg = pool(length, total.reshape(2, 3, own, span), small_part, grad_part)
        return hidden, sums, gg.reshape(rows, span)

    if line == 4 and channel_parts == 4:
        done = Order(small_mine)

        def run(function, *operands):
            return done(function(*done(operands)))

        pick_mine = jnp.stack([side, place // 2, place % 2]).astype(jnp.int32)
        pick_mine_far = jnp.stack([side, 1 - place // 2, place % 2]).astype(jnp.int32)
        pick_other = jnp.stack([other_side, place // 2, place % 2]).astype(jnp.int32)
        x_own = run(lambda x: mix(x.T, slots), inputs)
        far_got = lax.ppermute(x_own, "mp", chip_pairs)
        pair_got = lax.ppermute(x_own, "dp", pairs)
        near_got = lax.ppermute(x_own, "mp", core_pairs)
        grads = run(lambda g: mix(g.T, slots), out_grad)
        grads_mine, grads_other = done((half(grads, 0, side), half(grads, 0, other_side)))
        gates, near = run(gates_step, pick_mine, w_rows, x_own, near_got)
        far_own = done(far_got)
        far_got = lax.ppermute(far_own, "mp", core_pairs)
        x_pair = done(pair_got)
        pair_far_got = lax.ppermute(x_pair, "mp", chip_pairs)
        grads_pair = lax.ppermute(grads_other, "dp", pairs)
        small_pair = lax.ppermute(small_other, "dp", pairs)
        far_got = done(far_got)
        pair_near_got = lax.ppermute(done(x_pair), "mp", core_pairs)
        gates, far = run(gates_step, pick_mine_far, w_rows, far_own, far_got, gates)
        pair_gates, pair_near = run(gates_step, pick_mine, w_rows, x_pair, pair_near_got)
        gates, grads_mine = done((gates, grads_mine))
        hidden_mine, sums_mine, gg_mine = pooled(gates, lengths, done.token, grads_mine)
        done.token = sums_mine
        gg_mine = done(gg_mine)
        pair_far_own = done(pair_far_got)
        pair_far_got = lax.ppermute(pair_far_own, "mp", core_pairs)
        gates_other = run(gates_both, pick_other, w_rows, near, far)
        pair_gates, pair_far = run(
            gates_step, pick_mine_far, w_rows, pair_far_own, pair_far_got, pair_gates
        )
        small_pair, grads_pair = done((small_pair, grads_pair))
        length_pair = small_pair[0, 5:6].astype(jnp.int32)
        small_pair = jnp.where(lane[:own] < 3, small_mine, small_pair)
        _, sums_pair, gg_pair = run(pooled, pair_gates, length_pair, small_pair, grads_pair)

        size = rows // CHUNKS
        chunks = {}

        def products(first, last):
            def fill():
                part = run(
                    lambda *at: weight_products(*at, own, first, last),
                    gg_mine,
                    gg_pair,
                    near,
                    far,
                    pair_near,
                    pair_far,
                )
                for k in range(first * per, last * per):
                    at = (k - first * per) * size
                    chunks[k] = part[at : at + size]

            return fill

        kept = {}

        def fill_pool():
            kept["pool"] = run(pooled, gates_other, lengths, small_other, grads_other)

        def fill_back(part):
            def stage():
                keep, give = run(
                    back_products,
                    (pick_mine, pick_mine_far)[part],
                    w_rows,
                    gg_mine.reshape(2, 3, own, span),
                    kept["pool"][2].reshape(2, 3, own, span),
                )
                kept["keep", part] = keep
                kept["got", part] = lax.ppermute(give, "mp", core_pairs)

            return stage

        def fill_cross():
            far_sum = run(
                lambda a, b: (a + b.astype(jnp.float32)).astype(jnp.bfloat16),
                kept["keep", 1],
                kept["got", 1],
            )
            kept["cross"] = lax.ppermute(far_sum, "mp", chip_pairs)

        def fill_input():
            def total(a, b, c):
                total = a + b.astype(jnp.float32) + c.astype(jnp.float32)
                return mix(total.astype(jnp.bfloat16), slots, back=True).T

            kept["input"] = run(total, kept["keep", 0], kept["got", 0], kept["cross"])

        def fill_hidden():
            def whole(mine, other):
                return mix(join(is_low, mine, other, 0), slots, back=True).T

            kept["hidden"] = run(whole, hidden_mine, kept["pool"][0])

        per = own // size
        bias_sums = run(jnp.add, sums_mine, sums_pair)
        position = lax.axis_index("dp") // 2
        inner = (position == 1) | (position == 2)

        def fill_bias(stage):
            def run_stage():
                if stage == 0:
                    kept["bias"] = done(bias_sums)
                    moves = [(0, 1), (1, 0), (2, 3), (3, 2)]
                elif stage == 1:
                    kept["bias"] = run(jnp.add, kept["bias"], kept["bias got"])
                    moves = [(1, 2), (2, 1)]
                elif stage == 2:
                    kept["bias"] = run(jnp.add, kept["bias"], kept["bias got"])
                    moves = [(1, 0), (2, 3), (0, 1), (3, 2)]
                elif stage == 3:
                    kept["bias"] = run(
                        lambda a, b: jnp.where(inner, a, b), kept["bias"], kept["bias got"]
                    )
                if stage < 3:
                    kept["bias got"] = lax.ppermute(kept["bias"], "dp", line_pairs(moves))
                elif stage == 3:
                    kept["bias got"] = lax.ppermute(kept["bias"], "dp", pairs)
                else:
                    kept["bias got"] = done(kept["bias got"])

            return run_stage

        flags = jnp.stack([side, place // 2]).astype(jnp.int32)
        kept["out"] = None

        def arrived(k, finals, swapped):
            group = k // per
            members = range(group * per, (group + 1) * per)
            if k == members[-1]:
                parts = done(([finals[m] for m in members], [swapped[m] for m in members]))
                kept["out"] = done(write_chunks(flags, *parts, group, kept["out"], (2 * rows, depth)))

        products(0, 1)()
        fillers = {
            1: products(1, 3),
            2: fill_pool,
            3: fill_back(1),
            4: products(3, 6),
            5: fill_back(0),
            6: fill_cross,
            7: fill_bias(0),
            8: fill_hidden,
            9: fill_bias(1),
            11: fill_input,
            12: fill_bias(2),
            14: fill_bias(3),
            16: fill_bias(4),
        }
        piped_sums(done, chunks, pairs, fillers, arrived)
        hidden_other, sums_other, _ = kept["pool"]
        input_grad, hidden = kept["input"], kept["hidden"]
        wgrad = kept["out"].reshape(2, 3, width, depth)
        bias_grad = join(is_low, kept["bias"], kept["bias got"], 0)[:, 2:5].T
        sums_mine = done.token
    else:
        x_own = mix(inputs.T, slots)
        grads = mix(out_grad.T, slots)
        grads_mine, grads_other = half(grads, 0, side), half(grads, 0, other_side)
        grads_pair = lax.ppermute(grads_other, "dp", pairs)
        small_pair = lax.ppermute(small_other, "dp", pairs)
        length_pair = small_pair[0, 5:6].astype(jnp.int32)
        small_pair = jnp.where(lane[:own] < 3, small_mine, small_pair)
        x_all = lax.all_gather(x_own, "mp", axis=0, tiled=True)
        x_pair = lax.all_gather(lax.ppermute(x_own, "dp", pairs), "mp", axis=0, tiled=True)
        w_mine = half(w_rows, 2, side).reshape(rows, depth)
        w_other = half(w_rows, 2, other_side).reshape(rows, depth)
        hidden_mine, sums_mine, gg_mine = pooled(
            times(w_mine, x_all), lengths, small_mine, grads_mine
        )
        _, sums_pair, gg_pair = pooled(times(w_mine, x_pair), length_pair, small_pair, grads_pair)
        hidden_other, sums_other, gg_other = pooled(
            times(w_other, x_all), lengths, small_other, grads_other
        )
        part = cols_dot(gg_mine, x_all) + cols_dot(gg_pair, x_pair)
        total = line_sum(part.astype(jnp.bfloat16), line)
        theirs = lax.ppermute(total, "dp", pairs)
        shape = (2, 3, own, depth)
        wgrad = join(is_low, total.reshape(shape), theirs.reshape(shape), 2).astype(jnp.float32)
        back = rows_dot(w_mine, gg_mine) + rows_dot(w_other, gg_other)
        input_grad = lax.psum_scatter(
            back.astype(jnp.bfloat16), "mp", scatter_dimension=0, tiled=True
        )
        input_grad = mix(input_grad, slots, back=True).T
        hidden = mix(join(is_low, hidden_mine, hidden_other, 0), slots, back=True).T
        bias_mine = line_sum(sums_mine + sums_pair, line)
        bias_pair = lax.ppermute(bias_mine, "dp", pairs)
        bias_grad = join(is_low, bias_mine, bias_pair, 0)[:, 2:5].T

    sums = join(is_low, sums_mine, sums_other, 0)
    return (
        hidden,
        sums[:, 0:1].T,
        input_grad,
        sums[:, 1:2].T,
        jnp.transpose(wgrad, (0, 3, 1, 2)),
        bias_grad,
    )


def solution(mesh):
    in_specs = (
        P("dp", "mp"),
        P("dp"),
        P("dp", "mp"),
        P(None, None, None, "mp"),
        P(None, "mp"),
        P("dp", "mp"),
        P("dp", "mp"),
    )
    out_specs = (
        P("dp", "mp"),
        P("dp", "mp"),
        P("dp", "mp"),
        P("dp", "mp"),
        P(None, None, None, "mp"),
        P(None, "mp"),
    )
    body = functools.partial(on_device, mesh.shape["dp"] // 2, mesh.shape["mp"])
    return jax.shard_map(
        body, mesh=mesh, in_specs=in_specs, out_specs=out_specs, check_vma=False
    )
```

```python
import functools

import jax
import jax.numpy as jnp
from jax import lax
from jax.experimental import pallas as pl
from jax.experimental.pallas import tpu as pltpu
from jax.sharding import PartitionSpec as P

LANES = 128
ROWS = 16
CHUNKS = 18
PART = 96
LAG = 4
HIDDEN_COST = pl.CostEstimate(flops=1, bytes_accessed=1, transcendentals=0)


def pool_kernel(length_ref, gates_ref, small_ref, grad_ref, hidden_ref, sums_ref, gg_ref, held):
    part, span = grad_ref.shape
    tiles = span // LANES
    length = length_ref[0]
    lane = lax.broadcasted_iota(jnp.int32, (ROWS, LANES), 1)
    zero = jnp.zeros((ROWS, LANES), jnp.float32)
    one = zero + 1.0
    first_lane = lane == 0
    last_lane = lane == LANES - 1
    cand_at, forget_at, out_at = 0, 1, 2
    run_at, back_at, decay_at = 0, 1, 2
    held_gates, held_runs = held

    def tile_of(j):
        return pl.ds(j * LANES, LANES)

    def is_live(j):
        return lane * tiles + j < length

    def local(step, unused):
        rows = pl.ds(pl.multiple_of(step * ROWS, ROWS), ROWS)
        small = small_ref[rows, :]
        bias = [jnp.broadcast_to(small[:, k : k + 1], (ROWS, LANES)) for k in range(3)]
        end_grad = jnp.where(last_lane, jnp.broadcast_to(small[:, 4:5], (ROWS, LANES)), 0.0)
        earlier = [
            jnp.where(first_lane, 0.0, pltpu.roll(gates_ref[1, k, rows, tile_of(tiles - 1)], 1, 1))
            for k in range(3)
        ]
        run, product, back = zero, one, zero
        for j in range(tiles):
            gates = []
            for k in range(3):
                gates.append(gates_ref[0, k, rows, tile_of(j)] + earlier[k] + bias[k])
                earlier[k] = gates_ref[1, k, rows, tile_of(j)]
            live = is_live(j)
            cand = jnp.tanh(gates[0])
            forget = jax.nn.sigmoid(gates[1])
            out_gate = jnp.where(live, 0.5 * jnp.tanh(0.5 * gates[2]) + 0.5, 0.0)
            kept = jnp.where(live, 1.0 - forget, 0.0)
            decay = 1.0 - kept
            emitted = out_gate * grad_ref[rows, tile_of(j)].astype(jnp.float32)
            if j == tiles - 1:
                emitted = emitted + end_grad
            run = decay * run + kept * cand
            product = product * decay
            back = back + product * emitted
            held_gates[cand_at, rows, tile_of(j)] = cand
            held_gates[forget_at, rows, tile_of(j)] = forget
            held_gates[out_at, rows, tile_of(j)] = out_gate
        held_runs[run_at, rows, :] = run
        held_runs[back_at, rows, :] = back
        held_runs[decay_at, rows, :] = product
        return unused

    lax.fori_loop(0, part // ROWS, local, 0)

    wide = lax.broadcasted_iota(jnp.int32, (part, LANES), 1)
    begin = jnp.broadcast_to(small_ref[:, 3:4], (part, LANES))
    run, back, product = held_runs[run_at], held_runs[back_at], held_runs[decay_at]
    run = jnp.where(wide == 0, run + product * begin, run)
    up = product
    for k in (1, 2, 4, 8, 16, 32, 64):
        inside = wide >= k
        run = run + up * jnp.where(inside, pltpu.roll(run, k, 1), 0.0)
        up = up * jnp.where(inside, pltpu.roll(up, k, 1), 1.0)
        inside = wide < LANES - k
        back = back + product * jnp.where(inside, pltpu.roll(back, LANES - k, 1), 0.0)
        product = product * jnp.where(inside, pltpu.roll(product, LANES - k, 1), 1.0)
    held_runs[run_at] = jnp.where(wide == 0, begin, pltpu.roll(run, 1, 1))
    held_runs[decay_at] = jnp.where(wide == LANES - 1, 0.0, pltpu.roll(back, LANES - 1, 1))
    last_cell = jnp.broadcast_to(run[:, LANES - 1 :], (part, LANES))
    sums_ref[...] = jnp.where(wide == 0, last_cell, 0.0) + jnp.where(
        wide == 1, jnp.broadcast_to(back[:, :1], (part, LANES)), 0.0
    )

    def final(step, unused):
        rows = pl.ds(pl.multiple_of(step * ROWS, ROWS), ROWS)
        small = small_ref[rows, :]
        end_grad = jnp.where(last_lane, jnp.broadcast_to(small[:, 4:5], (ROWS, LANES)), 0.0)
        before = held_runs[run_at, rows, :]
        cells, befores = [], []
        for j in range(tiles):
            cand = held_gates[cand_at, rows, tile_of(j)]
            kept = jnp.where(is_live(j), 1.0 - held_gates[forget_at, rows, tile_of(j)], 0.0)
            cell = (1.0 - kept) * before + kept * cand
            befores.append(before)
            cells.append(cell)
            before = cell
        follow = held_runs[decay_at, rows, :]
        bias_sum = [zero] * 3
        for j in range(tiles - 1, -1, -1):
            cand = held_gates[cand_at, rows, tile_of(j)]
            forget = held_gates[forget_at, rows, tile_of(j)]
            out_gate = held_gates[out_at, rows, tile_of(j)]
            kept = jnp.where(is_live(j), 1.0 - forget, 0.0)
            emitted = out_gate * grad_ref[rows, tile_of(j)].astype(jnp.float32)
            hidden_ref[rows, tile_of(j)] = (out_gate * cells[j]).astype(jnp.bfloat16)
            out_part = emitted * cells[j] * (1.0 - out_gate)
            if j == tiles - 1:
                emitted = emitted + end_grad
            cell_grad = emitted + follow
            follow = (1.0 - kept) * cell_grad
            shared = cell_grad * kept
            parts = [
                shared * (1.0 - cand * cand),
                shared * (befores[j] - cand) * forget,
                out_part,
            ]
            for k in range(3):
                rounded = parts[k].astype(jnp.bfloat16)
                gg_ref[0, k, rows, tile_of(j)] = rounded
                wide_part = rounded.astype(jnp.float32)
                bias_sum[k] = bias_sum[k] + wide_part
                if j > 0:
                    gg_ref[1, k, rows, tile_of(j - 1)] = rounded
                else:
                    moved = jnp.where(last_lane, 0.0, pltpu.roll(wide_part, LANES - 1, 1))
                    gg_ref[1, k, rows, tile_of(tiles - 1)] = moved.astype(jnp.bfloat16)
        answer = sums_ref[rows, :]
        for k in range(3):
            total = jnp.sum(bias_sum[k], axis=1, keepdims=True)
            answer = jnp.where(lane == 2 + k, jnp.broadcast_to(total, (ROWS, LANES)), answer)
        sums_ref[rows, :] = answer
        return unused

    lax.fori_loop(0, part // ROWS, final, 0)


def pool(length, gates, small, grad):
    taps, kinds, width, span = gates.shape
    part = next(p for p in (96, 48, 16) if width % p == 0)
    return pl.pallas_call(
        lambda *refs: pool_kernel(*refs[:-2], refs[-2:]),
        grid=(width // part,),
        in_specs=[
            pl.BlockSpec(memory_space=pltpu.SMEM),
            pl.BlockSpec((2, 3, part, span), lambda i: (0, 0, i, 0)),
            pl.BlockSpec((part, LANES), lambda i: (i, 0)),
            pl.BlockSpec((part, span), lambda i: (i, 0)),
        ],
        out_specs=[
            pl.BlockSpec((part, span), lambda i: (i, 0)),
            pl.BlockSpec((part, LANES), lambda i: (i, 0)),
            pl.BlockSpec((2, 3, part, span), lambda i: (0, 0, i, 0)),
        ],
        out_shape=[
            jax.ShapeDtypeStruct((width, span), jnp.bfloat16),
            jax.ShapeDtypeStruct((width, LANES), jnp.float32),
            jax.ShapeDtypeStruct((2, 3, width, span), jnp.bfloat16),
        ],
        scratch_shapes=[
            pltpu.VMEM((3, part, span), jnp.float32),
            pltpu.VMEM((3, part, LANES), jnp.float32),
        ],
        compiler_params=pltpu.CompilerParams(vmem_limit_bytes=40 * 2**20),
        cost_estimate=HIDDEN_COST,
        name="pool",
    )(length, gates, small, grad)


def small_columns(bias, start_cell, cell_grad):
    stacked = jnp.concatenate([bias.astype(jnp.float32), start_cell, cell_grad], axis=0)
    return jnp.pad(stacked.T, ((0, 0), (0, LANES - 5)))


def slot_order(span):
    tiles = span // LANES
    slot = lax.broadcasted_iota(jnp.int32, (span, span), 0)
    place = lax.broadcasted_iota(jnp.int32, (span, span), 1)
    return (place == (slot % tiles) * LANES + slot // tiles).astype(jnp.bfloat16)


def mix(block, order, back=False):
    dims = (((1,), (1 if back else 0,)), ((), ()))
    return lax.dot_general(block, order, dims, preferred_element_type=jnp.float32).astype(jnp.bfloat16)


def times(left, right):
    return jnp.dot(left, right, preferred_element_type=jnp.float32)


def rows_dot(left, right):
    return lax.dot_general(left, right, (((0,), (0,)), ((), ())), preferred_element_type=jnp.float32)


def cols_dot(left, right):
    return lax.dot_general(left, right, (((1,), (1,)), ((), ())), preferred_element_type=jnp.float32)


def once(shape):
    zeros = (0,) * len(shape)
    return pl.BlockSpec(shape, lambda *at: zeros, pipeline_mode=pl.Buffered(1))


def gates_kernel(pick_ref, low_ref, high_ref, w_ref, out_ref, x_ref, *copy_refs):
    half_rows = low_ref.shape[0]

    @pl.when(pl.program_id(0) == 0)
    def _():
        at = pl.multiple_of(pick_ref[2] * half_rows, 64)
        x_ref[pl.ds(at, half_rows), :] = low_ref[...]
        at = pl.multiple_of((1 - pick_ref[2]) * half_rows, 64)
        x_ref[pl.ds(at, half_rows), :] = high_ref[...]

    kinds, width = w_ref.shape[1:3]
    weights = w_ref[0].reshape(kinds * width, w_ref.shape[3])
    total = jnp.dot(weights, x_ref[...], preferred_element_type=jnp.float32)
    out_ref[...] = total.reshape(out_ref.shape)
    for copy_ref in copy_refs:
        copy_ref[...] = w_ref[...]


def gates_step(pick, w_rows, own, sibling, copy):
    taps, kinds, width, depth = w_rows.shape
    rows, span = own.shape
    block = lambda last: pl.BlockSpec((1, kinds, width // 2, last), lambda g, p: (g, 0, 0, 0))
    specs = [
        once((rows, span)),
        once((rows, span)),
        pl.BlockSpec((1, kinds, width // 2, 2 * rows), lambda g, p: (g, 0, p[0], p[1])),
    ]
    operands = [own, sibling, w_rows]
    out_specs = [block(span), pl.BlockSpec((2 * rows, span), lambda g, p: (0, 0))]
    out_shape = [
        jax.ShapeDtypeStruct((taps, kinds, width // 2, span), jnp.float32),
        jax.ShapeDtypeStruct((2 * rows, span), jnp.bfloat16),
    ]
    if copy:
        out_specs.append(block(2 * rows))
        out_shape.append(jax.ShapeDtypeStruct((taps, kinds, width // 2, 2 * rows), jnp.bfloat16))
    return pl.pallas_call(
        gates_kernel,
        grid_spec=pltpu.PrefetchScalarGridSpec(
            num_scalar_prefetch=1,
            grid=(taps,),
            in_specs=specs,
            out_specs=out_specs,
        ),
        out_shape=out_shape,
        compiler_params=pltpu.CompilerParams(vmem_limit_bytes=32 * 2**20),
        cost_estimate=HIDDEN_COST,
        name="gates_step",
    )(pick, *operands)


def gates_pool_kernel(pick_ref, length_ref, low_ref, high_ref, w_ref, base_ref, small_ref, grad_ref,
                      hidden_ref, sums_ref, gg_ref, x_ref, *refs):
    half_rows = low_ref.shape[0]

    @pl.when(pl.program_id(0) == 0)
    def _():
        at = pl.multiple_of(pick_ref[2] * half_rows, 64)
        x_ref[pl.ds(at, half_rows), :] = low_ref[...]
        at = pl.multiple_of((1 - pick_ref[2]) * half_rows, 64)
        x_ref[pl.ds(at, half_rows), :] = high_ref[...]

    gates_ref = refs[-3]
    for copy_ref in refs[:-3]:
        copy_ref[...] = w_ref[...]
    weights = w_ref[...].reshape(-1, w_ref.shape[3])
    product = jnp.dot(weights, x_ref[...], preferred_element_type=jnp.float32)
    gates_ref[...] = product.reshape(gates_ref.shape) + base_ref[...]
    pool_kernel(length_ref, gates_ref, small_ref, grad_ref, hidden_ref, sums_ref, gg_ref, refs[-2:])


def pool_shapes(width, span):
    return [
        jax.ShapeDtypeStruct((width, span), jnp.bfloat16),
        jax.ShapeDtypeStruct((width, LANES), jnp.float32),
        jax.ShapeDtypeStruct((2, 3, width, span), jnp.bfloat16),
    ]


def pool_scratch(part, span):
    return [
        pltpu.VMEM((2, 3, part, span), jnp.float32),
        pltpu.VMEM((3, part, span), jnp.float32),
        pltpu.VMEM((3, part, LANES), jnp.float32),
    ]


def gates_pool(pick, length, w_rows, own, sibling, base, small, grad, copy):
    taps, kinds, width, depth = w_rows.shape
    rows, span = own.shape
    width //= 2
    part = PART
    count = width // part
    lines = lambda columns: pl.BlockSpec((part, columns), lambda i, p: (i, 0))
    wide = pl.BlockSpec((taps, kinds, part, span), lambda i, p: (0, 0, i, 0))
    copy_specs, copy_shapes = [], []
    if copy:
        copy_specs = [pl.BlockSpec((taps, kinds, part, 2 * rows), lambda i, p: (0, 0, i, 0))]
        copy_shapes = [jax.ShapeDtypeStruct((taps, kinds, width, 2 * rows), jnp.bfloat16)]
    return pl.pallas_call(
        gates_pool_kernel,
        grid_spec=pltpu.PrefetchScalarGridSpec(
            num_scalar_prefetch=1,
            grid=(count,),
            in_specs=[
                pl.BlockSpec(memory_space=pltpu.SMEM),
                once((rows, span)),
                once((rows, span)),
                pl.BlockSpec(
                    (taps, kinds, part, 2 * rows), lambda i, p: (0, 0, p[0] * count + i, p[1])
                ),
                wide,
                lines(LANES),
                lines(span),
            ],
            out_specs=[
                lines(span),
                lines(LANES),
                wide,
                pl.BlockSpec((2 * rows, span), lambda i, p: (0, 0)),
                *copy_specs,
            ],
            scratch_shapes=pool_scratch(part, span),
        ),
        out_shape=pool_shapes(width, span)
        + [jax.ShapeDtypeStruct((2 * rows, span), jnp.bfloat16)]
        + copy_shapes,
        compiler_params=pltpu.CompilerParams(vmem_limit_bytes=40 * 2**20),
        cost_estimate=HIDDEN_COST,
        name="gates_pool",
    )(pick, length, own, sibling, w_rows, base, small, grad)


def whole_kernel(function, count, *refs):
    results = function(*[ref[...] for ref in refs[:count]])
    for ref, result in zip(refs[count:], results):
        ref[...] = result.astype(ref.dtype)


def whole(function, outputs, *operands):
    return pl.pallas_call(
        functools.partial(whole_kernel, function, len(operands)),
        out_shape=[jax.ShapeDtypeStruct(*output) for output in outputs],
        compiler_params=pltpu.CompilerParams(vmem_limit_bytes=20 * 2**20),
        cost_estimate=HIDDEN_COST,
        name="whole",
    )(*operands)


def back_kernel(pick_ref, w_ref, gg_ref, keep_ref, give_ref, total_ref):
    step = pl.program_id(0)
    columns = w_ref.shape[1]
    total_ref[pl.ds(pl.multiple_of(step * columns, columns), columns), :] = lax.dot_general(
        w_ref[...], gg_ref[...], (((0,), (0,)), ((), ())), preferred_element_type=jnp.float32
    )

    @pl.when(step == pl.num_programs(0) - 1)
    def _():
        rows = keep_ref.shape[0]
        keep_ref[...] = total_ref[pl.ds(pl.multiple_of(pick_ref[2] * rows, 64), rows), :]
        give_ref[...] = total_ref[
            pl.ds(pl.multiple_of((1 - pick_ref[2]) * rows, 64), rows), :
        ].astype(jnp.bfloat16)


def back_products(pick, weights, gg):
    depth, columns = weights.shape
    span = gg.shape[1]
    part = 384
    return pl.pallas_call(
        back_kernel,
        grid_spec=pltpu.PrefetchScalarGridSpec(
            num_scalar_prefetch=1,
            grid=(columns // part,),
            in_specs=[
                pl.BlockSpec((depth, part), lambda i, p: (0, i)),
                once((depth, span)),
            ],
            out_specs=[
                pl.BlockSpec((columns // 2, span), lambda i, p: (0, 0)),
                pl.BlockSpec((columns // 2, span), lambda i, p: (0, 0)),
            ],
            scratch_shapes=[pltpu.VMEM((columns, span), jnp.float32)],
        ),
        out_shape=[
            jax.ShapeDtypeStruct((columns // 2, span), jnp.float32),
            jax.ShapeDtypeStruct((columns // 2, span), jnp.bfloat16),
        ],
        compiler_params=pltpu.CompilerParams(vmem_limit_bytes=26 * 2**20),
        cost_estimate=HIDDEN_COST,
        name="back_products",
    )(pick, weights, gg)


def chunk_kernel(function, inputs, inner_ref, *refs):
    function(inner_ref[0] == 1, *refs[:inputs], *refs[inputs:])


def chunk_step(function, outputs, inner, size, *operands):
    specs, arrays = [pl.BlockSpec(memory_space=pltpu.SMEM)], [inner]
    for operand in operands:
        array, at = operand if isinstance(operand, tuple) else (operand, 0)
        specs.append(pl.BlockSpec((size, array.shape[1]), lambda i, at=at: (at, 0)))
        arrays.append(array)
    depth = arrays[1].shape[1]
    return pl.pallas_call(
        functools.partial(chunk_kernel, function, len(operands)),
        grid=(1,),
        in_specs=specs,
        out_specs=[pl.BlockSpec((size, depth), lambda i: (0, 0))] * outputs,
        out_shape=[jax.ShapeDtypeStruct((size, depth), jnp.bfloat16)] * outputs,
        compiler_params=pltpu.CompilerParams(vmem_limit_bytes=8 * 2**20),
        cost_estimate=HIDDEN_COST,
        name="chunk_step",
    )(*arrays)


def rounded_sum(left_ref, right_ref):
    total = left_ref[...].astype(jnp.float32) + right_ref[...].astype(jnp.float32)
    return total.astype(jnp.bfloat16)


def take_chunk(inner, chunk_ref, out_ref):
    out_ref[...] = chunk_ref[...]


def sum_chunk(inner, chunk_ref, got_ref, sum_ref):
    sum_ref[...] = rounded_sum(chunk_ref, got_ref)


def sum_and_final(inner, chunk_ref, got_ref, total_ref, sum_ref, final_ref):
    sum_ref[...] = rounded_sum(chunk_ref, got_ref)
    final_ref[...] = jnp.where(inner, total_ref[...], got_ref[...])


def total_and_next(inner, sum_ref, got_ref, chunk_ref, total_ref, next_ref):
    total = rounded_sum(sum_ref, got_ref)
    total_ref[...] = total
    next_ref[...] = jnp.where(inner, total, chunk_ref[...])


def final_chunk(inner, got_ref, total_ref, final_ref):
    final_ref[...] = jnp.where(inner, total_ref[...], got_ref[...])


def total_chunk(inner, sum_ref, got_ref, total_ref):
    total_ref[...] = rounded_sum(sum_ref, got_ref)


def even_odd(count):
    return [(i, i ^ 1) for i in range(count)]


def line_pairs(moves):
    return [(2 * a + s, 2 * b + s) for a, b in moves for s in range(2)]


class Order:
    def __init__(self, token):
        self.token = token

    def __call__(self, values):
        values, self.token = lax.optimization_barrier((values, self.token))
        return values


def line_sum(part, length):
    if length & (length - 1) == 0:
        step = 1
        while step < length:
            part = part + lax.ppermute(part, "dp", line_pairs([(i, i ^ step) for i in range(length)]))
            step *= 2
        return part
    total = part
    for _ in range(length - 1):
        part = lax.ppermute(part, "dp", line_pairs([(i, (i + 1) % length) for i in range(length)]))
        total = total + part
    return total


def half(array, axis, which):
    size = array.shape[axis] // 2
    return lax.dynamic_slice_in_dim(array, which * size, size, axis)


def join(low_first, mine, other, axis):
    return jnp.where(
        low_first,
        jnp.concatenate([mine, other], axis=axis),
        jnp.concatenate([other, mine], axis=axis),
    )


def write_kernel(count, flags_ref, *refs):
    out_ref = refs[-1]
    size = refs[0].shape[0]
    middle = refs[0].shape[1] // 2
    mine = flags_ref[0] == pl.program_id(0)
    straight = flags_ref[1] == 0
    for j in range(count):
        at = pl.ds(j * size, size)
        block = jnp.where(mine, refs[j][...], refs[count + j][...]).astype(jnp.float32)
        left, right = block[:, :middle], block[:, middle:]
        out_ref[at, :middle] = jnp.where(straight, left, right)
        out_ref[at, middle:] = jnp.where(straight, right, left)


def write_chunks(flags, mine, theirs, group, whole, shape):
    count = len(mine)
    size, depth = mine[0].shape
    specs = [pl.BlockSpec(memory_space=pltpu.SMEM)]
    specs += [pl.BlockSpec((size, depth), lambda i: (0, 0))] * (2 * count)
    operands = [flags, *mine, *theirs]
    aliases = {}
    if whole is not None:
        specs.append(pl.BlockSpec(memory_space=pl.ANY))
        operands.append(whole)
        aliases = {len(operands) - 1: 0}
    return pl.pallas_call(
        functools.partial(write_kernel, count),
        grid=(2,),
        in_specs=specs,
        out_specs=pl.BlockSpec((count * size, depth), lambda i: (2 * group + i, 0)),
        out_shape=jax.ShapeDtypeStruct(shape, jnp.float32),
        input_output_aliases=aliases,
        compiler_params=pltpu.CompilerParams(vmem_limit_bytes=16 * 2**20),
        cost_estimate=HIDDEN_COST,
        name="write_chunks",
    )(*operands)


def add_times(total, left, right):
    return total + times(left, right)


def add_rounded(left, right):
    return (left.astype(jnp.float32) + right.astype(jnp.float32)).astype(jnp.bfloat16)


def piped_sums(order, chunks, pairs, fillers, arrived):
    position = lax.axis_index("dp") // 2
    inner = (position == 1) | (position == 2)
    flag = inner.astype(jnp.int32).reshape(1)
    edge = line_pairs([(0, 1), (1, 0), (2, 3), (3, 2)])
    middle = line_pairs([(1, 2), (2, 1)])
    sums, totals, finals = {}, {}, {}
    got_edge, got_middle, got_pair = {}, {}, {}
    size = chunks[0].shape[0]

    def run(function, outputs, *operands):
        return order(chunk_step(function, outputs, flag, size, *order(operands)))

    payload = order(chunks[0])
    got_edge[0] = lax.ppermute(payload, "dp", edge)
    for n in range(CHUNKS + LAG + 3):
        final = None
        k = n - 1
        if k in got_edge:
            got = got_edge.pop(k)
            if k < CHUNKS and k >= LAG:
                sums[k], final = run(sum_and_final, 2, chunks[k], got, totals.pop(k - LAG))
            elif k < CHUNKS:
                (sums[k],) = run(sum_chunk, 1, chunks[k], got)
            else:
                (final,) = run(final_chunk, 1, got, totals.pop(k - LAG))
            if k < CHUNKS:
                got_middle[k] = lax.ppermute(sums[k], "dp", middle)
        k = n - 2
        payload = None
        if k in got_middle:
            got = got_middle.pop(k)
            (totals[k],) = run(total_chunk, 1, sums.pop(k), got)
        k = n + 1 - LAG
        if k in totals and n + 1 < CHUNKS:
            (payload,) = run(final_chunk, 1, chunks[n + 1], totals[k])
        elif n + 1 < CHUNKS:
            payload = order(chunks[n + 1])
        elif k in totals:
            payload = totals[k]
        if payload is not None:
            got_edge[n + 1] = lax.ppermute(payload, "dp", edge)
        k = n - 1 - LAG
        if final is not None:
            finals[k] = final
            got_pair[k] = lax.ppermute(final, "dp", pairs)
        k = k - 1
        if k in got_pair:
            arrived(k, finals, order(got_pair.pop(k)))
        if n in fillers:
            fillers[n]()


def on_device(line, channel_parts, inputs, lengths, start_cell, weight, bias, out_grad, cell_grad):
    span, width = inputs.shape
    depth = weight.shape[1]
    own = width // 2
    rows = 6 * own
    side = lax.axis_index("dp") % 2
    other_side = 1 - side
    is_low = side == 0
    pairs = even_odd(2 * line)
    slots = slot_order(span)

    place = lax.axis_index("mp")
    core_low = place % 2 == 0
    near_low = place < 2
    core_pairs = even_odd(channel_parts)
    chip_pairs = [(i, i ^ 2) for i in range(4)]

    def split(array, axis):
        return half(array, axis, place // 2), half(array, axis, 1 - place // 2)

    small = small_columns(bias, start_cell, cell_grad)
    lane = lax.broadcasted_iota(jnp.int32, small.shape, 1)
    small = jnp.where(lane == 5, lengths[0].astype(jnp.float32), small)
    small_mine, small_other = half(small, 0, side), half(small, 0, other_side)
    w_rows = jnp.transpose(weight, (0, 2, 3, 1))

    def pooled(total, length, small_part, grad_part):
        hidden, sums, gg = pool(length, total.reshape(2, 3, own, span), small_part, grad_part)
        return hidden, sums, gg.reshape(rows, span)

    if line == 4 and channel_parts == 4:
        done = Order(small_mine)

        def run(function, *operands):
            return done(function(*done(operands)))

        pick_near = jnp.stack([side, place // 2, place % 2]).astype(jnp.int32)
        pick_far = jnp.stack([side, 1 - place // 2, place % 2]).astype(jnp.int32)
        small_pair = lax.ppermute(small_other, "dp", pairs)
        x_own = run(lambda x: mix(x.T, slots), inputs)
        far_got = lax.ppermute(x_own, "mp", chip_pairs)
        pair_got = lax.ppermute(x_own, "dp", pairs)
        near_got = lax.ppermute(x_own, "mp", core_pairs)
        grads = run(lambda g: mix(g.T, slots), out_grad)
        grads_mine, grads_other = done((half(grads, 0, side), half(grads, 0, other_side)))
        gates, near, w_near = run(
            lambda *given: gates_step(*given, True), pick_near, w_rows, x_own, near_got
        )
        cut = width * 2 // 3
        far_own = done(far_got)
        far_got = lax.ppermute(far_own, "mp", core_pairs)
        x_pair, small_pair = done((pair_got, small_pair))
        relay = [
            lax.ppermute(x_pair[:cut], "mp", chip_pairs),
            lax.ppermute(far_own[cut:], "dp", pairs),
        ]
        far_got = done(far_got)
        pair_near_got = lax.ppermute(done(x_pair), "mp", core_pairs)
        far_own, far_got, gates, grads_mine = done((far_own, far_got, gates, grads_mine))
        hidden_mine, sums_mine, gg_mine, far, w_far = gates_pool(
            pick_far, lengths, w_rows, far_own, far_got, gates, done.token, grads_mine, True
        )
        done.token = sums_mine
        gg_mine = done(gg_mine.reshape(rows, span))
        pair_far_own = run(lambda a, b: jnp.concatenate([a, b], axis=0), *relay)
        pair_far_got = lax.ppermute(pair_far_own, "mp", core_pairs)
        grads_pair = lax.ppermute(done(grads_other), "dp", pairs)
        kept = {}

        own_shape, wide_type, sent_type = (width, span), jnp.float32, jnp.bfloat16

        def add(left, right):
            return (left + right.astype(jnp.float32),)

        def add_both(left, right):
            total = left + right.astype(jnp.float32)
            return total, total

        def fill_back(window, part):
            keep, give = run(
                back_products,
                pick_near,
                (w_near, w_far)[part].reshape(rows, depth // 2),
                gg_mine if window == 0 else gg_pair,
            )
            kept["keep", window, part] = keep
            kept["core", window, part] = lax.ppermute(give, "mp", core_pairs)

        def fill_core(window, part):
            kind = wide_type if part == 0 else sent_type
            (kept["sum", window, part],) = run(
                lambda *given: whole(add, [(own_shape, kind)], *given),
                kept["keep", window, part],
                kept["core", window, part],
            )

        def fill_cross(window):
            kept["cross", window] = lax.ppermute(done(kept["sum", window, 1]), "mp", chip_pairs)

        pair_gates, pair_near = run(
            lambda *given: gates_step(*given, False), pick_near, w_rows, x_pair, pair_near_got
        )
        small_pair, grads_pair = done((small_pair, grads_pair))
        length_pair = small_pair[0, 5:6].astype(jnp.int32)
        small_pair = jnp.where(lane[:own] < 3, small_mine, small_pair)
        hidden_pair, sums_pair, gg_pair, pair_far = run(
            lambda *given: gates_pool(*given, False),
            pick_far,
            length_pair,
            w_rows,
            pair_far_own,
            pair_far_got,
            pair_gates,
            small_pair,
            grads_pair,
        )
        gg_pair = gg_pair.reshape(rows, span)

        size = rows // CHUNKS
        per = own // size
        chunks = {}

        def products():
            def more(total, gg, x):
                return (total + cols_dot(gg, x)).astype(jnp.bfloat16)

            own_near = run(cols_dot, gg_mine, near)
            near_part = run(more, own_near, gg_pair, pair_near)
            own_far = run(cols_dot, gg_mine, far)
            far_part = run(more, own_far, gg_pair, pair_far)
            for k in range(CHUNKS):
                at = slice(k * size, (k + 1) * size)
                chunks[k] = jnp.concatenate([near_part[at], far_part[at]], axis=1)

        def fill_send():
            (give,) = run(
                lambda *given: whole(add, [(own_shape, sent_type)], *given),
                kept["sum", 1, 0],
                kept["cross", 1],
            )
            kept["pair"] = lax.ppermute(give, "dp", pairs)

        def unmixed(total, slots):
            return (
                lax.dot_general(
                    total, slots, (((1,), (1,)), ((), ())), preferred_element_type=jnp.float32
                ),
            )

        def send(name, value):
            kept[name] = lax.ppermute(done(value), "dp", pairs)

        def receive(name):
            kept[name] = done(kept[name])

        def fill_input():
            def total(near_sum, cross, pair, slots):
                total = near_sum + cross.astype(jnp.float32) + pair.astype(jnp.float32)
                return unmixed(total.astype(jnp.bfloat16), slots)

            (total,) = run(
                lambda *given: whole(total, [(own_shape, sent_type)], *given),
                kept["sum", 0, 0],
                kept["cross", 0],
                kept["pair"],
                slots,
            )
            kept["input"] = total.T

        def fill_hidden():
            low, high = done((hidden_mine, kept["hidden"]))
            low, high = jnp.where(is_low, low, high), jnp.where(is_low, high, low)

            def both(low, high, slots):
                return unmixed(jnp.concatenate([low, high], axis=0), slots)

            (total,) = run(
                lambda *given: whole(both, [(own_shape, sent_type)], *given), low, high, slots
            )
            kept["hidden out"] = total.T

        position = lax.axis_index("dp") // 2
        inner = (position == 1) | (position == 2)

        def fill_bias(stage):
            def run_stage():
                if stage == 0:
                    kept["bias"] = run(jnp.add, sums_mine, sums_pair)
                    moves = [(0, 1), (1, 0), (2, 3), (3, 2)]
                elif stage == 1:
                    kept["bias"] = run(jnp.add, kept["bias"], kept["bias got"])
                    moves = [(1, 2), (2, 1)]
                elif stage == 2:
                    kept["bias"] = run(jnp.add, kept["bias"], kept["bias got"])
                    moves = [(1, 0), (2, 3), (0, 1), (3, 2)]
                elif stage == 3:
                    kept["bias"] = run(
                        lambda a, b: jnp.where(inner, a, b), kept["bias"], kept["bias got"]
                    )
                if stage < 3:
                    kept["bias got"] = lax.ppermute(kept["bias"], "dp", line_pairs(moves))
                elif stage == 3:
                    kept["bias got"] = lax.ppermute(kept["bias"], "dp", pairs)
                else:
                    kept["bias got"] = done(kept["bias got"])

            return run_stage

        flags = jnp.stack([side, place // 2]).astype(jnp.int32)
        kept["out"] = None

        swapped = {}

        def arrived(k, finals, got):
            swapped[k] = got
            group = k // per
            members = range(group * per, (group + 1) * per)
            if k == members[-1]:
                parts = done(([finals[m] for m in members], [swapped[m] for m in members]))
                kept["out"] = done(write_chunks(flags, *parts, group, kept["out"], (2 * rows, depth)))

        def fill(*steps):
            def run_all():
                for step, *given in steps:
                    step(*given)

            return run_all

        fill_bias(0)()
        send("hidden", hidden_pair)
        fill_back(1, 1)
        fill_back(1, 0)
        fill_core(1, 1)
        fill_cross(1)
        fill_bias(1)()
        fill_back(0, 1)
        fill_core(1, 0)
        fill_bias(2)()
        fill_back(0, 0)
        fill_core(0, 1)
        fill_bias(3)()
        products()
        fill_core(0, 0)
        receive("hidden")
        fill_bias(4)()
        fillers = {
            0: fill((receive, ("cross", 1)), (fill_cross, 0)),
            1: fill((fill_send,)),
            3: fill((receive, ("cross", 0))),
            4: fill((receive, "pair")),
            CHUNKS - 1: fill((fill_hidden,)),
            CHUNKS: fill((send, "sums", sums_pair)),
            CHUNKS + 2: fill((receive, "sums"), (fill_input,)),
        }
        piped_sums(done, chunks, pairs, fillers, arrived)
        input_grad, hidden = kept["input"], kept["hidden out"]
        wgrad = kept["out"].reshape(2, 3, width, depth)
        bias_grad = join(is_low, kept["bias"], kept["bias got"], 0)[:, 2:5].T
        sums_mine, sums_other = done.token, kept["sums"]
    else:
        x_own = mix(inputs.T, slots)
        grads = mix(out_grad.T, slots)
        grads_mine, grads_other = half(grads, 0, side), half(grads, 0, other_side)
        grads_pair = lax.ppermute(grads_other, "dp", pairs)
        small_pair = lax.ppermute(small_other, "dp", pairs)
        length_pair = small_pair[0, 5:6].astype(jnp.int32)
        small_pair = jnp.where(lane[:own] < 3, small_mine, small_pair)
        x_all = lax.all_gather(x_own, "mp", axis=0, tiled=True)
        x_pair = lax.all_gather(lax.ppermute(x_own, "dp", pairs), "mp", axis=0, tiled=True)
        w_mine = half(w_rows, 2, side).reshape(rows, depth)
        w_other = half(w_rows, 2, other_side).reshape(rows, depth)
        hidden_mine, sums_mine, gg_mine = pooled(
            times(w_mine, x_all), lengths, small_mine, grads_mine
        )
        _, sums_pair, gg_pair = pooled(times(w_mine, x_pair), length_pair, small_pair, grads_pair)
        hidden_other, sums_other, gg_other = pooled(
            times(w_other, x_all), lengths, small_other, grads_other
        )
        part = cols_dot(gg_mine, x_all) + cols_dot(gg_pair, x_pair)
        total = line_sum(part.astype(jnp.bfloat16), line)
        theirs = lax.ppermute(total, "dp", pairs)
        shape = (2, 3, own, depth)
        wgrad = join(is_low, total.reshape(shape), theirs.reshape(shape), 2).astype(jnp.float32)
        back = rows_dot(w_mine, gg_mine) + rows_dot(w_other, gg_other)
        input_grad = lax.psum_scatter(
            back.astype(jnp.bfloat16), "mp", scatter_dimension=0, tiled=True
        )
        input_grad = mix(input_grad, slots, back=True).T
        hidden = mix(join(is_low, hidden_mine, hidden_other, 0), slots, back=True).T
        bias_mine = line_sum(sums_mine + sums_pair, line)
        bias_pair = lax.ppermute(bias_mine, "dp", pairs)
        bias_grad = join(is_low, bias_mine, bias_pair, 0)[:, 2:5].T

    sums = join(is_low, sums_mine, sums_other, 0)
    return (
        hidden,
        sums[:, 0:1].T,
        input_grad,
        sums[:, 1:2].T,
        jnp.transpose(wgrad, (0, 3, 1, 2)),
        bias_grad,
    )


def solution(mesh):
    in_specs = (
        P("dp", "mp"),
        P("dp"),
        P("dp", "mp"),
        P(None, None, None, "mp"),
        P(None, "mp"),
        P("dp", "mp"),
        P("dp", "mp"),
    )
    out_specs = (
        P("dp", "mp"),
        P("dp", "mp"),
        P("dp", "mp"),
        P("dp", "mp"),
        P(None, None, None, "mp"),
        P(None, "mp"),
    )
    body = functools.partial(on_device, mesh.shape["dp"] // 2, mesh.shape["mp"])
    return jax.shard_map(
        body, mesh=mesh, in_specs=in_specs, out_specs=out_specs, check_vma=False
    )
```

```python
import functools

import jax
import jax.numpy as jnp
from jax import lax
from jax.experimental import pallas as pl
from jax.experimental.pallas import tpu as pltpu
from jax.sharding import PartitionSpec as P

LANES = 128
ROWS = 16
CHUNKS = 18
PART = 144
LAG = 4
HIDDEN_COST = pl.CostEstimate(flops=1, bytes_accessed=1, transcendentals=0)


def pool_kernel(length_ref, gates_ref, small_ref, grad_ref, hidden_ref, sums_ref, gg_ref, held):
    part, span = grad_ref.shape
    tiles = span // LANES
    length = length_ref[0]
    lane = lax.broadcasted_iota(jnp.int32, (ROWS, LANES), 1)
    zero = jnp.zeros((ROWS, LANES), jnp.float32)
    one = zero + 1.0
    first_lane = lane == 0
    last_lane = lane == LANES - 1
    cand_at, forget_at, out_at = 0, 1, 2
    run_at, back_at, decay_at = 0, 1, 2
    held_gates, held_runs = held

    def tile_of(j):
        return pl.ds(j * LANES, LANES)

    def is_live(j):
        return lane * tiles + j < length

    def local(step, unused):
        rows = pl.ds(pl.multiple_of(step * ROWS, ROWS), ROWS)
        small = small_ref[rows, :]
        bias = [jnp.broadcast_to(small[:, k : k + 1], (ROWS, LANES)) for k in range(3)]
        end_grad = jnp.where(last_lane, jnp.broadcast_to(small[:, 4:5], (ROWS, LANES)), 0.0)
        earlier = [
            jnp.where(first_lane, 0.0, pltpu.roll(gates_ref[1, k, rows, tile_of(tiles - 1)], 1, 1))
            for k in range(3)
        ]
        run, product, back = zero, one, zero
        for j in range(tiles):
            gates = []
            for k in range(3):
                gates.append(gates_ref[0, k, rows, tile_of(j)] + earlier[k] + bias[k])
                earlier[k] = gates_ref[1, k, rows, tile_of(j)]
            live = is_live(j)
            cand = jnp.tanh(gates[0])
            forget = jax.nn.sigmoid(gates[1])
            out_gate = jnp.where(live, 0.5 * jnp.tanh(0.5 * gates[2]) + 0.5, 0.0)
            kept = jnp.where(live, 1.0 - forget, 0.0)
            decay = 1.0 - kept
            emitted = out_gate * grad_ref[rows, tile_of(j)].astype(jnp.float32)
            if j == tiles - 1:
                emitted = emitted + end_grad
            run = decay * run + kept * cand
            product = product * decay
            back = back + product * emitted
            held_gates[cand_at, rows, tile_of(j)] = cand
            held_gates[forget_at, rows, tile_of(j)] = forget
            held_gates[out_at, rows, tile_of(j)] = out_gate
        held_runs[run_at, rows, :] = run
        held_runs[back_at, rows, :] = back
        held_runs[decay_at, rows, :] = product
        return unused

    lax.fori_loop(0, part // ROWS, local, 0)

    wide = lax.broadcasted_iota(jnp.int32, (part, LANES), 1)
    begin = jnp.broadcast_to(small_ref[:, 3:4], (part, LANES))
    run, back, product = held_runs[run_at], held_runs[back_at], held_runs[decay_at]
    run = jnp.where(wide == 0, run + product * begin, run)
    up = product
    for k in (1, 2, 4, 8, 16, 32, 64):
        inside = wide >= k
        run = run + up * jnp.where(inside, pltpu.roll(run, k, 1), 0.0)
        up = up * jnp.where(inside, pltpu.roll(up, k, 1), 1.0)
        inside = wide < LANES - k
        back = back + product * jnp.where(inside, pltpu.roll(back, LANES - k, 1), 0.0)
        product = product * jnp.where(inside, pltpu.roll(product, LANES - k, 1), 1.0)
    held_runs[run_at] = jnp.where(wide == 0, begin, pltpu.roll(run, 1, 1))
    held_runs[decay_at] = jnp.where(wide == LANES - 1, 0.0, pltpu.roll(back, LANES - 1, 1))
    last_cell = jnp.broadcast_to(run[:, LANES - 1 :], (part, LANES))
    sums_ref[...] = jnp.where(wide == 0, last_cell, 0.0) + jnp.where(
        wide == 1, jnp.broadcast_to(back[:, :1], (part, LANES)), 0.0
    )

    def final(step, unused):
        rows = pl.ds(pl.multiple_of(step * ROWS, ROWS), ROWS)
        small = small_ref[rows, :]
        end_grad = jnp.where(last_lane, jnp.broadcast_to(small[:, 4:5], (ROWS, LANES)), 0.0)
        before = held_runs[run_at, rows, :]
        cells, befores = [], []
        for j in range(tiles):
            cand = held_gates[cand_at, rows, tile_of(j)]
            kept = jnp.where(is_live(j), 1.0 - held_gates[forget_at, rows, tile_of(j)], 0.0)
            cell = (1.0 - kept) * before + kept * cand
            befores.append(before)
            cells.append(cell)
            before = cell
        follow = held_runs[decay_at, rows, :]
        bias_sum = [zero] * 3
        for j in range(tiles - 1, -1, -1):
            cand = held_gates[cand_at, rows, tile_of(j)]
            forget = held_gates[forget_at, rows, tile_of(j)]
            out_gate = held_gates[out_at, rows, tile_of(j)]
            kept = jnp.where(is_live(j), 1.0 - forget, 0.0)
            emitted = out_gate * grad_ref[rows, tile_of(j)].astype(jnp.float32)
            hidden_ref[rows, tile_of(j)] = (out_gate * cells[j]).astype(jnp.bfloat16)
            out_part = emitted * cells[j] * (1.0 - out_gate)
            if j == tiles - 1:
                emitted = emitted + end_grad
            cell_grad = emitted + follow
            follow = (1.0 - kept) * cell_grad
            shared = cell_grad * kept
            parts = [
                shared * (1.0 - cand * cand),
                shared * (befores[j] - cand) * forget,
                out_part,
            ]
            for k in range(3):
                rounded = parts[k].astype(jnp.bfloat16)
                gg_ref[0, k, rows, tile_of(j)] = rounded
                wide_part = rounded.astype(jnp.float32)
                bias_sum[k] = bias_sum[k] + wide_part
                if j > 0:
                    gg_ref[1, k, rows, tile_of(j - 1)] = rounded
                else:
                    moved = jnp.where(last_lane, 0.0, pltpu.roll(wide_part, LANES - 1, 1))
                    gg_ref[1, k, rows, tile_of(tiles - 1)] = moved.astype(jnp.bfloat16)
        answer = sums_ref[rows, :]
        for k in range(3):
            total = jnp.sum(bias_sum[k], axis=1, keepdims=True)
            answer = jnp.where(lane == 2 + k, jnp.broadcast_to(total, (ROWS, LANES)), answer)
        sums_ref[rows, :] = answer
        return unused

    lax.fori_loop(0, part // ROWS, final, 0)


def pool(length, gates, small, grad):
    taps, kinds, width, span = gates.shape
    part = next(p for p in (96, 48, 16) if width % p == 0)
    return pl.pallas_call(
        lambda *refs: pool_kernel(*refs[:-2], refs[-2:]),
        grid=(width // part,),
        in_specs=[
            pl.BlockSpec(memory_space=pltpu.SMEM),
            pl.BlockSpec((2, 3, part, span), lambda i: (0, 0, i, 0)),
            pl.BlockSpec((part, LANES), lambda i: (i, 0)),
            pl.BlockSpec((part, span), lambda i: (i, 0)),
        ],
        out_specs=[
            pl.BlockSpec((part, span), lambda i: (i, 0)),
            pl.BlockSpec((part, LANES), lambda i: (i, 0)),
            pl.BlockSpec((2, 3, part, span), lambda i: (0, 0, i, 0)),
        ],
        out_shape=[
            jax.ShapeDtypeStruct((width, span), jnp.bfloat16),
            jax.ShapeDtypeStruct((width, LANES), jnp.float32),
            jax.ShapeDtypeStruct((2, 3, width, span), jnp.bfloat16),
        ],
        scratch_shapes=[
            pltpu.VMEM((3, part, span), jnp.float32),
            pltpu.VMEM((3, part, LANES), jnp.float32),
        ],
        compiler_params=pltpu.CompilerParams(vmem_limit_bytes=40 * 2**20),
        cost_estimate=HIDDEN_COST,
        name="pool",
    )(length, gates, small, grad)


def small_columns(bias, start_cell, cell_grad):
    stacked = jnp.concatenate([bias.astype(jnp.float32), start_cell, cell_grad], axis=0)
    return jnp.pad(stacked.T, ((0, 0), (0, LANES - 5)))


def slot_order(span):
    tiles = span // LANES
    slot = lax.broadcasted_iota(jnp.int32, (span, span), 0)
    place = lax.broadcasted_iota(jnp.int32, (span, span), 1)
    return (place == (slot % tiles) * LANES + slot // tiles).astype(jnp.bfloat16)


def mix(block, order, back=False):
    dims = (((1,), (1 if back else 0,)), ((), ()))
    return lax.dot_general(block, order, dims, preferred_element_type=jnp.float32).astype(jnp.bfloat16)


def times(left, right):
    return jnp.dot(left, right, preferred_element_type=jnp.float32)


def rows_dot(left, right):
    return lax.dot_general(left, right, (((0,), (0,)), ((), ())), preferred_element_type=jnp.float32)


def cols_dot(left, right):
    return lax.dot_general(left, right, (((1,), (1,)), ((), ())), preferred_element_type=jnp.float32)


def once(shape):
    zeros = (0,) * len(shape)
    return pl.BlockSpec(shape, lambda *at: zeros, pipeline_mode=pl.Buffered(1))


def gates_kernel(pick_ref, low_ref, high_ref, w_ref, out_ref, x_ref, *copy_refs):
    half_rows = low_ref.shape[0]

    @pl.when(pl.program_id(0) == 0)
    def _():
        at = pl.multiple_of(pick_ref[2] * half_rows, 64)
        x_ref[pl.ds(at, half_rows), :] = low_ref[...]
        at = pl.multiple_of((1 - pick_ref[2]) * half_rows, 64)
        x_ref[pl.ds(at, half_rows), :] = high_ref[...]

    kinds, width = w_ref.shape[1:3]
    weights = w_ref[0].reshape(kinds * width, w_ref.shape[3])
    total = jnp.dot(weights, x_ref[...], preferred_element_type=jnp.float32)
    out_ref[...] = total.reshape(out_ref.shape)
    for copy_ref in copy_refs:
        copy_ref[...] = w_ref[...]


def gates_step(pick, w_rows, own, sibling, copy):
    taps, kinds, width, depth = w_rows.shape
    rows, span = own.shape
    block = lambda last: pl.BlockSpec((1, kinds, width // 2, last), lambda g, p: (g, 0, 0, 0))
    specs = [
        once((rows, span)),
        once((rows, span)),
        pl.BlockSpec((1, kinds, width // 2, 2 * rows), lambda g, p: (g, 0, p[0], p[1])),
    ]
    operands = [own, sibling, w_rows]
    out_specs = [block(span), pl.BlockSpec((2 * rows, span), lambda g, p: (0, 0))]
    out_shape = [
        jax.ShapeDtypeStruct((taps, kinds, width // 2, span), jnp.float32),
        jax.ShapeDtypeStruct((2 * rows, span), jnp.bfloat16),
    ]
    if copy:
        out_specs.append(block(2 * rows))
        out_shape.append(jax.ShapeDtypeStruct((taps, kinds, width // 2, 2 * rows), jnp.bfloat16))
    return pl.pallas_call(
        gates_kernel,
        grid_spec=pltpu.PrefetchScalarGridSpec(
            num_scalar_prefetch=1,
            grid=(taps,),
            in_specs=specs,
            out_specs=out_specs,
        ),
        out_shape=out_shape,
        compiler_params=pltpu.CompilerParams(vmem_limit_bytes=32 * 2**20),
        cost_estimate=HIDDEN_COST,
        name="gates_step",
    )(pick, *operands)


def gates_pool_kernel(pick_ref, length_ref, low_ref, high_ref, w_ref, base_ref, small_ref, grad_ref,
                      hidden_ref, sums_ref, gg_ref, x_ref, *refs):
    half_rows = low_ref.shape[0]

    @pl.when(pl.program_id(0) == 0)
    def _():
        at = pl.multiple_of(pick_ref[2] * half_rows, 64)
        x_ref[pl.ds(at, half_rows), :] = low_ref[...]
        at = pl.multiple_of((1 - pick_ref[2]) * half_rows, 64)
        x_ref[pl.ds(at, half_rows), :] = high_ref[...]

    gates_ref = refs[-3]
    for copy_ref in refs[:-3]:
        copy_ref[...] = w_ref[...]
    weights = w_ref[...].reshape(-1, w_ref.shape[3])
    product = jnp.dot(weights, x_ref[...], preferred_element_type=jnp.float32)
    gates_ref[...] = product.reshape(gates_ref.shape) + base_ref[...]
    pool_kernel(length_ref, gates_ref, small_ref, grad_ref, hidden_ref, sums_ref, gg_ref, refs[-2:])


def pool_shapes(width, span):
    return [
        jax.ShapeDtypeStruct((width, span), jnp.bfloat16),
        jax.ShapeDtypeStruct((width, LANES), jnp.float32),
        jax.ShapeDtypeStruct((2, 3, width, span), jnp.bfloat16),
    ]


def pool_scratch(part, span):
    return [
        pltpu.VMEM((2, 3, part, span), jnp.float32),
        pltpu.VMEM((3, part, span), jnp.float32),
        pltpu.VMEM((3, part, LANES), jnp.float32),
    ]


def gates_pool(pick, length, w_rows, own, sibling, base, small, grad, copy):
    taps, kinds, width, depth = w_rows.shape
    rows, span = own.shape
    width //= 2
    part = PART
    count = width // part
    lines = lambda columns: pl.BlockSpec((part, columns), lambda i, p: (i, 0))
    wide = pl.BlockSpec((taps, kinds, part, span), lambda i, p: (0, 0, i, 0))
    copy_specs, copy_shapes = [], []
    if copy:
        copy_specs = [pl.BlockSpec((taps, kinds, part, 2 * rows), lambda i, p: (0, 0, i, 0))]
        copy_shapes = [jax.ShapeDtypeStruct((taps, kinds, width, 2 * rows), jnp.bfloat16)]
    return pl.pallas_call(
        gates_pool_kernel,
        grid_spec=pltpu.PrefetchScalarGridSpec(
            num_scalar_prefetch=1,
            grid=(count,),
            in_specs=[
                pl.BlockSpec(memory_space=pltpu.SMEM),
                once((rows, span)),
                once((rows, span)),
                pl.BlockSpec(
                    (taps, kinds, part, 2 * rows), lambda i, p: (0, 0, p[0] * count + i, p[1])
                ),
                wide,
                lines(LANES),
                lines(span),
            ],
            out_specs=[
                lines(span),
                lines(LANES),
                wide,
                pl.BlockSpec((2 * rows, span), lambda i, p: (0, 0)),
                *copy_specs,
            ],
            scratch_shapes=pool_scratch(part, span),
        ),
        out_shape=pool_shapes(width, span)
        + [jax.ShapeDtypeStruct((2 * rows, span), jnp.bfloat16)]
        + copy_shapes,
        compiler_params=pltpu.CompilerParams(vmem_limit_bytes=40 * 2**20),
        cost_estimate=HIDDEN_COST,
        name="gates_pool",
    )(pick, length, own, sibling, w_rows, base, small, grad)


def whole_kernel(function, count, *refs):
    results = function(*[ref[...] for ref in refs[:count]])
    for ref, result in zip(refs[count:], results):
        ref[...] = result.astype(ref.dtype)


def whole(function, outputs, *operands):
    return pl.pallas_call(
        functools.partial(whole_kernel, function, len(operands)),
        out_shape=[jax.ShapeDtypeStruct(*output) for output in outputs],
        compiler_params=pltpu.CompilerParams(vmem_limit_bytes=20 * 2**20),
        cost_estimate=HIDDEN_COST,
        name="whole",
    )(*operands)


def back_kernel(pick_ref, w_ref, gg_ref, keep_ref, give_ref, total_ref):
    step = pl.program_id(0)
    columns = w_ref.shape[1]
    total_ref[pl.ds(pl.multiple_of(step * columns, columns), columns), :] = lax.dot_general(
        w_ref[...], gg_ref[...], (((0,), (0,)), ((), ())), preferred_element_type=jnp.float32
    )

    @pl.when(step == pl.num_programs(0) - 1)
    def _():
        rows = keep_ref.shape[0]
        keep_ref[...] = total_ref[pl.ds(pl.multiple_of(pick_ref[2] * rows, 64), rows), :]
        give_ref[...] = total_ref[
            pl.ds(pl.multiple_of((1 - pick_ref[2]) * rows, 64), rows), :
        ].astype(jnp.bfloat16)


def back_products(pick, weights, gg):
    depth, columns = weights.shape
    span = gg.shape[1]
    part = 384
    return pl.pallas_call(
        back_kernel,
        grid_spec=pltpu.PrefetchScalarGridSpec(
            num_scalar_prefetch=1,
            grid=(columns // part,),
            in_specs=[
                pl.BlockSpec((depth, part), lambda i, p: (0, i)),
                once((depth, span)),
            ],
            out_specs=[
                pl.BlockSpec((columns // 2, span), lambda i, p: (0, 0)),
                pl.BlockSpec((columns // 2, span), lambda i, p: (0, 0)),
            ],
            scratch_shapes=[pltpu.VMEM((columns, span), jnp.float32)],
        ),
        out_shape=[
            jax.ShapeDtypeStruct((columns // 2, span), jnp.float32),
            jax.ShapeDtypeStruct((columns // 2, span), jnp.bfloat16),
        ],
        compiler_params=pltpu.CompilerParams(vmem_limit_bytes=26 * 2**20),
        cost_estimate=HIDDEN_COST,
        name="back_products",
    )(pick, weights, gg)


def chunk_kernel(function, inputs, inner_ref, *refs):
    function(inner_ref[0] == 1, *refs[:inputs], *refs[inputs:])


def chunk_step(function, outputs, inner, size, *operands):
    specs, arrays = [pl.BlockSpec(memory_space=pltpu.SMEM)], [inner]
    for operand in operands:
        array, at = operand if isinstance(operand, tuple) else (operand, 0)
        specs.append(pl.BlockSpec((size, array.shape[1]), lambda i, at=at: (at, 0)))
        arrays.append(array)
    depth = arrays[1].shape[1]
    return pl.pallas_call(
        functools.partial(chunk_kernel, function, len(operands)),
        grid=(1,),
        in_specs=specs,
        out_specs=[pl.BlockSpec((size, depth), lambda i: (0, 0))] * outputs,
        out_shape=[jax.ShapeDtypeStruct((size, depth), jnp.bfloat16)] * outputs,
        compiler_params=pltpu.CompilerParams(vmem_limit_bytes=8 * 2**20),
        cost_estimate=HIDDEN_COST,
        name="chunk_step",
    )(*arrays)


def rounded_sum(left_ref, right_ref):
    total = left_ref[...].astype(jnp.float32) + right_ref[...].astype(jnp.float32)
    return total.astype(jnp.bfloat16)


def take_chunk(inner, chunk_ref, out_ref):
    out_ref[...] = chunk_ref[...]


def sum_chunk(inner, chunk_ref, got_ref, sum_ref):
    sum_ref[...] = rounded_sum(chunk_ref, got_ref)


def sum_and_final(inner, chunk_ref, got_ref, total_ref, sum_ref, final_ref):
    sum_ref[...] = rounded_sum(chunk_ref, got_ref)
    final_ref[...] = jnp.where(inner, total_ref[...], got_ref[...])


def total_and_next(inner, sum_ref, got_ref, chunk_ref, total_ref, next_ref):
    total = rounded_sum(sum_ref, got_ref)
    total_ref[...] = total
    next_ref[...] = jnp.where(inner, total, chunk_ref[...])


def final_chunk(inner, got_ref, total_ref, final_ref):
    final_ref[...] = jnp.where(inner, total_ref[...], got_ref[...])


def total_chunk(inner, sum_ref, got_ref, total_ref):
    total_ref[...] = rounded_sum(sum_ref, got_ref)


def even_odd(count):
    return [(i, i ^ 1) for i in range(count)]


def line_pairs(moves):
    return [(2 * a + s, 2 * b + s) for a, b in moves for s in range(2)]


class Order:
    def __init__(self, token):
        self.token = token

    def __call__(self, values):
        values, self.token = lax.optimization_barrier((values, self.token))
        return values


def line_sum(part, length):
    if length & (length - 1) == 0:
        step = 1
        while step < length:
            part = part + lax.ppermute(part, "dp", line_pairs([(i, i ^ step) for i in range(length)]))
            step *= 2
        return part
    total = part
    for _ in range(length - 1):
        part = lax.ppermute(part, "dp", line_pairs([(i, (i + 1) % length) for i in range(length)]))
        total = total + part
    return total


def half(array, axis, which):
    size = array.shape[axis] // 2
    return lax.dynamic_slice_in_dim(array, which * size, size, axis)


def join(low_first, mine, other, axis):
    return jnp.where(
        low_first,
        jnp.concatenate([mine, other], axis=axis),
        jnp.concatenate([other, mine], axis=axis),
    )


def write_kernel(count, flags_ref, *refs):
    out_ref = refs[-1]
    size = refs[0].shape[0]
    middle = refs[0].shape[1] // 2
    mine = flags_ref[0] == pl.program_id(0)
    straight = flags_ref[1] == 0
    for j in range(count):
        at = pl.ds(j * size, size)
        block = jnp.where(mine, refs[j][...], refs[count + j][...]).astype(jnp.float32)
        left, right = block[:, :middle], block[:, middle:]
        out_ref[at, :middle] = jnp.where(straight, left, right)
        out_ref[at, middle:] = jnp.where(straight, right, left)


def write_chunks(flags, mine, theirs, group, whole, shape):
    count = len(mine)
    size, depth = mine[0].shape
    specs = [pl.BlockSpec(memory_space=pltpu.SMEM)]
    specs += [pl.BlockSpec((size, depth), lambda i: (0, 0))] * (2 * count)
    operands = [flags, *mine, *theirs]
    aliases = {}
    if whole is not None:
        specs.append(pl.BlockSpec(memory_space=pl.ANY))
        operands.append(whole)
        aliases = {len(operands) - 1: 0}
    return pl.pallas_call(
        functools.partial(write_kernel, count),
        grid=(2,),
        in_specs=specs,
        out_specs=pl.BlockSpec((count * size, depth), lambda i: (2 * group + i, 0)),
        out_shape=jax.ShapeDtypeStruct(shape, jnp.float32),
        input_output_aliases=aliases,
        compiler_params=pltpu.CompilerParams(vmem_limit_bytes=16 * 2**20),
        cost_estimate=HIDDEN_COST,
        name="write_chunks",
    )(*operands)


def add_times(total, left, right):
    return total + times(left, right)


def add_rounded(left, right):
    return (left.astype(jnp.float32) + right.astype(jnp.float32)).astype(jnp.bfloat16)


def piped_sums(order, chunks, pairs, fillers, arrived):
    position = lax.axis_index("dp") // 2
    inner = (position == 1) | (position == 2)
    flag = inner.astype(jnp.int32).reshape(1)
    edge = line_pairs([(0, 1), (1, 0), (2, 3), (3, 2)])
    middle = line_pairs([(1, 2), (2, 1)])
    sums, totals, finals = {}, {}, {}
    got_edge, got_middle, got_pair = {}, {}, {}
    size = chunks[0].shape[0]

    def run(function, outputs, *operands):
        return order(chunk_step(function, outputs, flag, size, *order(operands)))

    payload = order(chunks[0])
    got_edge[0] = lax.ppermute(payload, "dp", edge)
    for n in range(CHUNKS + LAG + 3):
        final = None
        k = n - 1
        if k in got_edge:
            got = got_edge.pop(k)
            if k < CHUNKS and k >= LAG:
                sums[k], final = run(sum_and_final, 2, chunks[k], got, totals.pop(k - LAG))
            elif k < CHUNKS:
                (sums[k],) = run(sum_chunk, 1, chunks[k], got)
            else:
                (final,) = run(final_chunk, 1, got, totals.pop(k - LAG))
            if k < CHUNKS:
                got_middle[k] = lax.ppermute(sums[k], "dp", middle)
        k = n - 2
        payload = None
        if k in got_middle:
            got = got_middle.pop(k)
            (totals[k],) = run(total_chunk, 1, sums.pop(k), got)
        k = n + 1 - LAG
        if k in totals and n + 1 < CHUNKS:
            (payload,) = run(final_chunk, 1, chunks[n + 1], totals[k])
        elif n + 1 < CHUNKS:
            payload = order(chunks[n + 1])
        elif k in totals:
            payload = totals[k]
        if payload is not None:
            got_edge[n + 1] = lax.ppermute(payload, "dp", edge)
        k = n - 1 - LAG
        if final is not None:
            finals[k] = final
            got_pair[k] = lax.ppermute(final, "dp", pairs)
        k = k - 1
        if k in got_pair:
            arrived(k, finals, order(got_pair.pop(k)))
        if n in fillers:
            fillers[n]()


def on_device(line, channel_parts, inputs, lengths, start_cell, weight, bias, out_grad, cell_grad):
    span, width = inputs.shape
    depth = weight.shape[1]
    own = width // 2
    rows = 6 * own
    side = lax.axis_index("dp") % 2
    other_side = 1 - side
    is_low = side == 0
    pairs = even_odd(2 * line)
    slots = slot_order(span)

    place = lax.axis_index("mp")
    core_low = place % 2 == 0
    near_low = place < 2
    core_pairs = even_odd(channel_parts)
    chip_pairs = [(i, i ^ 2) for i in range(4)]

    def split(array, axis):
        return half(array, axis, place // 2), half(array, axis, 1 - place // 2)

    small = small_columns(bias, start_cell, cell_grad)
    lane = lax.broadcasted_iota(jnp.int32, small.shape, 1)
    small = jnp.where(lane == 5, lengths[0].astype(jnp.float32), small)
    small_mine, small_other = half(small, 0, side), half(small, 0, other_side)
    w_rows = jnp.transpose(weight, (0, 2, 3, 1))

    def pooled(total, length, small_part, grad_part):
        hidden, sums, gg = pool(length, total.reshape(2, 3, own, span), small_part, grad_part)
        return hidden, sums, gg.reshape(rows, span)

    if line == 4 and channel_parts == 4:
        done = Order(out_grad)

        def run(function, *operands):
            return done(function(*done(operands)))

        pick_near = jnp.stack([side, place // 2, place % 2]).astype(jnp.int32)
        pick_far = jnp.stack([side, 1 - place // 2, place % 2]).astype(jnp.int32)
        x_own = run(lambda x: mix(x.T, slots), inputs)
        far_got = lax.ppermute(x_own, "mp", chip_pairs)
        pair_got = lax.ppermute(x_own, "dp", pairs)
        near_got = lax.ppermute(x_own, "mp", core_pairs)
        out_grad, done.token = done.token, small_mine
        grads = run(lambda g: mix(g.T, slots), out_grad)
        grads_mine, grads_other = done((half(grads, 0, side), half(grads, 0, other_side)))
        gates, near, w_near = run(
            lambda *given: gates_step(*given, True), pick_near, w_rows, x_own, near_got
        )
        cut = width * 2 // 3
        far_own = done(far_got)
        far_got = lax.ppermute(far_own, "mp", core_pairs)
        x_pair = done(pair_got)
        relay = [
            lax.ppermute(x_pair[:cut], "mp", chip_pairs),
            lax.ppermute(jnp.concatenate([far_own[cut:], grads_other], axis=0), "dp", pairs),
        ]
        far_got = done(far_got)
        pair_near_got = lax.ppermute(done(x_pair), "mp", core_pairs)
        far_own, far_got, gates, grads_mine = done((far_own, far_got, gates, grads_mine))
        hidden_mine, sums_mine, gg_mine, far, w_far = gates_pool(
            pick_far, lengths, w_rows, far_own, far_got, gates, done.token, grads_mine, True
        )
        done.token = sums_mine
        gg_mine = done(gg_mine.reshape(rows, span))
        pair_far_own, grads_pair = run(
            lambda a, b: (jnp.concatenate([a, b[: width - cut]], axis=0), b[width - cut :]), *relay
        )
        pair_far_got = lax.ppermute(pair_far_own, "mp", core_pairs)
        small_pair = lax.ppermute(done(small_other), "dp", pairs)
        kept = {}

        own_shape, wide_type, sent_type = (width, span), jnp.float32, jnp.bfloat16

        def add(left, right):
            return (left + right.astype(jnp.float32),)

        def add_both(left, right):
            total = left + right.astype(jnp.float32)
            return total, total

        def fill_back(window, part):
            keep, give = run(
                back_products,
                pick_near,
                (w_near, w_far)[part].reshape(rows, depth // 2),
                gg_mine if window == 0 else gg_pair,
            )
            kept["keep", window, part] = keep
            kept["core", window, part] = lax.ppermute(give, "mp", core_pairs)

        def fill_core(window, part):
            kind = wide_type if part == 0 else sent_type
            (kept["sum", window, part],) = run(
                lambda *given: whole(add, [(own_shape, kind)], *given),
                kept["keep", window, part],
                kept["core", window, part],
            )

        def fill_cross(window):
            kept["cross", window] = lax.ppermute(done(kept["sum", window, 1]), "mp", chip_pairs)

        pair_gates, pair_near = run(
            lambda *given: gates_step(*given, False), pick_near, w_rows, x_pair, pair_near_got
        )
        small_pair, grads_pair = done((small_pair, grads_pair))
        length_pair = small_pair[0, 5:6].astype(jnp.int32)
        small_pair = jnp.where(lane[:own] < 3, small_mine, small_pair)
        hidden_pair, sums_pair, gg_pair, pair_far = run(
            lambda *given: gates_pool(*given, False),
            pick_far,
            length_pair,
            w_rows,
            pair_far_own,
            pair_far_got,
            pair_gates,
            small_pair,
            grads_pair,
        )
        gg_pair = gg_pair.reshape(rows, span)

        size = rows // CHUNKS
        per = own // size
        chunks = {}

        def products():
            def more(total, gg, x):
                return (total + cols_dot(gg, x)).astype(jnp.bfloat16)

            own_near = run(cols_dot, gg_mine, near)
            near_part = run(more, own_near, gg_pair, pair_near)
            own_far = run(cols_dot, gg_mine, far)
            far_part = run(more, own_far, gg_pair, pair_far)
            for k in range(CHUNKS):
                at = slice(k * size, (k + 1) * size)
                chunks[k] = jnp.concatenate([near_part[at], far_part[at]], axis=1)

        def fill_send():
            (give,) = run(
                lambda *given: whole(add, [(own_shape, sent_type)], *given),
                kept["sum", 1, 0],
                kept["cross", 1],
            )
            kept["pair"] = lax.ppermute(give, "dp", pairs)

        def unmixed(total, slots):
            return (
                lax.dot_general(
                    total, slots, (((1,), (1,)), ((), ())), preferred_element_type=jnp.float32
                ),
            )

        def send(name, value):
            kept[name] = lax.ppermute(done(value), "dp", pairs)

        def receive(name):
            kept[name] = done(kept[name])

        def fill_input():
            def total(near_sum, cross, pair, slots):
                total = near_sum + cross.astype(jnp.float32) + pair.astype(jnp.float32)
                return unmixed(total.astype(jnp.bfloat16), slots)

            (total,) = run(
                lambda *given: whole(total, [(own_shape, sent_type)], *given),
                kept["sum", 0, 0],
                kept["cross", 0],
                kept["pair"],
                slots,
            )
            kept["input"] = total.T

        def fill_hidden():
            low, high = done((hidden_mine, kept["hidden"]))
            low, high = jnp.where(is_low, low, high), jnp.where(is_low, high, low)

            def both(low, high, slots):
                return unmixed(jnp.concatenate([low, high], axis=0), slots)

            (total,) = run(
                lambda *given: whole(both, [(own_shape, sent_type)], *given), low, high, slots
            )
            kept["hidden out"] = total.T

        position = lax.axis_index("dp") // 2
        inner = (position == 1) | (position == 2)

        def fill_bias(stage):
            def run_stage():
                if stage == 0:
                    kept["bias"] = run(jnp.add, sums_mine, sums_pair)
                    moves = [(0, 1), (1, 0), (2, 3), (3, 2)]
                elif stage == 1:
                    kept["bias"] = run(jnp.add, kept["bias"], kept["bias got"])
                    moves = [(1, 2), (2, 1)]
                elif stage == 2:
                    kept["bias"] = run(jnp.add, kept["bias"], kept["bias got"])
                    moves = [(1, 0), (2, 3), (0, 1), (3, 2)]
                elif stage == 3:
                    kept["bias"] = run(
                        lambda a, b: jnp.where(inner, a, b), kept["bias"], kept["bias got"]
                    )
                if stage < 3:
                    kept["bias got"] = lax.ppermute(kept["bias"], "dp", line_pairs(moves))
                elif stage == 3:
                    kept["bias got"] = lax.ppermute(kept["bias"], "dp", pairs)
                else:
                    kept["bias got"] = done(kept["bias got"])

            return run_stage

        flags = jnp.stack([side, place // 2]).astype(jnp.int32)
        kept["out"] = None

        swapped = {}

        def arrived(k, finals, got):
            swapped[k] = got
            group = k // per
            members = range(group * per, (group + 1) * per)
            if k == members[-1]:
                parts = done(([finals[m] for m in members], [swapped[m] for m in members]))
                kept["out"] = done(write_chunks(flags, *parts, group, kept["out"], (2 * rows, depth)))

        def fill(*steps):
            def run_all():
                for step, *given in steps:
                    step(*given)

            return run_all

        fill_bias(0)()
        fill_bias(0)()
        fill_bias(0)()
        fill_bias(0)()
        send("hidden", hidden_pair)
        fill_back(1, 1)
        fill_back(1, 0)
        fill_core(1, 1)
        fill_cross(1)
        fill_bias(1)()
        fill_back(0, 1)
        fill_core(1, 0)
        fill_back(0, 0)
        fill_bias(2)()
        fill_core(0, 1)
        products()
        fill_core(0, 0)
        receive("hidden")
        fill_bias(3)()
        fillers = {
            0: fill((receive, ("cross", 1)), (fill_cross, 0), (fill_bias(4),)),
            1: fill((fill_send,)),
            3: fill((receive, ("cross", 0))),
            4: fill((receive, "pair")),
            CHUNKS - 1: fill((fill_hidden,)),
            CHUNKS: fill((send, "sums", sums_pair)),
            CHUNKS + 2: fill((receive, "sums"), (fill_input,)),
        }
        piped_sums(done, chunks, pairs, fillers, arrived)
        input_grad, hidden = kept["input"], kept["hidden out"]
        wgrad = kept["out"].reshape(2, 3, width, depth)
        bias_grad = join(is_low, kept["bias"], kept["bias got"], 0)[:, 2:5].T
        sums_mine, sums_other = done.token, kept["sums"]
    else:
        x_own = mix(inputs.T, slots)
        grads = mix(out_grad.T, slots)
        grads_mine, grads_other = half(grads, 0, side), half(grads, 0, other_side)
        grads_pair = lax.ppermute(grads_other, "dp", pairs)
        small_pair = lax.ppermute(small_other, "dp", pairs)
        length_pair = small_pair[0, 5:6].astype(jnp.int32)
        small_pair = jnp.where(lane[:own] < 3, small_mine, small_pair)
        x_all = lax.all_gather(x_own, "mp", axis=0, tiled=True)
        x_pair = lax.all_gather(lax.ppermute(x_own, "dp", pairs), "mp", axis=0, tiled=True)
        w_mine = half(w_rows, 2, side).reshape(rows, depth)
        w_other = half(w_rows, 2, other_side).reshape(rows, depth)
        hidden_mine, sums_mine, gg_mine = pooled(
            times(w_mine, x_all), lengths, small_mine, grads_mine
        )
        _, sums_pair, gg_pair = pooled(times(w_mine, x_pair), length_pair, small_pair, grads_pair)
        hidden_other, sums_other, gg_other = pooled(
            times(w_other, x_all), lengths, small_other, grads_other
        )
        part = cols_dot(gg_mine, x_all) + cols_dot(gg_pair, x_pair)
        total = line_sum(part.astype(jnp.bfloat16), line)
        theirs = lax.ppermute(total, "dp", pairs)
        shape = (2, 3, own, depth)
        wgrad = join(is_low, total.reshape(shape), theirs.reshape(shape), 2).astype(jnp.float32)
        back = rows_dot(w_mine, gg_mine) + rows_dot(w_other, gg_other)
        input_grad = lax.psum_scatter(
            back.astype(jnp.bfloat16), "mp", scatter_dimension=0, tiled=True
        )
        input_grad = mix(input_grad, slots, back=True).T
        hidden = mix(join(is_low, hidden_mine, hidden_other, 0), slots, back=True).T
        bias_mine = line_sum(sums_mine + sums_pair, line)
        bias_pair = lax.ppermute(bias_mine, "dp", pairs)
        bias_grad = join(is_low, bias_mine, bias_pair, 0)[:, 2:5].T

    sums = join(is_low, sums_mine, sums_other, 0)
    return (
        hidden,
        sums[:, 0:1].T,
        input_grad,
        sums[:, 1:2].T,
        jnp.transpose(wgrad, (0, 3, 1, 2)),
        bias_grad,
    )


def solution(mesh):
    in_specs = (
        P("dp", "mp"),
        P("dp"),
        P("dp", "mp"),
        P(None, None, None, "mp"),
        P(None, "mp"),
        P("dp", "mp"),
        P("dp", "mp"),
    )
    out_specs = (
        P("dp", "mp"),
        P("dp", "mp"),
        P("dp", "mp"),
        P("dp", "mp"),
        P(None, None, None, "mp"),
        P(None, "mp"),
    )
    body = functools.partial(on_device, mesh.shape["dp"] // 2, mesh.shape["mp"])
    return jax.shard_map(
        body, mesh=mesh, in_specs=in_specs, out_specs=out_specs, check_vma=False
    )
```

```python
import functools

import jax
import jax.numpy as jnp
from jax import lax
from jax.experimental import pallas as pl
from jax.experimental.pallas import tpu as pltpu
from jax.sharding import PartitionSpec as P

LANES = 128
ROWS = 16
CHUNKS = 18
PART = 144
LAG = 4
HIDDEN_COST = pl.CostEstimate(flops=1, bytes_accessed=1, transcendentals=0)


def pool_kernel(length_ref, gates_ref, small_ref, grad_ref, hidden_ref, sums_ref, gg_ref, held):
    part, span = grad_ref.shape
    tiles = span // LANES
    length = length_ref[0]
    lane = lax.broadcasted_iota(jnp.int32, (ROWS, LANES), 1)
    zero = jnp.zeros((ROWS, LANES), jnp.float32)
    one = zero + 1.0
    first_lane = lane == 0
    last_lane = lane == LANES - 1
    cand_at, forget_at, out_at = 0, 1, 2
    run_at, back_at, decay_at = 0, 1, 2
    held_gates, held_runs = held

    def tile_of(j):
        return pl.ds(j * LANES, LANES)

    def is_live(j):
        return lane * tiles + j < length

    def local(step, unused):
        rows = pl.ds(pl.multiple_of(step * ROWS, ROWS), ROWS)
        small = small_ref[rows, :]
        bias = [jnp.broadcast_to(small[:, k : k + 1], (ROWS, LANES)) for k in range(3)]
        end_grad = jnp.where(last_lane, jnp.broadcast_to(small[:, 4:5], (ROWS, LANES)), 0.0)
        earlier = [
            jnp.where(first_lane, 0.0, pltpu.roll(gates_ref[1, k, rows, tile_of(tiles - 1)], 1, 1))
            for k in range(3)
        ]
        run, product, back = zero, one, zero
        for j in range(tiles):
            gates = []
            for k in range(3):
                gates.append(gates_ref[0, k, rows, tile_of(j)] + earlier[k] + bias[k])
                earlier[k] = gates_ref[1, k, rows, tile_of(j)]
            live = is_live(j)
            cand = jnp.tanh(gates[0])
            forget = jax.nn.sigmoid(gates[1])
            out_gate = jnp.where(live, 0.5 * jnp.tanh(0.5 * gates[2]) + 0.5, 0.0)
            kept = jnp.where(live, 1.0 - forget, 0.0)
            decay = 1.0 - kept
            emitted = out_gate * grad_ref[rows, tile_of(j)].astype(jnp.float32)
            if j == tiles - 1:
                emitted = emitted + end_grad
            run = decay * run + kept * cand
            product = product * decay
            back = back + product * emitted
            held_gates[cand_at, rows, tile_of(j)] = cand
            held_gates[forget_at, rows, tile_of(j)] = forget
            held_gates[out_at, rows, tile_of(j)] = out_gate
        held_runs[run_at, rows, :] = run
        held_runs[back_at, rows, :] = back
        held_runs[decay_at, rows, :] = product
        return unused

    lax.fori_loop(0, part // ROWS, local, 0)

    wide = lax.broadcasted_iota(jnp.int32, (part, LANES), 1)
    begin = jnp.broadcast_to(small_ref[:, 3:4], (part, LANES))
    run, back, product = held_runs[run_at], held_runs[back_at], held_runs[decay_at]
    run = jnp.where(wide == 0, run + product * begin, run)
    up = product
    for k in (1, 2, 4, 8, 16, 32, 64):
        inside = wide >= k
        run = run + up * jnp.where(inside, pltpu.roll(run, k, 1), 0.0)
        up = up * jnp.where(inside, pltpu.roll(up, k, 1), 1.0)
        inside = wide < LANES - k
        back = back + product * jnp.where(inside, pltpu.roll(back, LANES - k, 1), 0.0)
        product = product * jnp.where(inside, pltpu.roll(product, LANES - k, 1), 1.0)
    held_runs[run_at] = jnp.where(wide == 0, begin, pltpu.roll(run, 1, 1))
    held_runs[decay_at] = jnp.where(wide == LANES - 1, 0.0, pltpu.roll(back, LANES - 1, 1))
    last_cell = jnp.broadcast_to(run[:, LANES - 1 :], (part, LANES))
    sums_ref[...] = jnp.where(wide == 0, last_cell, 0.0) + jnp.where(
        wide == 1, jnp.broadcast_to(back[:, :1], (part, LANES)), 0.0
    )

    def final(step, unused):
        rows = pl.ds(pl.multiple_of(step * ROWS, ROWS), ROWS)
        small = small_ref[rows, :]
        end_grad = jnp.where(last_lane, jnp.broadcast_to(small[:, 4:5], (ROWS, LANES)), 0.0)
        before = held_runs[run_at, rows, :]
        cells, befores = [], []
        for j in range(tiles):
            cand = held_gates[cand_at, rows, tile_of(j)]
            kept = jnp.where(is_live(j), 1.0 - held_gates[forget_at, rows, tile_of(j)], 0.0)
            cell = (1.0 - kept) * before + kept * cand
            befores.append(before)
            cells.append(cell)
            before = cell
        follow = held_runs[decay_at, rows, :]
        bias_sum = [zero] * 3
        for j in range(tiles - 1, -1, -1):
            cand = held_gates[cand_at, rows, tile_of(j)]
            forget = held_gates[forget_at, rows, tile_of(j)]
            out_gate = held_gates[out_at, rows, tile_of(j)]
            kept = jnp.where(is_live(j), 1.0 - forget, 0.0)
            emitted = out_gate * grad_ref[rows, tile_of(j)].astype(jnp.float32)
            hidden_ref[rows, tile_of(j)] = (out_gate * cells[j]).astype(jnp.bfloat16)
            out_part = emitted * cells[j] * (1.0 - out_gate)
            if j == tiles - 1:
                emitted = emitted + end_grad
            cell_grad = emitted + follow
            follow = (1.0 - kept) * cell_grad
            shared = cell_grad * kept
            parts = [
                shared * (1.0 - cand * cand),
                shared * (befores[j] - cand) * forget,
                out_part,
            ]
            for k in range(3):
                rounded = parts[k].astype(jnp.bfloat16)
                gg_ref[0, k, rows, tile_of(j)] = rounded
                wide_part = rounded.astype(jnp.float32)
                bias_sum[k] = bias_sum[k] + wide_part
                if j > 0:
                    gg_ref[1, k, rows, tile_of(j - 1)] = rounded
                else:
                    moved = jnp.where(last_lane, 0.0, pltpu.roll(wide_part, LANES - 1, 1))
                    gg_ref[1, k, rows, tile_of(tiles - 1)] = moved.astype(jnp.bfloat16)
        answer = sums_ref[rows, :]
        for k in range(3):
            total = jnp.sum(bias_sum[k], axis=1, keepdims=True)
            answer = jnp.where(lane == 2 + k, jnp.broadcast_to(total, (ROWS, LANES)), answer)
        sums_ref[rows, :] = answer
        return unused

    lax.fori_loop(0, part // ROWS, final, 0)


def pool(length, gates, small, grad):
    taps, kinds, width, span = gates.shape
    part = next(p for p in (96, 48, 16) if width % p == 0)
    return pl.pallas_call(
        lambda *refs: pool_kernel(*refs[:-2], refs[-2:]),
        grid=(width // part,),
        in_specs=[
            pl.BlockSpec(memory_space=pltpu.SMEM),
            pl.BlockSpec((2, 3, part, span), lambda i: (0, 0, i, 0)),
            pl.BlockSpec((part, LANES), lambda i: (i, 0)),
            pl.BlockSpec((part, span), lambda i: (i, 0)),
        ],
        out_specs=[
            pl.BlockSpec((part, span), lambda i: (i, 0)),
            pl.BlockSpec((part, LANES), lambda i: (i, 0)),
            pl.BlockSpec((2, 3, part, span), lambda i: (0, 0, i, 0)),
        ],
        out_shape=[
            jax.ShapeDtypeStruct((width, span), jnp.bfloat16),
            jax.ShapeDtypeStruct((width, LANES), jnp.float32),
            jax.ShapeDtypeStruct((2, 3, width, span), jnp.bfloat16),
        ],
        scratch_shapes=[
            pltpu.VMEM((3, part, span), jnp.float32),
            pltpu.VMEM((3, part, LANES), jnp.float32),
        ],
        compiler_params=pltpu.CompilerParams(vmem_limit_bytes=40 * 2**20),
        cost_estimate=HIDDEN_COST,
        name="pool",
    )(length, gates, small, grad)


def small_columns(bias, start_cell, cell_grad):
    stacked = jnp.concatenate([bias.astype(jnp.float32), start_cell, cell_grad], axis=0)
    return jnp.pad(stacked.T, ((0, 0), (0, LANES - 5)))


def slot_order(span):
    tiles = span // LANES
    slot = lax.broadcasted_iota(jnp.int32, (span, span), 0)
    place = lax.broadcasted_iota(jnp.int32, (span, span), 1)
    return (place == (slot % tiles) * LANES + slot // tiles).astype(jnp.bfloat16)


def mix(block, order, back=False):
    dims = (((1,), (1 if back else 0,)), ((), ()))
    return lax.dot_general(block, order, dims, preferred_element_type=jnp.float32).astype(jnp.bfloat16)


def times(left, right):
    return jnp.dot(left, right, preferred_element_type=jnp.float32)


def rows_dot(left, right):
    return lax.dot_general(left, right, (((0,), (0,)), ((), ())), preferred_element_type=jnp.float32)


def cols_dot(left, right):
    return lax.dot_general(left, right, (((1,), (1,)), ((), ())), preferred_element_type=jnp.float32)


def once(shape):
    zeros = (0,) * len(shape)
    return pl.BlockSpec(shape, lambda *at: zeros, pipeline_mode=pl.Buffered(1))


def gates_kernel(skip, pick_ref, low_ref, high_ref, w_ref, *refs):
    out_ref, x_ref, *copy_refs = refs[skip:]
    half_rows = low_ref.shape[0]

    @pl.when(pl.program_id(0) == 0)
    def _():
        at = pl.multiple_of(pick_ref[2] * half_rows, 64)
        x_ref[pl.ds(at, half_rows), :] = low_ref[...]
        at = pl.multiple_of((1 - pick_ref[2]) * half_rows, 64)
        x_ref[pl.ds(at, half_rows), :] = high_ref[...]

    kinds, width = w_ref.shape[1:3]
    weights = w_ref[0].reshape(kinds * width, w_ref.shape[3])
    total = jnp.dot(weights, x_ref[...], preferred_element_type=jnp.float32)
    out_ref[...] = total.reshape(out_ref.shape)
    for copy_ref in copy_refs:
        copy_ref[...] = w_ref[...]


def gates_step(pick, w_rows, own, sibling, copy, window, held):
    taps, kinds, width, depth = w_rows.shape
    rows, span = own.shape
    block = lambda last: pl.BlockSpec((1, kinds, width // 2, last), lambda g, p: (g, 0, 0, 0))
    specs = [
        once((rows, span)),
        once((rows, span)),
        pl.BlockSpec((1, kinds, width // 2, 2 * rows), lambda g, p: (g, 0, p[0], p[1])),
    ]
    operands = [own, sibling, w_rows]
    aliases = {}
    if held is not None:
        specs.append(pl.BlockSpec(memory_space=pltpu.HBM))
        operands.append(held)
        aliases = {len(operands): 1}
    out_specs = [block(span), pl.BlockSpec((2 * rows, span), lambda g, p: (0, window))]
    out_shape = [
        jax.ShapeDtypeStruct((taps, kinds, width // 2, span), jnp.float32),
        jax.ShapeDtypeStruct((depth, 2 * span), jnp.bfloat16),
    ]
    if copy:
        out_specs.append(block(2 * rows))
        out_shape.append(jax.ShapeDtypeStruct((taps, kinds, width // 2, 2 * rows), jnp.bfloat16))
    return pl.pallas_call(
        functools.partial(gates_kernel, 0 if held is None else 1),
        grid_spec=pltpu.PrefetchScalarGridSpec(
            num_scalar_prefetch=1,
            grid=(taps,),
            in_specs=specs,
            out_specs=out_specs,
        ),
        out_shape=out_shape,
        input_output_aliases=aliases,
        compiler_params=pltpu.CompilerParams(vmem_limit_bytes=50 * 2**20),
        cost_estimate=HIDDEN_COST,
        name="gates_step",
    )(pick, *operands)


def gates_pool_kernel(skip, pick_ref, length_ref, low_ref, high_ref, w_ref, base_ref, small_ref,
                      grad_ref, *refs):
    hidden_ref, sums_ref, gg_ref, x_ref, *refs = refs[skip:]
    half_rows = low_ref.shape[0]

    @pl.when(pl.program_id(0) == 0)
    def _():
        at = pl.multiple_of(pick_ref[2] * half_rows, 64)
        x_ref[pl.ds(at, half_rows), :] = low_ref[...]
        at = pl.multiple_of((1 - pick_ref[2]) * half_rows, 64)
        x_ref[pl.ds(at, half_rows), :] = high_ref[...]

    gates_ref = refs[-3]
    for copy_ref in refs[:-3]:
        copy_ref[...] = w_ref[...]
    weights = w_ref[...].reshape(-1, w_ref.shape[3])
    product = jnp.dot(weights, x_ref[...], preferred_element_type=jnp.float32)
    gates_ref[...] = product.reshape(gates_ref.shape) + base_ref[...]
    pool_kernel(length_ref, gates_ref, small_ref, grad_ref, hidden_ref, sums_ref, gg_ref, refs[-2:])


def pool_shapes(width, span):
    return [
        jax.ShapeDtypeStruct((width, span), jnp.bfloat16),
        jax.ShapeDtypeStruct((width, LANES), jnp.float32),
        jax.ShapeDtypeStruct((2, 3, width, span), jnp.bfloat16),
    ]


def pool_scratch(part, span):
    return [
        pltpu.VMEM((2, 3, part, span), jnp.float32),
        pltpu.VMEM((3, part, span), jnp.float32),
        pltpu.VMEM((3, part, LANES), jnp.float32),
    ]


def gates_pool(pick, length, w_rows, own, sibling, base, small, grad, held, copy, window, before):
    taps, kinds, width, depth = w_rows.shape
    rows, span = own.shape
    width //= 2
    part = PART
    count = width // part
    lines = lambda columns: pl.BlockSpec((part, columns), lambda i, p: (i, 0))
    wide = pl.BlockSpec((taps, kinds, part, span), lambda i, p: (0, 0, i, 0))
    copy_specs, copy_shapes = [], []
    if copy:
        copy_specs = [pl.BlockSpec((taps, kinds, part, 2 * rows), lambda i, p: (0, 0, i, 0))]
        copy_shapes = [jax.ShapeDtypeStruct((taps, kinds, width, 2 * rows), jnp.bfloat16)]
    return pl.pallas_call(
        functools.partial(gates_pool_kernel, 1 + len(before)),
        grid_spec=pltpu.PrefetchScalarGridSpec(
            num_scalar_prefetch=1,
            grid=(count,),
            in_specs=[
                pl.BlockSpec(memory_space=pltpu.SMEM),
                once((rows, span)),
                once((rows, span)),
                pl.BlockSpec(
                    (taps, kinds, part, 2 * rows), lambda i, p: (0, 0, p[0] * count + i, p[1])
                ),
                wide,
                lines(LANES),
                lines(span),
            ]
            + [pl.BlockSpec(memory_space=pltpu.HBM)] * (1 + len(before)),
            out_specs=[
                lines(span),
                lines(LANES),
                pl.BlockSpec((taps, kinds, part, span), lambda i, p: (0, 0, i, window)),
                pl.BlockSpec((2 * rows, span), lambda i, p: (1, window)),
                *copy_specs,
            ],
            scratch_shapes=pool_scratch(part, span),
        ),
        out_shape=pool_shapes(width, span)[:2]
        + [
            jax.ShapeDtypeStruct((taps, kinds, width, 2 * span), jnp.bfloat16),
            jax.ShapeDtypeStruct((depth, 2 * span), jnp.bfloat16),
        ]
        + copy_shapes,
        input_output_aliases={8: 3, **({9: 2} if before else {})},
        compiler_params=pltpu.CompilerParams(vmem_limit_bytes=50 * 2**20),
        cost_estimate=HIDDEN_COST,
        name="gates_pool",
    )(pick, length, own, sibling, w_rows, base, small, grad, held, *before)


def whole_kernel(function, count, *refs):
    results = function(*[ref[...] for ref in refs[:count]])
    for ref, result in zip(refs[count:], results):
        ref[...] = result.astype(ref.dtype)


def whole(function, outputs, *operands):
    return pl.pallas_call(
        functools.partial(whole_kernel, function, len(operands)),
        out_shape=[jax.ShapeDtypeStruct(*output) for output in outputs],
        compiler_params=pltpu.CompilerParams(vmem_limit_bytes=20 * 2**20),
        cost_estimate=HIDDEN_COST,
        name="whole",
    )(*operands)


def back_kernel(pick_ref, w_ref, gg_ref, keep_ref, give_ref, total_ref):
    step = pl.program_id(0)
    columns = w_ref.shape[1]
    total_ref[pl.ds(pl.multiple_of(step * columns, columns), columns), :] = lax.dot_general(
        w_ref[...], gg_ref[...], (((0,), (0,)), ((), ())), preferred_element_type=jnp.float32
    )

    @pl.when(step == pl.num_programs(0) - 1)
    def _():
        rows = keep_ref.shape[0]
        keep_ref[...] = total_ref[pl.ds(pl.multiple_of(pick_ref[2] * rows, 64), rows), :]
        give_ref[...] = total_ref[
            pl.ds(pl.multiple_of((1 - pick_ref[2]) * rows, 64), rows), :
        ].astype(jnp.bfloat16)


def back_products(pick, weights, gg, window):
    depth, columns = weights.shape
    span = gg.shape[1] // 2
    part = 384
    return pl.pallas_call(
        back_kernel,
        grid_spec=pltpu.PrefetchScalarGridSpec(
            num_scalar_prefetch=1,
            grid=(columns // part,),
            in_specs=[
                pl.BlockSpec((depth, part), lambda i, p: (0, i)),
                pl.BlockSpec(
                    (depth, span), lambda i, p: (0, window), pipeline_mode=pl.Buffered(1)
                ),
            ],
            out_specs=[
                pl.BlockSpec((columns // 2, span), lambda i, p: (0, 0)),
                pl.BlockSpec((columns // 2, span), lambda i, p: (0, 0)),
            ],
            scratch_shapes=[pltpu.VMEM((columns, span), jnp.float32)],
        ),
        out_shape=[
            jax.ShapeDtypeStruct((columns // 2, span), jnp.float32),
            jax.ShapeDtypeStruct((columns // 2, span), jnp.bfloat16),
        ],
        compiler_params=pltpu.CompilerParams(vmem_limit_bytes=26 * 2**20),
        cost_estimate=HIDDEN_COST,
        name="back_products",
    )(pick, weights, gg)


def chunk_kernel(function, inputs, inner_ref, *refs):
    function(inner_ref[0] == 1, *refs[:inputs], *refs[inputs:])


def chunk_step(function, outputs, inner, size, *operands):
    specs, arrays = [pl.BlockSpec(memory_space=pltpu.SMEM)], [inner]
    for operand in operands:
        array, at = operand if isinstance(operand, tuple) else (operand, 0)
        specs.append(pl.BlockSpec((size, array.shape[1]), lambda i, at=at: (at, 0)))
        arrays.append(array)
    depth = arrays[1].shape[1]
    return pl.pallas_call(
        functools.partial(chunk_kernel, function, len(operands)),
        grid=(1,),
        in_specs=specs,
        out_specs=[pl.BlockSpec((size, depth), lambda i: (0, 0))] * outputs,
        out_shape=[jax.ShapeDtypeStruct((size, depth), jnp.bfloat16)] * outputs,
        compiler_params=pltpu.CompilerParams(vmem_limit_bytes=8 * 2**20),
        cost_estimate=HIDDEN_COST,
        name="chunk_step",
    )(*arrays)


def rounded_sum(left_ref, right_ref):
    total = left_ref[...].astype(jnp.float32) + right_ref[...].astype(jnp.float32)
    return total.astype(jnp.bfloat16)


def take_chunk(inner, chunk_ref, out_ref):
    out_ref[...] = chunk_ref[...]


def sum_chunk(inner, chunk_ref, got_ref, sum_ref):
    sum_ref[...] = rounded_sum(chunk_ref, got_ref)


def sum_and_final(inner, chunk_ref, got_ref, total_ref, sum_ref, final_ref):
    sum_ref[...] = rounded_sum(chunk_ref, got_ref)
    final_ref[...] = jnp.where(inner, total_ref[...], got_ref[...])


def total_and_next(inner, sum_ref, got_ref, chunk_ref, total_ref, next_ref):
    total = rounded_sum(sum_ref, got_ref)
    total_ref[...] = total
    next_ref[...] = jnp.where(inner, total, chunk_ref[...])


def final_chunk(inner, got_ref, total_ref, final_ref):
    final_ref[...] = jnp.where(inner, total_ref[...], got_ref[...])


def total_chunk(inner, sum_ref, got_ref, total_ref):
    total_ref[...] = rounded_sum(sum_ref, got_ref)


def even_odd(count):
    return [(i, i ^ 1) for i in range(count)]


def line_pairs(moves):
    return [(2 * a + s, 2 * b + s) for a, b in moves for s in range(2)]


class Order:
    def __init__(self, token):
        self.token = token

    def __call__(self, values):
        values, self.token = lax.optimization_barrier((values, self.token))
        return values


def line_sum(part, length):
    if length & (length - 1) == 0:
        step = 1
        while step < length:
            part = part + lax.ppermute(part, "dp", line_pairs([(i, i ^ step) for i in range(length)]))
            step *= 2
        return part
    total = part
    for _ in range(length - 1):
        part = lax.ppermute(part, "dp", line_pairs([(i, (i + 1) % length) for i in range(length)]))
        total = total + part
    return total


def half(array, axis, which):
    size = array.shape[axis] // 2
    return lax.dynamic_slice_in_dim(array, which * size, size, axis)


def join(low_first, mine, other, axis):
    return jnp.where(
        low_first,
        jnp.concatenate([mine, other], axis=axis),
        jnp.concatenate([other, mine], axis=axis),
    )


def write_kernel(count, flags_ref, *refs):
    out_ref = refs[-1]
    size = refs[0].shape[0]
    middle = refs[0].shape[1] // 2
    mine = flags_ref[0] == pl.program_id(0)
    straight = flags_ref[1] == 0
    for j in range(count):
        at = pl.ds(j * size, size)
        block = jnp.where(mine, refs[j][...], refs[count + j][...]).astype(jnp.float32)
        left, right = block[:, :middle], block[:, middle:]
        out_ref[at, :middle] = jnp.where(straight, left, right)
        out_ref[at, middle:] = jnp.where(straight, right, left)


def write_chunks(flags, mine, theirs, group, whole, shape):
    count = len(mine)
    size, depth = mine[0].shape
    specs = [pl.BlockSpec(memory_space=pltpu.SMEM)]
    specs += [pl.BlockSpec((size, depth), lambda i: (0, 0))] * (2 * count)
    operands = [flags, *mine, *theirs]
    aliases = {}
    if whole is not None:
        specs.append(pl.BlockSpec(memory_space=pl.ANY))
        operands.append(whole)
        aliases = {len(operands) - 1: 0}
    return pl.pallas_call(
        functools.partial(write_kernel, count),
        grid=(2,),
        in_specs=specs,
        out_specs=pl.BlockSpec((count * size, depth), lambda i: (2 * group + i, 0)),
        out_shape=jax.ShapeDtypeStruct(shape, jnp.float32),
        input_output_aliases=aliases,
        compiler_params=pltpu.CompilerParams(vmem_limit_bytes=16 * 2**20),
        cost_estimate=HIDDEN_COST,
        name="write_chunks",
    )(*operands)


def add_times(total, left, right):
    return total + times(left, right)


def add_rounded(left, right):
    return (left.astype(jnp.float32) + right.astype(jnp.float32)).astype(jnp.bfloat16)


def piped_sums(order, chunks, pairs, fillers, arrived):
    position = lax.axis_index("dp") // 2
    inner = (position == 1) | (position == 2)
    flag = inner.astype(jnp.int32).reshape(1)
    edge = line_pairs([(0, 1), (1, 0), (2, 3), (3, 2)])
    middle = line_pairs([(1, 2), (2, 1)])
    sums, totals, finals = {}, {}, {}
    got_edge, got_middle, got_pair = {}, {}, {}
    size = chunks.shape[0] // CHUNKS

    def run(function, outputs, *operands):
        arrays = order(tuple(o[0] if isinstance(o, tuple) else o for o in operands))
        operands = [
            (array, o[1]) if isinstance(o, tuple) else array for array, o in zip(arrays, operands)
        ]
        return order(chunk_step(function, outputs, flag, size, *operands))

    (payload,) = run(take_chunk, 1, (chunks, 0))
    got_edge[0] = lax.ppermute(payload, "dp", edge)
    for n in range(CHUNKS + LAG + 3):
        final = None
        k = n - 1
        if k in got_edge:
            got = got_edge.pop(k)
            if k < CHUNKS and k >= LAG:
                sums[k], final = run(sum_and_final, 2, (chunks, k), got, totals.pop(k - LAG))
            elif k < CHUNKS:
                (sums[k],) = run(sum_chunk, 1, (chunks, k), got)
            else:
                (final,) = run(final_chunk, 1, got, totals.pop(k - LAG))
            if k < CHUNKS:
                got_middle[k] = lax.ppermute(sums[k], "dp", middle)
        k = n - 2
        payload = None
        if k in got_middle:
            got = got_middle.pop(k)
            (totals[k],) = run(total_chunk, 1, sums.pop(k), got)
        k = n + 1 - LAG
        if k in totals and n + 1 < CHUNKS:
            (payload,) = run(final_chunk, 1, (chunks, n + 1), totals[k])
        elif n + 1 < CHUNKS:
            (payload,) = run(take_chunk, 1, (chunks, n + 1))
        elif k in totals:
            payload = totals[k]
        if payload is not None:
            got_edge[n + 1] = lax.ppermute(payload, "dp", edge)
        k = n - 1 - LAG
        if final is not None:
            finals[k] = final
            got_pair[k] = lax.ppermute(final, "dp", pairs)
        k = k - 1
        if k in got_pair:
            arrived(k, finals, order(got_pair.pop(k)))
        if n in fillers:
            fillers[n]()


def on_device(line, channel_parts, inputs, lengths, start_cell, weight, bias, out_grad, cell_grad):
    span, width = inputs.shape
    depth = weight.shape[1]
    own = width // 2
    rows = 6 * own
    side = lax.axis_index("dp") % 2
    other_side = 1 - side
    is_low = side == 0
    pairs = even_odd(2 * line)
    slots = slot_order(span)

    place = lax.axis_index("mp")
    core_low = place % 2 == 0
    near_low = place < 2
    core_pairs = even_odd(channel_parts)
    chip_pairs = [(i, i ^ 2) for i in range(4)]

    def split(array, axis):
        return half(array, axis, place // 2), half(array, axis, 1 - place // 2)

    small = small_columns(bias, start_cell, cell_grad)
    lane = lax.broadcasted_iota(jnp.int32, small.shape, 1)
    small = jnp.where(lane == 5, lengths[0].astype(jnp.float32), small)
    small_mine, small_other = half(small, 0, side), half(small, 0, other_side)
    w_rows = jnp.transpose(weight, (0, 2, 3, 1))

    def pooled(total, length, small_part, grad_part):
        hidden, sums, gg = pool(length, total.reshape(2, 3, own, span), small_part, grad_part)
        return hidden, sums, gg.reshape(rows, span)

    if line == 4 and channel_parts == 4:
        done = Order(out_grad)

        def run(function, *operands):
            return done(function(*done(operands)))

        pick_near = jnp.stack([side, place // 2, place % 2]).astype(jnp.int32)
        pick_far = jnp.stack([side, 1 - place // 2, place % 2]).astype(jnp.int32)
        x_own = run(lambda x: mix(x.T, slots), inputs)
        far_got = lax.ppermute(x_own, "mp", chip_pairs)
        pair_got = lax.ppermute(x_own, "dp", pairs)
        near_got = lax.ppermute(x_own, "mp", core_pairs)
        out_grad, done.token = done.token, small_mine
        grads = run(lambda g: mix(g.T, slots), out_grad)
        grads_mine, grads_other = done((half(grads, 0, side), half(grads, 0, other_side)))
        gates, held, w_near = run(
            lambda *given: gates_step(*given, True, 0, None), pick_near, w_rows, x_own, near_got
        )
        cut = width * 2 // 3
        far_own = done(far_got)
        far_got = lax.ppermute(far_own, "mp", core_pairs)
        x_pair = done(pair_got)
        relay = [
            lax.ppermute(x_pair[:cut], "mp", chip_pairs),
            lax.ppermute(jnp.concatenate([far_own[cut:], grads_other], axis=0), "dp", pairs),
        ]
        far_got = done(far_got)
        pair_near_got = lax.ppermute(done(x_pair), "mp", core_pairs)
        far_own, far_got, gates, grads_mine = done((far_own, far_got, gates, grads_mine))
        held = done(held)
        hidden_mine, sums_mine, gg, held, w_far = gates_pool(
            pick_far,
            lengths,
            w_rows,
            far_own,
            far_got,
            gates,
            done.token,
            grads_mine,
            held,
            True,
            0,
            (),
        )
        done.token = sums_mine
        gg, held = done((gg, held))
        pair_far_own, grads_pair = run(
            lambda a, b: (jnp.concatenate([a, b[: width - cut]], axis=0), b[width - cut :]), *relay
        )
        pair_far_got = lax.ppermute(pair_far_own, "mp", core_pairs)
        small_pair = lax.ppermute(done(small_other), "dp", pairs)
        kept = {}

        own_shape, wide_type, sent_type = (width, span), jnp.float32, jnp.bfloat16

        def add(left, right):
            return (left + right.astype(jnp.float32),)

        def add_both(left, right):
            total = left + right.astype(jnp.float32)
            return total, total

        def fill_back(window, part):
            keep, give = run(
                lambda *given: back_products(*given, window),
                pick_near,
                (w_near, w_far)[part].reshape(rows, depth // 2),
                gg.reshape(rows, 2 * span),
            )
            kept["keep", window, part] = keep
            kept["core", window, part] = lax.ppermute(give, "mp", core_pairs)

        def fill_core(window, part):
            kind = wide_type if part == 0 else sent_type
            (kept["sum", window, part],) = run(
                lambda *given: whole(add, [(own_shape, kind)], *given),
                kept["keep", window, part],
                kept["core", window, part],
            )

        def fill_cross(window):
            kept["cross", window] = lax.ppermute(done(kept["sum", window, 1]), "mp", chip_pairs)

        pair_gates, held = run(
            lambda *given: gates_step(*given[:4], False, 1, given[4]),
            pick_near,
            w_rows,
            x_pair,
            pair_near_got,
            held,
        )
        small_pair, grads_pair = done((small_pair, grads_pair))
        length_pair = small_pair[0, 5:6].astype(jnp.int32)
        small_pair = jnp.where(lane[:own] < 3, small_mine, small_pair)
        hidden_pair, sums_pair, gg, held = run(
            lambda *given: gates_pool(*given[:9], False, 1, given[9:]),
            pick_far,
            length_pair,
            w_rows,
            pair_far_own,
            pair_far_got,
            pair_gates,
            small_pair,
            grads_pair,
            held,
            gg,
        )

        size = rows // CHUNKS
        per = own // size

        def products():
            return run(
                lambda gg, x: cols_dot(gg.reshape(rows, 2 * span), x).astype(jnp.bfloat16), gg, held
            )

        def fill_send():
            (give,) = run(
                lambda *given: whole(add, [(own_shape, sent_type)], *given),
                kept["sum", 1, 0],
                kept["cross", 1],
            )
            kept["pair"] = lax.ppermute(give, "dp", pairs)

        def unmixed(total, slots):
            return (
                lax.dot_general(
                    total, slots, (((1,), (1,)), ((), ())), preferred_element_type=jnp.float32
                ),
            )

        def send(name, value):
            kept[name] = lax.ppermute(done(value), "dp", pairs)

        def receive(name):
            kept[name] = done(kept[name])

        def fill_input():
            def total(near_sum, cross, pair, slots):
                total = near_sum + cross.astype(jnp.float32) + pair.astype(jnp.float32)
                return unmixed(total.astype(jnp.bfloat16), slots)

            (total,) = run(
                lambda *given: whole(total, [(own_shape, sent_type)], *given),
                kept["sum", 0, 0],
                kept["cross", 0],
                kept["pair"],
                slots,
            )
            kept["input"] = total.T

        def fill_hidden():
            low, high = done((hidden_mine, kept["hidden"]))
            low, high = jnp.where(is_low, low, high), jnp.where(is_low, high, low)

            def both(low, high, slots):
                return unmixed(jnp.concatenate([low, high], axis=0), slots)

            (total,) = run(
                lambda *given: whole(both, [(own_shape, sent_type)], *given), low, high, slots
            )
            kept["hidden out"] = total.T

        position = lax.axis_index("dp") // 2
        inner = (position == 1) | (position == 2)

        def fill_bias(stage):
            def run_stage():
                if stage == 0:
                    kept["bias"] = run(jnp.add, sums_mine, sums_pair)
                    moves = [(0, 1), (1, 0), (2, 3), (3, 2)]
                elif stage == 1:
                    kept["bias"] = run(jnp.add, kept["bias"], kept["bias got"])
                    moves = [(1, 2), (2, 1)]
                elif stage == 2:
                    kept["bias"] = run(jnp.add, kept["bias"], kept["bias got"])
                    moves = [(1, 0), (2, 3), (0, 1), (3, 2)]
                elif stage == 3:
                    kept["bias"] = run(
                        lambda a, b: jnp.where(inner, a, b), kept["bias"], kept["bias got"]
                    )
                if stage < 3:
                    kept["bias got"] = lax.ppermute(kept["bias"], "dp", line_pairs(moves))
                elif stage == 3:
                    kept["bias got"] = lax.ppermute(kept["bias"], "dp", pairs)
                else:
                    kept["bias got"] = done(kept["bias got"])

            return run_stage

        flags = jnp.stack([side, place // 2]).astype(jnp.int32)
        kept["out"] = None

        swapped = {}

        def arrived(k, finals, got):
            swapped[k] = got
            group = k // per
            members = range(group * per, (group + 1) * per)
            if k == members[-1]:
                parts = done(([finals[m] for m in members], [swapped[m] for m in members]))
                kept["out"] = done(write_chunks(flags, *parts, group, kept["out"], (2 * rows, depth)))

        def fill(*steps):
            def run_all():
                for step, *given in steps:
                    step(*given)

            return run_all

        fill_bias(0)()
        fill_bias(0)()
        fill_bias(0)()
        fill_bias(0)()
        send("hidden", hidden_pair)
        fill_back(1, 1)
        fill_back(1, 0)
        fill_core(1, 1)
        fill_cross(1)
        fill_bias(1)()
        fill_back(0, 1)
        fill_core(1, 0)
        fill_back(0, 0)
        fill_bias(2)()
        fill_core(0, 1)
        chunks = products()
        fill_core(0, 0)
        receive("hidden")
        fill_bias(3)()
        fillers = {
            0: fill((receive, ("cross", 1)), (fill_cross, 0), (fill_bias(4),)),
            1: fill((fill_send,)),
            3: fill((receive, ("cross", 0))),
            4: fill((receive, "pair")),
            CHUNKS: fill((send, "sums", sums_pair)),
            CHUNKS + 2: fill((fill_hidden,)),
            CHUNKS + 3: fill((fill_input,)),
            CHUNKS + 4: fill((receive, "sums")),
        }
        piped_sums(done, chunks, pairs, fillers, arrived)
        input_grad, hidden = kept["input"], kept["hidden out"]
        wgrad = kept["out"].reshape(2, 3, width, depth)
        bias_grad = join(is_low, kept["bias"], kept["bias got"], 0)[:, 2:5].T
        sums_mine, sums_other = done.token, kept["sums"]
    else:
        x_own = mix(inputs.T, slots)
        grads = mix(out_grad.T, slots)
        grads_mine, grads_other = half(grads, 0, side), half(grads, 0, other_side)
        grads_pair = lax.ppermute(grads_other, "dp", pairs)
        small_pair = lax.ppermute(small_other, "dp", pairs)
        length_pair = small_pair[0, 5:6].astype(jnp.int32)
        small_pair = jnp.where(lane[:own] < 3, small_mine, small_pair)
        x_all = lax.all_gather(x_own, "mp", axis=0, tiled=True)
        x_pair = lax.all_gather(lax.ppermute(x_own, "dp", pairs), "mp", axis=0, tiled=True)
        w_mine = half(w_rows, 2, side).reshape(rows, depth)
        w_other = half(w_rows, 2, other_side).reshape(rows, depth)
        hidden_mine, sums_mine, gg_mine = pooled(
            times(w_mine, x_all), lengths, small_mine, grads_mine
        )
        _, sums_pair, gg_pair = pooled(times(w_mine, x_pair), length_pair, small_pair, grads_pair)
        hidden_other, sums_other, gg_other = pooled(
            times(w_other, x_all), lengths, small_other, grads_other
        )
        part = cols_dot(gg_mine, x_all) + cols_dot(gg_pair, x_pair)
        total = line_sum(part.astype(jnp.bfloat16), line)
        theirs = lax.ppermute(total, "dp", pairs)
        shape = (2, 3, own, depth)
        wgrad = join(is_low, total.reshape(shape), theirs.reshape(shape), 2).astype(jnp.float32)
        back = rows_dot(w_mine, gg_mine) + rows_dot(w_other, gg_other)
        input_grad = lax.psum_scatter(
            back.astype(jnp.bfloat16), "mp", scatter_dimension=0, tiled=True
        )
        input_grad = mix(input_grad, slots, back=True).T
        hidden = mix(join(is_low, hidden_mine, hidden_other, 0), slots, back=True).T
        bias_mine = line_sum(sums_mine + sums_pair, line)
        bias_pair = lax.ppermute(bias_mine, "dp", pairs)
        bias_grad = join(is_low, bias_mine, bias_pair, 0)[:, 2:5].T

    sums = join(is_low, sums_mine, sums_other, 0)
    return (
        hidden,
        sums[:, 0:1].T,
        input_grad,
        sums[:, 1:2].T,
        jnp.transpose(wgrad, (0, 3, 1, 2)),
        bias_grad,
    )


def solution(mesh):
    in_specs = (
        P("dp", "mp"),
        P("dp"),
        P("dp", "mp"),
        P(None, None, None, "mp"),
        P(None, "mp"),
        P("dp", "mp"),
        P("dp", "mp"),
    )
    out_specs = (
        P("dp", "mp"),
        P("dp", "mp"),
        P("dp", "mp"),
        P("dp", "mp"),
        P(None, None, None, "mp"),
        P(None, "mp"),
    )
    body = functools.partial(on_device, mesh.shape["dp"] // 2, mesh.shape["mp"])
    return jax.shard_map(
        body, mesh=mesh, in_specs=in_specs, out_specs=out_specs, check_vma=False
    )
```

```python
import functools

import jax
import jax.numpy as jnp
from jax import lax
from jax.experimental import pallas as pl
from jax.experimental.pallas import tpu as pltpu
from jax.sharding import PartitionSpec as P

LANES = 128
ROWS = 16
CHUNKS = 18
PART = 144
LAG = 4
HIDDEN_COST = pl.CostEstimate(flops=1, bytes_accessed=1, transcendentals=0)


def pool_kernel(length_ref, gates_ref, small_ref, grad_ref, hidden_ref, sums_ref, gg_ref, held):
    part, span = grad_ref.shape
    tiles = span // LANES
    length = length_ref[0]
    lane = lax.broadcasted_iota(jnp.int32, (ROWS, LANES), 1)
    zero = jnp.zeros((ROWS, LANES), jnp.float32)
    one = zero + 1.0
    first_lane = lane == 0
    last_lane = lane == LANES - 1
    cand_at, forget_at, out_at = 0, 1, 2
    run_at, back_at, decay_at = 0, 1, 2
    held_gates, held_runs = held

    def tile_of(j):
        return pl.ds(j * LANES, LANES)

    def is_live(j):
        return lane * tiles + j < length

    def local(step, unused):
        rows = pl.ds(pl.multiple_of(step * ROWS, ROWS), ROWS)
        small = small_ref[rows, :]
        bias = [jnp.broadcast_to(small[:, k : k + 1], (ROWS, LANES)) for k in range(3)]
        end_grad = jnp.where(last_lane, jnp.broadcast_to(small[:, 4:5], (ROWS, LANES)), 0.0)
        earlier = [
            jnp.where(first_lane, 0.0, pltpu.roll(gates_ref[1, k, rows, tile_of(tiles - 1)], 1, 1))
            for k in range(3)
        ]
        run, product, back = zero, one, zero
        for j in range(tiles):
            gates = []
            for k in range(3):
                gates.append(gates_ref[0, k, rows, tile_of(j)] + earlier[k] + bias[k])
                earlier[k] = gates_ref[1, k, rows, tile_of(j)]
            live = is_live(j)
            cand = jnp.tanh(gates[0])
            forget = jax.nn.sigmoid(gates[1])
            out_gate = jnp.where(live, 0.5 * jnp.tanh(0.5 * gates[2]) + 0.5, 0.0)
            kept = jnp.where(live, 1.0 - forget, 0.0)
            decay = 1.0 - kept
            emitted = out_gate * grad_ref[rows, tile_of(j)].astype(jnp.float32)
            if j == tiles - 1:
                emitted = emitted + end_grad
            run = decay * run + kept * cand
            product = product * decay
            back = back + product * emitted
            held_gates[cand_at, rows, tile_of(j)] = cand
            held_gates[forget_at, rows, tile_of(j)] = forget
            held_gates[out_at, rows, tile_of(j)] = out_gate
        held_runs[run_at, rows, :] = run
        held_runs[back_at, rows, :] = back
        held_runs[decay_at, rows, :] = product
        return unused

    lax.fori_loop(0, part // ROWS, local, 0)

    wide = lax.broadcasted_iota(jnp.int32, (part, LANES), 1)
    begin = jnp.broadcast_to(small_ref[:, 3:4], (part, LANES))
    run, back, product = held_runs[run_at], held_runs[back_at], held_runs[decay_at]
    run = jnp.where(wide == 0, run + product * begin, run)
    up = product
    for k in (1, 2, 4, 8, 16, 32, 64):
        inside = wide >= k
        run = run + up * jnp.where(inside, pltpu.roll(run, k, 1), 0.0)
        up = up * jnp.where(inside, pltpu.roll(up, k, 1), 1.0)
        inside = wide < LANES - k
        back = back + product * jnp.where(inside, pltpu.roll(back, LANES - k, 1), 0.0)
        product = product * jnp.where(inside, pltpu.roll(product, LANES - k, 1), 1.0)
    held_runs[run_at] = jnp.where(wide == 0, begin, pltpu.roll(run, 1, 1))
    held_runs[decay_at] = jnp.where(wide == LANES - 1, 0.0, pltpu.roll(back, LANES - 1, 1))
    last_cell = jnp.broadcast_to(run[:, LANES - 1 :], (part, LANES))
    sums_ref[...] = jnp.where(wide == 0, last_cell, 0.0) + jnp.where(
        wide == 1, jnp.broadcast_to(back[:, :1], (part, LANES)), 0.0
    )

    def final(step, unused):
        rows = pl.ds(pl.multiple_of(step * ROWS, ROWS), ROWS)
        small = small_ref[rows, :]
        end_grad = jnp.where(last_lane, jnp.broadcast_to(small[:, 4:5], (ROWS, LANES)), 0.0)
        before = held_runs[run_at, rows, :]
        cells, befores = [], []
        for j in range(tiles):
            cand = held_gates[cand_at, rows, tile_of(j)]
            kept = jnp.where(is_live(j), 1.0 - held_gates[forget_at, rows, tile_of(j)], 0.0)
            cell = (1.0 - kept) * before + kept * cand
            befores.append(before)
            cells.append(cell)
            before = cell
        follow = held_runs[decay_at, rows, :]
        bias_sum = [zero] * 3
        for j in range(tiles - 1, -1, -1):
            cand = held_gates[cand_at, rows, tile_of(j)]
            forget = held_gates[forget_at, rows, tile_of(j)]
            out_gate = held_gates[out_at, rows, tile_of(j)]
            kept = jnp.where(is_live(j), 1.0 - forget, 0.0)
            emitted = out_gate * grad_ref[rows, tile_of(j)].astype(jnp.float32)
            hidden_ref[rows, tile_of(j)] = (out_gate * cells[j]).astype(jnp.bfloat16)
            out_part = emitted * cells[j] * (1.0 - out_gate)
            if j == tiles - 1:
                emitted = emitted + end_grad
            cell_grad = emitted + follow
            follow = (1.0 - kept) * cell_grad
            shared = cell_grad * kept
            parts = [
                shared * (1.0 - cand * cand),
                shared * (befores[j] - cand) * forget,
                out_part,
            ]
            for k in range(3):
                rounded = parts[k].astype(jnp.bfloat16)
                gg_ref[0, k, rows, tile_of(j)] = rounded
                wide_part = rounded.astype(jnp.float32)
                bias_sum[k] = bias_sum[k] + wide_part
                if j > 0:
                    gg_ref[1, k, rows, tile_of(j - 1)] = rounded
                else:
                    moved = jnp.where(last_lane, 0.0, pltpu.roll(wide_part, LANES - 1, 1))
                    gg_ref[1, k, rows, tile_of(tiles - 1)] = moved.astype(jnp.bfloat16)
        answer = sums_ref[rows, :]
        for k in range(3):
            total = jnp.sum(bias_sum[k], axis=1, keepdims=True)
            answer = jnp.where(lane == 2 + k, jnp.broadcast_to(total, (ROWS, LANES)), answer)
        sums_ref[rows, :] = answer
        return unused

    lax.fori_loop(0, part // ROWS, final, 0)


def pool(length, gates, small, grad):
    taps, kinds, width, span = gates.shape
    part = next(p for p in (96, 48, 16) if width % p == 0)
    return pl.pallas_call(
        lambda *refs: pool_kernel(*refs[:-2], refs[-2:]),
        grid=(width // part,),
        in_specs=[
            pl.BlockSpec(memory_space=pltpu.SMEM),
            pl.BlockSpec((2, 3, part, span), lambda i: (0, 0, i, 0)),
            pl.BlockSpec((part, LANES), lambda i: (i, 0)),
            pl.BlockSpec((part, span), lambda i: (i, 0)),
        ],
        out_specs=[
            pl.BlockSpec((part, span), lambda i: (i, 0)),
            pl.BlockSpec((part, LANES), lambda i: (i, 0)),
            pl.BlockSpec((2, 3, part, span), lambda i: (0, 0, i, 0)),
        ],
        out_shape=[
            jax.ShapeDtypeStruct((width, span), jnp.bfloat16),
            jax.ShapeDtypeStruct((width, LANES), jnp.float32),
            jax.ShapeDtypeStruct((2, 3, width, span), jnp.bfloat16),
        ],
        scratch_shapes=[
            pltpu.VMEM((3, part, span), jnp.float32),
            pltpu.VMEM((3, part, LANES), jnp.float32),
        ],
        compiler_params=pltpu.CompilerParams(vmem_limit_bytes=40 * 2**20),
        cost_estimate=HIDDEN_COST,
        name="pool",
    )(length, gates, small, grad)


def small_columns(bias, start_cell, cell_grad):
    stacked = jnp.concatenate([bias.astype(jnp.float32), start_cell, cell_grad], axis=0)
    return jnp.pad(stacked.T, ((0, 0), (0, LANES - 5)))


def slot_order(span):
    tiles = span // LANES
    slot = lax.broadcasted_iota(jnp.int32, (span, span), 0)
    place = lax.broadcasted_iota(jnp.int32, (span, span), 1)
    return (place == (slot % tiles) * LANES + slot // tiles).astype(jnp.bfloat16)


def mix(block, order, back=False):
    dims = (((1,), (1 if back else 0,)), ((), ()))
    return lax.dot_general(block, order, dims, preferred_element_type=jnp.float32).astype(jnp.bfloat16)


def times(left, right):
    return jnp.dot(left, right, preferred_element_type=jnp.float32)


def rows_dot(left, right):
    return lax.dot_general(left, right, (((0,), (0,)), ((), ())), preferred_element_type=jnp.float32)


def cols_dot(left, right):
    return lax.dot_general(left, right, (((1,), (1,)), ((), ())), preferred_element_type=jnp.float32)


def once(shape):
    zeros = (0,) * len(shape)
    return pl.BlockSpec(shape, lambda *at: zeros, pipeline_mode=pl.Buffered(1))


def gates_kernel(skip, pick_ref, low_ref, high_ref, w_ref, *refs):
    out_ref, x_ref, *copy_refs = refs[skip:]
    half_rows = low_ref.shape[0]

    @pl.when(pl.program_id(0) == 0)
    def _():
        at = pl.multiple_of(pick_ref[2] * half_rows, 64)
        x_ref[pl.ds(at, half_rows), :] = low_ref[...]
        at = pl.multiple_of((1 - pick_ref[2]) * half_rows, 64)
        x_ref[pl.ds(at, half_rows), :] = high_ref[...]

    kinds, width = w_ref.shape[1:3]
    weights = w_ref[0].reshape(kinds * width, w_ref.shape[3])
    total = jnp.dot(weights, x_ref[...], preferred_element_type=jnp.float32)
    out_ref[...] = total.reshape(out_ref.shape)
    for copy_ref in copy_refs:
        copy_ref[...] = w_ref[...]


def gates_step(pick, w_rows, own, sibling, copy, window, held):
    taps, kinds, width, depth = w_rows.shape
    rows, span = own.shape
    block = lambda last: pl.BlockSpec((1, kinds, width // 2, last), lambda g, p: (g, 0, 0, 0))
    specs = [
        once((rows, span)),
        once((rows, span)),
        pl.BlockSpec((1, kinds, width // 2, 2 * rows), lambda g, p: (g, 0, p[0], p[1])),
    ]
    operands = [own, sibling, w_rows]
    aliases = {}
    if held is not None:
        specs.append(pl.BlockSpec(memory_space=pltpu.HBM))
        operands.append(held)
        aliases = {len(operands): 1}
    out_specs = [block(span), pl.BlockSpec((2 * rows, span), lambda g, p: (0, window))]
    out_shape = [
        jax.ShapeDtypeStruct((taps, kinds, width // 2, span), jnp.float32),
        jax.ShapeDtypeStruct((depth, 2 * span), jnp.bfloat16),
    ]
    if copy:
        out_specs.append(block(2 * rows))
        out_shape.append(jax.ShapeDtypeStruct((taps, kinds, width // 2, 2 * rows), jnp.bfloat16))
    return pl.pallas_call(
        functools.partial(gates_kernel, 0 if held is None else 1),
        grid_spec=pltpu.PrefetchScalarGridSpec(
            num_scalar_prefetch=1,
            grid=(taps,),
            in_specs=specs,
            out_specs=out_specs,
        ),
        out_shape=out_shape,
        input_output_aliases=aliases,
        compiler_params=pltpu.CompilerParams(vmem_limit_bytes=50 * 2**20),
        cost_estimate=HIDDEN_COST,
        name="gates_step",
    )(pick, *operands)


def gates_pool_kernel(skip, pick_ref, length_ref, low_ref, high_ref, w_ref, base_ref, small_ref,
                      grad_ref, *refs):
    hidden_ref, sums_ref, gg_ref, x_ref, *refs = refs[skip:]
    half_rows = low_ref.shape[0]

    @pl.when(pl.program_id(0) == 0)
    def _():
        at = pl.multiple_of(pick_ref[2] * half_rows, 64)
        x_ref[pl.ds(at, half_rows), :] = low_ref[...]
        at = pl.multiple_of((1 - pick_ref[2]) * half_rows, 64)
        x_ref[pl.ds(at, half_rows), :] = high_ref[...]

    gates_ref = refs[-3]
    for copy_ref in refs[:-3]:
        copy_ref[...] = w_ref[...]
    weights = w_ref[...].reshape(-1, w_ref.shape[3])
    product = jnp.dot(weights, x_ref[...], preferred_element_type=jnp.float32)
    gates_ref[...] = product.reshape(gates_ref.shape) + base_ref[...]
    pool_kernel(length_ref, gates_ref, small_ref, grad_ref, hidden_ref, sums_ref, gg_ref, refs[-2:])


def pool_shapes(width, span):
    return [
        jax.ShapeDtypeStruct((width, span), jnp.bfloat16),
        jax.ShapeDtypeStruct((width, LANES), jnp.float32),
        jax.ShapeDtypeStruct((2, 3, width, span), jnp.bfloat16),
    ]


def pool_scratch(part, span):
    return [
        pltpu.VMEM((2, 3, part, span), jnp.float32),
        pltpu.VMEM((3, part, span), jnp.float32),
        pltpu.VMEM((3, part, LANES), jnp.float32),
    ]


def gates_pool(pick, length, w_rows, own, sibling, base, small, grad, held, copy, window, before):
    taps, kinds, width, depth = w_rows.shape
    rows, span = own.shape
    width //= 2
    part = PART
    count = width // part
    lines = lambda columns: pl.BlockSpec((part, columns), lambda i, p: (i, 0))
    wide = pl.BlockSpec((taps, kinds, part, span), lambda i, p: (0, 0, i, 0))
    copy_specs, copy_shapes = [], []
    if copy:
        copy_specs = [pl.BlockSpec((taps, kinds, part, 2 * rows), lambda i, p: (0, 0, i, 0))]
        copy_shapes = [jax.ShapeDtypeStruct((taps, kinds, width, 2 * rows), jnp.bfloat16)]
    return pl.pallas_call(
        functools.partial(gates_pool_kernel, 1 + len(before)),
        grid_spec=pltpu.PrefetchScalarGridSpec(
            num_scalar_prefetch=1,
            grid=(count,),
            in_specs=[
                pl.BlockSpec(memory_space=pltpu.SMEM),
                once((rows, span)),
                once((rows, span)),
                pl.BlockSpec(
                    (taps, kinds, part, 2 * rows), lambda i, p: (0, 0, p[0] * count + i, p[1])
                ),
                wide,
                lines(LANES),
                lines(span),
            ]
            + [pl.BlockSpec(memory_space=pltpu.HBM)] * (1 + len(before)),
            out_specs=[
                lines(span),
                lines(LANES),
                pl.BlockSpec((taps, kinds, part, span), lambda i, p: (0, 0, i, window)),
                pl.BlockSpec((2 * rows, span), lambda i, p: (1, window)),
                *copy_specs,
            ],
            scratch_shapes=pool_scratch(part, span),
        ),
        out_shape=pool_shapes(width, span)[:2]
        + [
            jax.ShapeDtypeStruct((taps, kinds, width, 2 * span), jnp.bfloat16),
            jax.ShapeDtypeStruct((depth, 2 * span), jnp.bfloat16),
        ]
        + copy_shapes,
        input_output_aliases={8: 3, **({9: 2} if before else {})},
        compiler_params=pltpu.CompilerParams(vmem_limit_bytes=50 * 2**20),
        cost_estimate=HIDDEN_COST,
        name="gates_pool",
    )(pick, length, own, sibling, w_rows, base, small, grad, held, *before)


def whole_kernel(function, count, *refs):
    results = function(*[ref[...] for ref in refs[:count]])
    for ref, result in zip(refs[count:], results):
        ref[...] = result.astype(ref.dtype)


def whole(function, outputs, *operands):
    return pl.pallas_call(
        functools.partial(whole_kernel, function, len(operands)),
        out_shape=[jax.ShapeDtypeStruct(*output) for output in outputs],
        compiler_params=pltpu.CompilerParams(vmem_limit_bytes=20 * 2**20),
        cost_estimate=HIDDEN_COST,
        name="whole",
    )(*operands)


def back_kernel(pick_ref, w_ref, gg_ref, keep_ref, give_ref, total_ref):
    step = pl.program_id(0)
    columns = w_ref.shape[1]
    total_ref[pl.ds(pl.multiple_of(step * columns, columns), columns), :] = lax.dot_general(
        w_ref[...], gg_ref[...], (((0,), (0,)), ((), ())), preferred_element_type=jnp.float32
    )

    @pl.when(step == pl.num_programs(0) - 1)
    def _():
        rows = keep_ref.shape[0]
        keep_ref[...] = total_ref[pl.ds(pl.multiple_of(pick_ref[2] * rows, 64), rows), :]
        give_ref[...] = total_ref[
            pl.ds(pl.multiple_of((1 - pick_ref[2]) * rows, 64), rows), :
        ].astype(jnp.bfloat16)


def back_products(pick, weights, gg, window):
    depth, columns = weights.shape
    span = gg.shape[1] // 2
    part = 384
    return pl.pallas_call(
        back_kernel,
        grid_spec=pltpu.PrefetchScalarGridSpec(
            num_scalar_prefetch=1,
            grid=(columns // part,),
            in_specs=[
                pl.BlockSpec((depth, part), lambda i, p: (0, i)),
                pl.BlockSpec(
                    (depth, span), lambda i, p: (0, window), pipeline_mode=pl.Buffered(1)
                ),
            ],
            out_specs=[
                pl.BlockSpec((columns // 2, span), lambda i, p: (0, 0)),
                pl.BlockSpec((columns // 2, span), lambda i, p: (0, 0)),
            ],
            scratch_shapes=[pltpu.VMEM((columns, span), jnp.float32)],
        ),
        out_shape=[
            jax.ShapeDtypeStruct((columns // 2, span), jnp.float32),
            jax.ShapeDtypeStruct((columns // 2, span), jnp.bfloat16),
        ],
        compiler_params=pltpu.CompilerParams(vmem_limit_bytes=26 * 2**20),
        cost_estimate=HIDDEN_COST,
        name="back_products",
    )(pick, weights, gg)


def chunk_kernel(function, inputs, inner_ref, *refs):
    function(inner_ref[0] == 1, *refs[:inputs], *refs[inputs:])


def chunk_step(function, outputs, inner, size, *operands):
    specs, arrays = [pl.BlockSpec(memory_space=pltpu.SMEM)], [inner]
    for operand in operands:
        array, at = operand if isinstance(operand, tuple) else (operand, 0)
        specs.append(pl.BlockSpec((size, array.shape[1]), lambda i, at=at: (at, 0)))
        arrays.append(array)
    depth = arrays[1].shape[1]
    return pl.pallas_call(
        functools.partial(chunk_kernel, function, len(operands)),
        grid=(1,),
        in_specs=specs,
        out_specs=[pl.BlockSpec((size, depth), lambda i: (0, 0))] * outputs,
        out_shape=[jax.ShapeDtypeStruct((size, depth), jnp.bfloat16)] * outputs,
        compiler_params=pltpu.CompilerParams(vmem_limit_bytes=8 * 2**20),
        cost_estimate=HIDDEN_COST,
        name="chunk_step",
    )(*arrays)


def rounded_sum(left_ref, right_ref):
    total = left_ref[...].astype(jnp.float32) + right_ref[...].astype(jnp.float32)
    return total.astype(jnp.bfloat16)


def take_chunk(inner, chunk_ref, out_ref):
    out_ref[...] = chunk_ref[...]


def sum_chunk(inner, chunk_ref, got_ref, sum_ref):
    sum_ref[...] = rounded_sum(chunk_ref, got_ref)


def sum_and_final(inner, chunk_ref, got_ref, total_ref, sum_ref, final_ref):
    sum_ref[...] = rounded_sum(chunk_ref, got_ref)
    final_ref[...] = jnp.where(inner, total_ref[...], got_ref[...])


def total_and_next(inner, sum_ref, got_ref, chunk_ref, total_ref, next_ref):
    total = rounded_sum(sum_ref, got_ref)
    total_ref[...] = total
    next_ref[...] = jnp.where(inner, total, chunk_ref[...])


def final_chunk(inner, got_ref, total_ref, final_ref):
    final_ref[...] = jnp.where(inner, total_ref[...], got_ref[...])


def total_chunk(inner, sum_ref, got_ref, total_ref):
    total_ref[...] = rounded_sum(sum_ref, got_ref)


def even_odd(count):
    return [(i, i ^ 1) for i in range(count)]


def line_pairs(moves):
    return [(2 * a + s, 2 * b + s) for a, b in moves for s in range(2)]


class Order:
    def __init__(self, token):
        self.token = token

    def __call__(self, values):
        values, self.token = lax.optimization_barrier((values, self.token))
        return values


def line_sum(part, length):
    if length & (length - 1) == 0:
        step = 1
        while step < length:
            part = part + lax.ppermute(part, "dp", line_pairs([(i, i ^ step) for i in range(length)]))
            step *= 2
        return part
    total = part
    for _ in range(length - 1):
        part = lax.ppermute(part, "dp", line_pairs([(i, (i + 1) % length) for i in range(length)]))
        total = total + part
    return total


def half(array, axis, which):
    size = array.shape[axis] // 2
    return lax.dynamic_slice_in_dim(array, which * size, size, axis)


def join(low_first, mine, other, axis):
    return jnp.where(
        low_first,
        jnp.concatenate([mine, other], axis=axis),
        jnp.concatenate([other, mine], axis=axis),
    )


def write_kernel(count, flags_ref, *refs):
    out_ref = refs[-1]
    size = refs[0].shape[0]
    middle = refs[0].shape[1] // 2
    mine = flags_ref[0] == pl.program_id(0)
    straight = flags_ref[1] == 0
    for j in range(count):
        at = pl.ds(j * size, size)
        block = jnp.where(mine, refs[j][...], refs[count + j][...]).astype(jnp.float32)
        left, right = block[:, :middle], block[:, middle:]
        out_ref[at, :middle] = jnp.where(straight, left, right)
        out_ref[at, middle:] = jnp.where(straight, right, left)


def write_chunks(flags, mine, theirs, group, whole, shape):
    count = len(mine)
    size, depth = mine[0].shape
    specs = [pl.BlockSpec(memory_space=pltpu.SMEM)]
    specs += [pl.BlockSpec((size, depth), lambda i: (0, 0))] * (2 * count)
    operands = [flags, *mine, *theirs]
    aliases = {}
    if whole is not None:
        specs.append(pl.BlockSpec(memory_space=pl.ANY))
        operands.append(whole)
        aliases = {len(operands) - 1: 0}
    return pl.pallas_call(
        functools.partial(write_kernel, count),
        grid=(2,),
        in_specs=specs,
        out_specs=pl.BlockSpec((count * size, depth), lambda i: (2 * group + i, 0)),
        out_shape=jax.ShapeDtypeStruct(shape, jnp.float32),
        input_output_aliases=aliases,
        compiler_params=pltpu.CompilerParams(vmem_limit_bytes=16 * 2**20),
        cost_estimate=HIDDEN_COST,
        name="write_chunks",
    )(*operands)


def add_times(total, left, right):
    return total + times(left, right)


def add_rounded(left, right):
    return (left.astype(jnp.float32) + right.astype(jnp.float32)).astype(jnp.bfloat16)


def piped_sums(order, chunks, pairs, fillers, arrived):
    position = lax.axis_index("dp") // 2
    inner = (position == 1) | (position == 2)
    flag = inner.astype(jnp.int32).reshape(1)
    edge = line_pairs([(0, 1), (1, 0), (2, 3), (3, 2)])
    middle = line_pairs([(1, 2), (2, 1)])
    sums, totals, finals = {}, {}, {}
    got_edge, got_middle, got_pair = {}, {}, {}
    size = chunks.shape[0] // CHUNKS

    def run(function, outputs, *operands):
        arrays = order(tuple(o[0] if isinstance(o, tuple) else o for o in operands))
        operands = [
            (array, o[1]) if isinstance(o, tuple) else array for array, o in zip(arrays, operands)
        ]
        return order(chunk_step(function, outputs, flag, size, *operands))

    (payload,) = run(take_chunk, 1, (chunks, 0))
    got_edge[0] = lax.ppermute(payload, "dp", edge)
    for n in range(CHUNKS + LAG + 3):
        final = None
        k = n - 1
        if k in got_edge:
            got = got_edge.pop(k)
            if k < CHUNKS and k >= LAG:
                sums[k], final = run(sum_and_final, 2, (chunks, k), got, totals.pop(k - LAG))
            elif k < CHUNKS:
                (sums[k],) = run(sum_chunk, 1, (chunks, k), got)
            else:
                (final,) = run(final_chunk, 1, got, totals.pop(k - LAG))
            if k < CHUNKS:
                got_middle[k] = lax.ppermute(sums[k], "dp", middle)
        k = n - 2
        payload = None
        if k in got_middle:
            got = got_middle.pop(k)
            (totals[k],) = run(total_chunk, 1, sums.pop(k), got)
        k = n + 1 - LAG
        if k in totals and n + 1 < CHUNKS:
            (payload,) = run(final_chunk, 1, (chunks, n + 1), totals[k])
        elif n + 1 < CHUNKS:
            (payload,) = run(take_chunk, 1, (chunks, n + 1))
        elif k in totals:
            payload = totals[k]
        if payload is not None:
            got_edge[n + 1] = lax.ppermute(payload, "dp", edge)
        k = n - 1 - LAG
        if final is not None:
            finals[k] = final
            got_pair[k] = lax.ppermute(final, "dp", pairs)
        k = k - 1
        if k in got_pair:
            arrived(k, finals, order(got_pair.pop(k)))
        if n in fillers:
            fillers[n]()


def on_device(line, channel_parts, inputs, lengths, start_cell, weight, bias, out_grad, cell_grad):
    span, width = inputs.shape
    depth = weight.shape[1]
    own = width // 2
    rows = 6 * own
    side = lax.axis_index("dp") % 2
    other_side = 1 - side
    is_low = side == 0
    pairs = even_odd(2 * line)
    slots = slot_order(span)

    place = lax.axis_index("mp")
    core_low = place % 2 == 0
    near_low = place < 2
    core_pairs = even_odd(channel_parts)
    chip_pairs = [(i, i ^ 2) for i in range(4)]

    def split(array, axis):
        return half(array, axis, place // 2), half(array, axis, 1 - place // 2)

    small = small_columns(bias, start_cell, cell_grad)
    lane = lax.broadcasted_iota(jnp.int32, small.shape, 1)
    small = jnp.where(lane == 5, lengths[0].astype(jnp.float32), small)
    small_mine, small_other = half(small, 0, side), half(small, 0, other_side)
    w_rows = jnp.transpose(weight, (0, 2, 3, 1))

    def pooled(total, length, small_part, grad_part):
        hidden, sums, gg = pool(length, total.reshape(2, 3, own, span), small_part, grad_part)
        return hidden, sums, gg.reshape(rows, span)

    if line == 4 and channel_parts == 4:
        done = Order(out_grad)

        def run(function, *operands):
            return done(function(*done(operands)))

        pick_near = jnp.stack([side, place // 2, place % 2]).astype(jnp.int32)
        pick_far = jnp.stack([side, 1 - place // 2, place % 2]).astype(jnp.int32)
        x_own = run(lambda x: mix(x.T, slots), inputs)
        far_got = lax.ppermute(x_own, "mp", chip_pairs)
        pair_got = lax.ppermute(x_own, "dp", pairs)
        near_got = lax.ppermute(x_own, "mp", core_pairs)
        out_grad, done.token = done.token, small_mine
        grads = run(lambda g: mix(g.T, slots), out_grad)
        grads_mine, grads_other = done((half(grads, 0, side), half(grads, 0, other_side)))
        gates, held, w_near = run(
            lambda *given: gates_step(*given, True, 0, None), pick_near, w_rows, x_own, near_got
        )
        cut = width * 2 // 3
        far_own = done(far_got)
        far_got = lax.ppermute(far_own, "mp", core_pairs)
        x_pair = done(pair_got)
        relay = [
            lax.ppermute(x_pair[:cut], "mp", chip_pairs),
            lax.ppermute(jnp.concatenate([far_own[cut:], grads_other], axis=0), "dp", pairs),
        ]
        far_got = done(far_got)
        pair_near_got = lax.ppermute(done(x_pair), "mp", core_pairs)
        far_own, far_got, gates, grads_mine = done((far_own, far_got, gates, grads_mine))
        held = done(held)
        hidden_mine, sums_mine, gg, held, w_far = gates_pool(
            pick_far,
            lengths,
            w_rows,
            far_own,
            far_got,
            gates,
            done.token,
            grads_mine,
            held,
            True,
            0,
            (),
        )
        done.token = sums_mine
        gg, held = done((gg, held))
        pair_far_own, grads_pair = run(
            lambda a, b: (jnp.concatenate([a, b[: width - cut]], axis=0), b[width - cut :]), *relay
        )
        pair_far_got = lax.ppermute(pair_far_own, "mp", core_pairs)
        small_pair = lax.ppermute(done(small_other), "dp", pairs)
        kept = {}

        own_shape, wide_type, sent_type = (width, span), jnp.float32, jnp.bfloat16

        def add(left, right):
            return (left + right.astype(jnp.float32),)

        def add_both(left, right):
            total = left + right.astype(jnp.float32)
            return total, total

        def fill_back(window, part):
            keep, give = run(
                lambda *given: back_products(*given, window),
                pick_near,
                (w_near, w_far)[part].reshape(rows, depth // 2),
                gg.reshape(rows, 2 * span),
            )
            kept["keep", window, part] = keep
            kept["core", window, part] = lax.ppermute(give, "mp", core_pairs)

        def fill_core(window, part):
            kind = wide_type if part == 0 else sent_type
            (kept["sum", window, part],) = run(
                lambda *given: whole(add, [(own_shape, kind)], *given),
                kept["keep", window, part],
                kept["core", window, part],
            )

        def fill_cross(window):
            kept["cross", window] = lax.ppermute(done(kept["sum", window, 1]), "mp", chip_pairs)

        pair_gates, held = run(
            lambda *given: gates_step(*given[:4], False, 1, given[4]),
            pick_near,
            w_rows,
            x_pair,
            pair_near_got,
            held,
        )
        small_pair, grads_pair = done((small_pair, grads_pair))
        length_pair = small_pair[0, 5:6].astype(jnp.int32)
        small_pair = jnp.where(lane[:own] < 3, small_mine, small_pair)
        hidden_pair, sums_pair, gg, held = run(
            lambda *given: gates_pool(*given[:9], False, 1, given[9:]),
            pick_far,
            length_pair,
            w_rows,
            pair_far_own,
            pair_far_got,
            pair_gates,
            small_pair,
            grads_pair,
            held,
            gg,
        )

        size = rows // CHUNKS
        per = own // size

        def products():
            return run(
                lambda gg, x: cols_dot(gg.reshape(rows, 2 * span), x).astype(jnp.bfloat16), gg, held
            )

        def fill_send():
            (give,) = run(
                lambda *given: whole(add, [(own_shape, sent_type)], *given),
                kept["sum", 1, 0],
                kept["cross", 1],
            )
            kept["pair"] = lax.ppermute(give, "dp", pairs)

        def unmixed(total, slots):
            return (
                lax.dot_general(
                    total, slots, (((1,), (1,)), ((), ())), preferred_element_type=jnp.float32
                ),
            )

        def send(name, value):
            kept[name] = lax.ppermute(done(value), "dp", pairs)

        def receive(name):
            kept[name] = done(kept[name])

        def fill_input():
            def total(near_sum, cross, pair, slots):
                total = near_sum + cross.astype(jnp.float32) + pair.astype(jnp.float32)
                return unmixed(total.astype(jnp.bfloat16), slots)

            (total,) = run(
                lambda *given: whole(total, [(own_shape, sent_type)], *given),
                kept["sum", 0, 0],
                kept["cross", 0],
                kept["pair"],
                slots,
            )
            kept["input"] = total.T

        def fill_hidden():
            low, high = done((hidden_mine, kept["hidden"]))
            low, high = jnp.where(is_low, low, high), jnp.where(is_low, high, low)

            def both(low, high, slots):
                return unmixed(jnp.concatenate([low, high], axis=0), slots)

            (total,) = run(
                lambda *given: whole(both, [(own_shape, sent_type)], *given), low, high, slots
            )
            kept["hidden out"] = total.T

        position = lax.axis_index("dp") // 2
        inner = (position == 1) | (position == 2)

        def fill_bias(stage):
            def run_stage():
                if stage == 0:
                    kept["bias"] = run(jnp.add, sums_mine, sums_pair)
                    moves = [(0, 1), (1, 0), (2, 3), (3, 2)]
                elif stage == 1:
                    kept["bias"] = run(jnp.add, kept["bias"], kept["bias got"])
                    moves = [(1, 2), (2, 1)]
                elif stage == 2:
                    kept["bias"] = run(jnp.add, kept["bias"], kept["bias got"])
                    moves = [(1, 0), (2, 3), (0, 1), (3, 2)]
                elif stage == 3:
                    kept["bias"] = run(
                        lambda a, b: jnp.where(inner, a, b), kept["bias"], kept["bias got"]
                    )
                if stage < 3:
                    kept["bias got"] = lax.ppermute(kept["bias"], "dp", line_pairs(moves))
                elif stage == 3:
                    kept["bias got"] = lax.ppermute(kept["bias"], "dp", pairs)
                else:
                    kept["bias got"] = done(kept["bias got"])

            return run_stage

        flags = jnp.stack([side, place // 2]).astype(jnp.int32)
        kept["out"] = None

        swapped = {}

        def arrived(k, finals, got):
            swapped[k] = got
            group = k // per
            members = range(group * per, (group + 1) * per)
            if k == members[-1]:
                parts = done(([finals[m] for m in members], [swapped[m] for m in members]))
                kept["out"] = done(write_chunks(flags, *parts, group, kept["out"], (2 * rows, depth)))

        def fill(*steps):
            def run_all():
                for step, *given in steps:
                    step(*given)

            return run_all

        fill_bias(0)()
        fill_bias(0)()
        fill_bias(0)()
        fill_bias(0)()
        send("sums", sums_pair)
        send("hidden", hidden_pair)
        fill_back(1, 1)
        fill_back(1, 0)
        fill_core(1, 1)
        fill_cross(1)
        fill_bias(1)()
        fill_back(0, 1)
        fill_core(1, 0)
        fill_back(0, 0)
        fill_bias(2)()
        fill_core(0, 1)
        chunks = products()
        fill_core(0, 0)
        receive("sums")
        receive("hidden")
        fill_bias(3)()
        fillers = {
            0: fill((receive, ("cross", 1)), (fill_cross, 0), (fill_bias(4),)),
            1: fill((fill_send,)),
            3: fill((receive, ("cross", 0))),
            4: fill((receive, "pair")),
            CHUNKS + 2: fill((fill_hidden,)),
            CHUNKS + 3: fill((fill_input,)),
        }
        piped_sums(done, chunks, pairs, fillers, arrived)
        input_grad, hidden = kept["input"], kept["hidden out"]
        wgrad = kept["out"].reshape(2, 3, width, depth)
        bias_grad = join(is_low, kept["bias"], kept["bias got"], 0)[:, 2:5].T
        sums_mine, sums_other = done.token, kept["sums"]
    else:
        x_own = mix(inputs.T, slots)
        grads = mix(out_grad.T, slots)
        grads_mine, grads_other = half(grads, 0, side), half(grads, 0, other_side)
        grads_pair = lax.ppermute(grads_other, "dp", pairs)
        small_pair = lax.ppermute(small_other, "dp", pairs)
        length_pair = small_pair[0, 5:6].astype(jnp.int32)
        small_pair = jnp.where(lane[:own] < 3, small_mine, small_pair)
        x_all = lax.all_gather(x_own, "mp", axis=0, tiled=True)
        x_pair = lax.all_gather(lax.ppermute(x_own, "dp", pairs), "mp", axis=0, tiled=True)
        w_mine = half(w_rows, 2, side).reshape(rows, depth)
        w_other = half(w_rows, 2, other_side).reshape(rows, depth)
        hidden_mine, sums_mine, gg_mine = pooled(
            times(w_mine, x_all), lengths, small_mine, grads_mine
        )
        _, sums_pair, gg_pair = pooled(times(w_mine, x_pair), length_pair, small_pair, grads_pair)
        hidden_other, sums_other, gg_other = pooled(
            times(w_other, x_all), lengths, small_other, grads_other
        )
        part = cols_dot(gg_mine, x_all) + cols_dot(gg_pair, x_pair)
        total = line_sum(part.astype(jnp.bfloat16), line)
        theirs = lax.ppermute(total, "dp", pairs)
        shape = (2, 3, own, depth)
        wgrad = join(is_low, total.reshape(shape), theirs.reshape(shape), 2).astype(jnp.float32)
        back = rows_dot(w_mine, gg_mine) + rows_dot(w_other, gg_other)
        input_grad = lax.psum_scatter(
            back.astype(jnp.bfloat16), "mp", scatter_dimension=0, tiled=True
        )
        input_grad = mix(input_grad, slots, back=True).T
        hidden = mix(join(is_low, hidden_mine, hidden_other, 0), slots, back=True).T
        bias_mine = line_sum(sums_mine + sums_pair, line)
        bias_pair = lax.ppermute(bias_mine, "dp", pairs)
        bias_grad = join(is_low, bias_mine, bias_pair, 0)[:, 2:5].T

    sums = join(is_low, sums_mine, sums_other, 0)
    return (
        hidden,
        sums[:, 0:1].T,
        input_grad,
        sums[:, 1:2].T,
        jnp.transpose(wgrad, (0, 3, 1, 2)),
        bias_grad,
    )


def solution(mesh):
    in_specs = (
        P("dp", "mp"),
        P("dp"),
        P("dp", "mp"),
        P(None, None, None, "mp"),
        P(None, "mp"),
        P("dp", "mp"),
        P("dp", "mp"),
    )
    out_specs = (
        P("dp", "mp"),
        P("dp", "mp"),
        P("dp", "mp"),
        P("dp", "mp"),
        P(None, None, None, "mp"),
        P(None, "mp"),
    )
    body = functools.partial(on_device, mesh.shape["dp"] // 2, mesh.shape["mp"])
    return jax.shard_map(
        body, mesh=mesh, in_specs=in_specs, out_specs=out_specs, check_vma=False
    )
```

```python
import functools

import jax
import jax.numpy as jnp
from jax import lax
from jax.experimental import pallas as pl
from jax.experimental.pallas import tpu as pltpu
from jax.sharding import PartitionSpec as P

LANES = 128
ROWS = 16
CHUNKS = 18
PART = 144
LAG = 4
HIDDEN_COST = pl.CostEstimate(flops=1, bytes_accessed=1, transcendentals=0)


def pool_kernel(length_ref, gates_ref, small_ref, grad_ref, hidden_ref, sums_ref, gg_ref, held):
    part, span = grad_ref.shape
    tiles = span // LANES
    length = length_ref[0]
    lane = lax.broadcasted_iota(jnp.int32, (ROWS, LANES), 1)
    zero = jnp.zeros((ROWS, LANES), jnp.float32)
    one = zero + 1.0
    first_lane = lane == 0
    last_lane = lane == LANES - 1
    cand_at, forget_at, out_at = 0, 1, 2
    run_at, back_at, decay_at = 0, 1, 2
    held_gates, held_runs = held

    def tile_of(j):
        return pl.ds(j * LANES, LANES)

    def is_live(j):
        return lane * tiles + j < length

    def local(step, unused):
        rows = pl.ds(pl.multiple_of(step * ROWS, ROWS), ROWS)
        small = small_ref[rows, :]
        bias = [jnp.broadcast_to(small[:, k : k + 1], (ROWS, LANES)) for k in range(3)]
        end_grad = jnp.where(last_lane, jnp.broadcast_to(small[:, 4:5], (ROWS, LANES)), 0.0)
        earlier = [
            jnp.where(first_lane, 0.0, pltpu.roll(gates_ref[1, k, rows, tile_of(tiles - 1)], 1, 1))
            for k in range(3)
        ]
        run, product, back = zero, one, zero
        for j in range(tiles):
            gates = []
            for k in range(3):
                gates.append(gates_ref[0, k, rows, tile_of(j)] + earlier[k] + bias[k])
                earlier[k] = gates_ref[1, k, rows, tile_of(j)]
            live = is_live(j)
            cand = jnp.tanh(gates[0])
            forget = jax.nn.sigmoid(gates[1])
            out_gate = jnp.where(live, 0.5 * jnp.tanh(0.5 * gates[2]) + 0.5, 0.0)
            kept = jnp.where(live, 1.0 - forget, 0.0)
            decay = 1.0 - kept
            emitted = out_gate * grad_ref[rows, tile_of(j)].astype(jnp.float32)
            if j == tiles - 1:
                emitted = emitted + end_grad
            run = decay * run + kept * cand
            product = product * decay
            back = back + product * emitted
            held_gates[cand_at, rows, tile_of(j)] = cand
            held_gates[forget_at, rows, tile_of(j)] = forget
            held_gates[out_at, rows, tile_of(j)] = out_gate
        held_runs[run_at, rows, :] = run
        held_runs[back_at, rows, :] = back
        held_runs[decay_at, rows, :] = product
        return unused

    lax.fori_loop(0, part // ROWS, local, 0)

    wide = lax.broadcasted_iota(jnp.int32, (part, LANES), 1)
    begin = jnp.broadcast_to(small_ref[:, 3:4], (part, LANES))
    run, back, product = held_runs[run_at], held_runs[back_at], held_runs[decay_at]
    run = jnp.where(wide == 0, run + product * begin, run)
    up = product
    for k in (1, 2, 4, 8, 16, 32, 64):
        inside = wide >= k
        run = run + up * jnp.where(inside, pltpu.roll(run, k, 1), 0.0)
        up = up * jnp.where(inside, pltpu.roll(up, k, 1), 1.0)
        inside = wide < LANES - k
        back = back + product * jnp.where(inside, pltpu.roll(back, LANES - k, 1), 0.0)
        product = product * jnp.where(inside, pltpu.roll(product, LANES - k, 1), 1.0)
    held_runs[run_at] = jnp.where(wide == 0, begin, pltpu.roll(run, 1, 1))
    held_runs[decay_at] = jnp.where(wide == LANES - 1, 0.0, pltpu.roll(back, LANES - 1, 1))
    last_cell = jnp.broadcast_to(run[:, LANES - 1 :], (part, LANES))
    sums_ref[...] = jnp.where(wide == 0, last_cell, 0.0) + jnp.where(
        wide == 1, jnp.broadcast_to(back[:, :1], (part, LANES)), 0.0
    )

    def final(step, unused):
        rows = pl.ds(pl.multiple_of(step * ROWS, ROWS), ROWS)
        small = small_ref[rows, :]
        end_grad = jnp.where(last_lane, jnp.broadcast_to(small[:, 4:5], (ROWS, LANES)), 0.0)
        before = held_runs[run_at, rows, :]
        cells, befores = [], []
        for j in range(tiles):
            cand = held_gates[cand_at, rows, tile_of(j)]
            kept = jnp.where(is_live(j), 1.0 - held_gates[forget_at, rows, tile_of(j)], 0.0)
            cell = (1.0 - kept) * before + kept * cand
            befores.append(before)
            cells.append(cell)
            before = cell
        follow = held_runs[decay_at, rows, :]
        bias_sum = [zero] * 3
        for j in range(tiles - 1, -1, -1):
            cand = held_gates[cand_at, rows, tile_of(j)]
            forget = held_gates[forget_at, rows, tile_of(j)]
            out_gate = held_gates[out_at, rows, tile_of(j)]
            kept = jnp.where(is_live(j), 1.0 - forget, 0.0)
            emitted = out_gate * grad_ref[rows, tile_of(j)].astype(jnp.float32)
            hidden_ref[rows, tile_of(j)] = (out_gate * cells[j]).astype(jnp.bfloat16)
            out_part = emitted * cells[j] * (1.0 - out_gate)
            if j == tiles - 1:
                emitted = emitted + end_grad
            cell_grad = emitted + follow
            follow = (1.0 - kept) * cell_grad
            shared = cell_grad * kept
            parts = [
                shared * (1.0 - cand * cand),
                shared * (befores[j] - cand) * forget,
                out_part,
            ]
            for k in range(3):
                rounded = parts[k].astype(jnp.bfloat16)
                gg_ref[0, k, rows, tile_of(j)] = rounded
                wide_part = rounded.astype(jnp.float32)
                bias_sum[k] = bias_sum[k] + wide_part
                if j > 0:
                    gg_ref[1, k, rows, tile_of(j - 1)] = rounded
                else:
                    moved = jnp.where(last_lane, 0.0, pltpu.roll(wide_part, LANES - 1, 1))
                    gg_ref[1, k, rows, tile_of(tiles - 1)] = moved.astype(jnp.bfloat16)
        answer = sums_ref[rows, :]
        for k in range(3):
            total = jnp.sum(bias_sum[k], axis=1, keepdims=True)
            answer = jnp.where(lane == 2 + k, jnp.broadcast_to(total, (ROWS, LANES)), answer)
        sums_ref[rows, :] = answer
        return unused

    lax.fori_loop(0, part // ROWS, final, 0)


def pool(length, gates, small, grad):
    taps, kinds, width, span = gates.shape
    part = next(p for p in (96, 48, 16) if width % p == 0)
    return pl.pallas_call(
        lambda *refs: pool_kernel(*refs[:-2], refs[-2:]),
        grid=(width // part,),
        in_specs=[
            pl.BlockSpec(memory_space=pltpu.SMEM),
            pl.BlockSpec((2, 3, part, span), lambda i: (0, 0, i, 0)),
            pl.BlockSpec((part, LANES), lambda i: (i, 0)),
            pl.BlockSpec((part, span), lambda i: (i, 0)),
        ],
        out_specs=[
            pl.BlockSpec((part, span), lambda i: (i, 0)),
            pl.BlockSpec((part, LANES), lambda i: (i, 0)),
            pl.BlockSpec((2, 3, part, span), lambda i: (0, 0, i, 0)),
        ],
        out_shape=[
            jax.ShapeDtypeStruct((width, span), jnp.bfloat16),
            jax.ShapeDtypeStruct((width, LANES), jnp.float32),
            jax.ShapeDtypeStruct((2, 3, width, span), jnp.bfloat16),
        ],
        scratch_shapes=[
            pltpu.VMEM((3, part, span), jnp.float32),
            pltpu.VMEM((3, part, LANES), jnp.float32),
        ],
        compiler_params=pltpu.CompilerParams(vmem_limit_bytes=40 * 2**20),
        cost_estimate=HIDDEN_COST,
        name="pool",
    )(length, gates, small, grad)


def small_columns(bias, start_cell, cell_grad):
    stacked = jnp.concatenate([bias.astype(jnp.float32), start_cell, cell_grad], axis=0)
    return jnp.pad(stacked.T, ((0, 0), (0, LANES - 5)))


def slot_order(span):
    tiles = span // LANES
    slot = lax.broadcasted_iota(jnp.int32, (span, span), 0)
    place = lax.broadcasted_iota(jnp.int32, (span, span), 1)
    return (place == (slot % tiles) * LANES + slot // tiles).astype(jnp.bfloat16)


def mix(block, order, back=False):
    dims = (((1,), (1 if back else 0,)), ((), ()))
    return lax.dot_general(block, order, dims, preferred_element_type=jnp.float32).astype(jnp.bfloat16)


def times(left, right):
    return jnp.dot(left, right, preferred_element_type=jnp.float32)


def rows_dot(left, right):
    return lax.dot_general(left, right, (((0,), (0,)), ((), ())), preferred_element_type=jnp.float32)


def cols_dot(left, right):
    return lax.dot_general(left, right, (((1,), (1,)), ((), ())), preferred_element_type=jnp.float32)


def once(shape):
    zeros = (0,) * len(shape)
    return pl.BlockSpec(shape, lambda *at: zeros, pipeline_mode=pl.Buffered(1))


def gates_kernel(skip, pick_ref, low_ref, high_ref, w_ref, *refs):
    out_ref, x_ref, *copy_refs = refs[skip:]
    half_rows = low_ref.shape[0]

    @pl.when(pl.program_id(0) == 0)
    def _():
        at = pl.multiple_of(pick_ref[2] * half_rows, 64)
        x_ref[pl.ds(at, half_rows), :] = low_ref[...]
        at = pl.multiple_of((1 - pick_ref[2]) * half_rows, 64)
        x_ref[pl.ds(at, half_rows), :] = high_ref[...]

    kinds, width = w_ref.shape[1:3]
    weights = w_ref[0].reshape(kinds * width, w_ref.shape[3])
    total = jnp.dot(weights, x_ref[...], preferred_element_type=jnp.float32)
    out_ref[...] = total.reshape(out_ref.shape)
    for copy_ref in copy_refs:
        copy_ref[...] = w_ref[...]


def gates_step(pick, w_rows, own, sibling, copy, window, held):
    taps, kinds, width, depth = w_rows.shape
    rows, span = own.shape
    block = lambda last: pl.BlockSpec((1, kinds, width // 2, last), lambda g, p: (g, 0, 0, 0))
    specs = [
        once((rows, span)),
        once((rows, span)),
        pl.BlockSpec((1, kinds, width // 2, 2 * rows), lambda g, p: (g, 0, p[0], p[1])),
    ]
    operands = [own, sibling, w_rows]
    aliases = {}
    if held is not None:
        specs.append(pl.BlockSpec(memory_space=pltpu.HBM))
        operands.append(held)
        aliases = {len(operands): 1}
    out_specs = [block(span), pl.BlockSpec((2 * rows, span), lambda g, p: (0, window))]
    out_shape = [
        jax.ShapeDtypeStruct((taps, kinds, width // 2, span), jnp.float32),
        jax.ShapeDtypeStruct((depth, 2 * span), jnp.bfloat16),
    ]
    if copy:
        out_specs.append(block(2 * rows))
        out_shape.append(jax.ShapeDtypeStruct((taps, kinds, width // 2, 2 * rows), jnp.bfloat16))
    return pl.pallas_call(
        functools.partial(gates_kernel, 0 if held is None else 1),
        grid_spec=pltpu.PrefetchScalarGridSpec(
            num_scalar_prefetch=1,
            grid=(taps,),
            in_specs=specs,
            out_specs=out_specs,
        ),
        out_shape=out_shape,
        input_output_aliases=aliases,
        compiler_params=pltpu.CompilerParams(vmem_limit_bytes=50 * 2**20),
        cost_estimate=HIDDEN_COST,
        name="gates_step",
    )(pick, *operands)


def gates_pool_kernel(skip, pick_ref, length_ref, low_ref, high_ref, w_ref, base_ref, small_ref,
                      grad_ref, *refs):
    hidden_ref, sums_ref, gg_ref, x_ref, *refs = refs[skip:]
    half_rows = low_ref.shape[0]

    @pl.when(pl.program_id(0) == 0)
    def _():
        at = pl.multiple_of(pick_ref[2] * half_rows, 64)
        x_ref[pl.ds(at, half_rows), :] = low_ref[...]
        at = pl.multiple_of((1 - pick_ref[2]) * half_rows, 64)
        x_ref[pl.ds(at, half_rows), :] = high_ref[...]

    gates_ref = refs[-3]
    for copy_ref in refs[:-3]:
        copy_ref[...] = w_ref[...]
    weights = w_ref[...].reshape(-1, w_ref.shape[3])
    product = jnp.dot(weights, x_ref[...], preferred_element_type=jnp.float32)
    gates_ref[...] = product.reshape(gates_ref.shape) + base_ref[...]
    pool_kernel(length_ref, gates_ref, small_ref, grad_ref, hidden_ref, sums_ref, gg_ref, refs[-2:])


def pool_shapes(width, span):
    return [
        jax.ShapeDtypeStruct((width, span), jnp.bfloat16),
        jax.ShapeDtypeStruct((width, LANES), jnp.float32),
        jax.ShapeDtypeStruct((2, 3, width, span), jnp.bfloat16),
    ]


def pool_scratch(part, span):
    return [
        pltpu.VMEM((2, 3, part, span), jnp.float32),
        pltpu.VMEM((3, part, span), jnp.float32),
        pltpu.VMEM((3, part, LANES), jnp.float32),
    ]


def gates_pool(pick, length, w_rows, own, sibling, base, small, grad, held, copy, window, before):
    taps, kinds, width, depth = w_rows.shape
    rows, span = own.shape
    width //= 2
    part = PART
    count = width // part
    lines = lambda columns: pl.BlockSpec((part, columns), lambda i, p: (i, 0))
    wide = pl.BlockSpec((taps, kinds, part, span), lambda i, p: (0, 0, i, 0))
    copy_specs, copy_shapes = [], []
    if copy:
        copy_specs = [pl.BlockSpec((taps, kinds, part, 2 * rows), lambda i, p: (0, 0, i, 0))]
        copy_shapes = [jax.ShapeDtypeStruct((taps, kinds, width, 2 * rows), jnp.bfloat16)]
    return pl.pallas_call(
        functools.partial(gates_pool_kernel, 1 + len(before)),
        grid_spec=pltpu.PrefetchScalarGridSpec(
            num_scalar_prefetch=1,
            grid=(count,),
            in_specs=[
                pl.BlockSpec(memory_space=pltpu.SMEM),
                once((rows, span)),
                once((rows, span)),
                pl.BlockSpec(
                    (taps, kinds, part, 2 * rows), lambda i, p: (0, 0, p[0] * count + i, p[1])
                ),
                wide,
                lines(LANES),
                lines(span),
            ]
            + [pl.BlockSpec(memory_space=pltpu.HBM)] * (1 + len(before)),
            out_specs=[
                lines(span),
                lines(LANES),
                pl.BlockSpec((taps, kinds, part, span), lambda i, p: (0, 0, i, window)),
                pl.BlockSpec((2 * rows, span), lambda i, p: (1, window)),
                *copy_specs,
            ],
            scratch_shapes=pool_scratch(part, span),
        ),
        out_shape=pool_shapes(width, span)[:2]
        + [
            jax.ShapeDtypeStruct((taps, kinds, width, 2 * span), jnp.bfloat16),
            jax.ShapeDtypeStruct((depth, 2 * span), jnp.bfloat16),
        ]
        + copy_shapes,
        input_output_aliases={8: 3, **({9: 2} if before else {})},
        compiler_params=pltpu.CompilerParams(vmem_limit_bytes=50 * 2**20),
        cost_estimate=HIDDEN_COST,
        name="gates_pool",
    )(pick, length, own, sibling, w_rows, base, small, grad, held, *before)


def whole_kernel(function, count, *refs):
    results = function(*[ref[...] for ref in refs[:count]])
    for ref, result in zip(refs[count:], results):
        ref[...] = result.astype(ref.dtype)


def whole(function, outputs, *operands):
    return pl.pallas_call(
        functools.partial(whole_kernel, function, len(operands)),
        out_shape=[jax.ShapeDtypeStruct(*output) for output in outputs],
        compiler_params=pltpu.CompilerParams(vmem_limit_bytes=20 * 2**20),
        cost_estimate=HIDDEN_COST,
        name="whole",
    )(*operands)


def back_kernel(pick_ref, w_ref, gg_ref, keep_ref, give_ref, total_ref):
    step = pl.program_id(0)
    columns = w_ref.shape[1]
    total_ref[pl.ds(pl.multiple_of(step * columns, columns), columns), :] = lax.dot_general(
        w_ref[...], gg_ref[...], (((0,), (0,)), ((), ())), preferred_element_type=jnp.float32
    )

    @pl.when(step == pl.num_programs(0) - 1)
    def _():
        rows = keep_ref.shape[0]
        keep_ref[...] = total_ref[pl.ds(pl.multiple_of(pick_ref[2] * rows, 64), rows), :]
        give_ref[...] = total_ref[
            pl.ds(pl.multiple_of((1 - pick_ref[2]) * rows, 64), rows), :
        ].astype(jnp.bfloat16)


def back_products(pick, weights, gg, window):
    depth, columns = weights.shape
    span = gg.shape[1] // 2
    part = 384
    return pl.pallas_call(
        back_kernel,
        grid_spec=pltpu.PrefetchScalarGridSpec(
            num_scalar_prefetch=1,
            grid=(columns // part,),
            in_specs=[
                pl.BlockSpec((depth, part), lambda i, p: (0, i)),
                pl.BlockSpec(
                    (depth, span), lambda i, p: (0, window), pipeline_mode=pl.Buffered(1)
                ),
            ],
            out_specs=[
                pl.BlockSpec((columns // 2, span), lambda i, p: (0, 0)),
                pl.BlockSpec((columns // 2, span), lambda i, p: (0, 0)),
            ],
            scratch_shapes=[pltpu.VMEM((columns, span), jnp.float32)],
        ),
        out_shape=[
            jax.ShapeDtypeStruct((columns // 2, span), jnp.float32),
            jax.ShapeDtypeStruct((columns // 2, span), jnp.bfloat16),
        ],
        compiler_params=pltpu.CompilerParams(vmem_limit_bytes=44 * 2**20),
        cost_estimate=HIDDEN_COST,
        name="back_products",
    )(pick, weights, gg)


def chunk_kernel(function, inputs, inner_ref, *refs):
    function(inner_ref[0] == 1, *refs[:inputs], *refs[inputs:])


def chunk_step(function, outputs, inner, size, *operands):
    specs, arrays = [pl.BlockSpec(memory_space=pltpu.SMEM)], [inner]
    for operand in operands:
        array, at = operand if isinstance(operand, tuple) else (operand, 0)
        specs.append(pl.BlockSpec((size, array.shape[1]), lambda i, at=at: (at, 0)))
        arrays.append(array)
    depth = arrays[1].shape[1]
    return pl.pallas_call(
        functools.partial(chunk_kernel, function, len(operands)),
        grid=(1,),
        in_specs=specs,
        out_specs=[pl.BlockSpec((size, depth), lambda i: (0, 0))] * outputs,
        out_shape=[jax.ShapeDtypeStruct((size, depth), jnp.bfloat16)] * outputs,
        compiler_params=pltpu.CompilerParams(vmem_limit_bytes=8 * 2**20),
        cost_estimate=HIDDEN_COST,
        name="chunk_step",
    )(*arrays)


def rounded_sum(left_ref, right_ref):
    total = left_ref[...].astype(jnp.float32) + right_ref[...].astype(jnp.float32)
    return total.astype(jnp.bfloat16)


def take_chunk(inner, chunk_ref, out_ref):
    out_ref[...] = chunk_ref[...]


def sum_chunk(inner, chunk_ref, got_ref, sum_ref):
    sum_ref[...] = rounded_sum(chunk_ref, got_ref)


def sum_and_final(inner, chunk_ref, got_ref, total_ref, sum_ref, final_ref):
    sum_ref[...] = rounded_sum(chunk_ref, got_ref)
    final_ref[...] = jnp.where(inner, total_ref[...], got_ref[...])


def total_and_next(inner, sum_ref, got_ref, chunk_ref, total_ref, next_ref):
    total = rounded_sum(sum_ref, got_ref)
    total_ref[...] = total
    next_ref[...] = jnp.where(inner, total, chunk_ref[...])


def final_chunk(inner, got_ref, total_ref, final_ref):
    final_ref[...] = jnp.where(inner, total_ref[...], got_ref[...])


def total_chunk(inner, sum_ref, got_ref, total_ref):
    total_ref[...] = rounded_sum(sum_ref, got_ref)


def even_odd(count):
    return [(i, i ^ 1) for i in range(count)]


def line_pairs(moves):
    return [(2 * a + s, 2 * b + s) for a, b in moves for s in range(2)]


class Order:
    def __init__(self, token):
        self.token = token

    def __call__(self, values):
        values, self.token = lax.optimization_barrier((values, self.token))
        return values


def line_sum(part, length):
    if length & (length - 1) == 0:
        step = 1
        while step < length:
            part = part + lax.ppermute(part, "dp", line_pairs([(i, i ^ step) for i in range(length)]))
            step *= 2
        return part
    total = part
    for _ in range(length - 1):
        part = lax.ppermute(part, "dp", line_pairs([(i, (i + 1) % length) for i in range(length)]))
        total = total + part
    return total


def half(array, axis, which):
    size = array.shape[axis] // 2
    return lax.dynamic_slice_in_dim(array, which * size, size, axis)


def join(low_first, mine, other, axis):
    return jnp.where(
        low_first,
        jnp.concatenate([mine, other], axis=axis),
        jnp.concatenate([other, mine], axis=axis),
    )


def write_kernel(count, flags_ref, *refs):
    out_ref = refs[-1]
    size = refs[0].shape[0]
    middle = refs[0].shape[1] // 2
    mine = flags_ref[0] == pl.program_id(0)
    straight = flags_ref[1] == 0
    for j in range(count):
        at = pl.ds(j * size, size)
        block = jnp.where(mine, refs[j][...], refs[count + j][...]).astype(jnp.float32)
        left, right = block[:, :middle], block[:, middle:]
        out_ref[at, :middle] = jnp.where(straight, left, right)
        out_ref[at, middle:] = jnp.where(straight, right, left)


def write_chunks(flags, mine, theirs, group, whole, shape):
    count = len(mine)
    size, depth = mine[0].shape
    specs = [pl.BlockSpec(memory_space=pltpu.SMEM)]
    specs += [pl.BlockSpec((size, depth), lambda i: (0, 0))] * (2 * count)
    operands = [flags, *mine, *theirs]
    aliases = {}
    if whole is not None:
        specs.append(pl.BlockSpec(memory_space=pl.ANY))
        operands.append(whole)
        aliases = {len(operands) - 1: 0}
    return pl.pallas_call(
        functools.partial(write_kernel, count),
        grid=(2,),
        in_specs=specs,
        out_specs=pl.BlockSpec((count * size, depth), lambda i: (2 * group + i, 0)),
        out_shape=jax.ShapeDtypeStruct(shape, jnp.float32),
        input_output_aliases=aliases,
        compiler_params=pltpu.CompilerParams(vmem_limit_bytes=16 * 2**20),
        cost_estimate=HIDDEN_COST,
        name="write_chunks",
    )(*operands)


def add_times(total, left, right):
    return total + times(left, right)


def add_rounded(left, right):
    return (left.astype(jnp.float32) + right.astype(jnp.float32)).astype(jnp.bfloat16)


def piped_sums(order, chunks, pairs, fillers, arrived):
    position = lax.axis_index("dp") // 2
    inner = (position == 1) | (position == 2)
    flag = inner.astype(jnp.int32).reshape(1)
    edge = line_pairs([(0, 1), (1, 0), (2, 3), (3, 2)])
    middle = line_pairs([(1, 2), (2, 1)])
    sums, totals, finals = {}, {}, {}
    got_edge, got_middle, got_pair = {}, {}, {}
    size = chunks.shape[0] // CHUNKS

    def run(function, outputs, *operands):
        arrays = order(tuple(o[0] if isinstance(o, tuple) else o for o in operands))
        operands = [
            (array, o[1]) if isinstance(o, tuple) else array for array, o in zip(arrays, operands)
        ]
        return order(chunk_step(function, outputs, flag, size, *operands))

    (payload,) = run(take_chunk, 1, (chunks, 0))
    got_edge[0] = lax.ppermute(payload, "dp", edge)
    for n in range(CHUNKS + LAG + 3):
        final = None
        k = n - 1
        if k in got_edge:
            got = got_edge.pop(k)
            if k < CHUNKS and k >= LAG:
                sums[k], final = run(sum_and_final, 2, (chunks, k), got, totals.pop(k - LAG))
            elif k < CHUNKS:
                (sums[k],) = run(sum_chunk, 1, (chunks, k), got)
            else:
                (final,) = run(final_chunk, 1, got, totals.pop(k - LAG))
            if k < CHUNKS:
                got_middle[k] = lax.ppermute(sums[k], "dp", middle)
        k = n - 2
        payload = None
        if k in got_middle:
            got = got_middle.pop(k)
            (totals[k],) = run(total_chunk, 1, sums.pop(k), got)
        k = n + 1 - LAG
        if k in totals and n + 1 < CHUNKS:
            (payload,) = run(final_chunk, 1, (chunks, n + 1), totals[k])
        elif n + 1 < CHUNKS:
            (payload,) = run(take_chunk, 1, (chunks, n + 1))
        elif k in totals:
            payload = totals[k]
        if payload is not None:
            got_edge[n + 1] = lax.ppermute(payload, "dp", edge)
        k = n - 1 - LAG
        if final is not None:
            finals[k] = final
            got_pair[k] = lax.ppermute(final, "dp", pairs)
        k = k - 1
        if k in got_pair:
            arrived(k, finals, order(got_pair.pop(k)))
        if n in fillers:
            fillers[n]()


def on_device(line, channel_parts, inputs, lengths, start_cell, weight, bias, out_grad, cell_grad):
    span, width = inputs.shape
    depth = weight.shape[1]
    own = width // 2
    rows = 6 * own
    side = lax.axis_index("dp") % 2
    other_side = 1 - side
    is_low = side == 0
    pairs = even_odd(2 * line)
    slots = slot_order(span)

    place = lax.axis_index("mp")
    core_low = place % 2 == 0
    near_low = place < 2
    core_pairs = even_odd(channel_parts)
    chip_pairs = [(i, i ^ 2) for i in range(4)]

    def split(array, axis):
        return half(array, axis, place // 2), half(array, axis, 1 - place // 2)

    small = small_columns(bias, start_cell, cell_grad)
    lane = lax.broadcasted_iota(jnp.int32, small.shape, 1)
    small = jnp.where(lane == 5, lengths[0].astype(jnp.float32), small)
    small_mine, small_other = half(small, 0, side), half(small, 0, other_side)
    w_rows = jnp.transpose(weight, (0, 2, 3, 1))

    def pooled(total, length, small_part, grad_part):
        hidden, sums, gg = pool(length, total.reshape(2, 3, own, span), small_part, grad_part)
        return hidden, sums, gg.reshape(rows, span)

    if line == 4 and channel_parts == 4:
        done = Order(out_grad)

        def run(function, *operands):
            return done(function(*done(operands)))

        pick_near = jnp.stack([side, place // 2, place % 2]).astype(jnp.int32)
        pick_far = jnp.stack([side, 1 - place // 2, place % 2]).astype(jnp.int32)
        x_own = run(lambda x: mix(x.T, slots), inputs)
        far_got = lax.ppermute(x_own, "mp", chip_pairs)
        pair_got = lax.ppermute(x_own, "dp", pairs)
        near_got = lax.ppermute(x_own, "mp", core_pairs)
        out_grad, done.token = done.token, small_mine
        grads = run(lambda g: mix(g.T, slots), out_grad)
        grads_mine, grads_other = done((half(grads, 0, side), half(grads, 0, other_side)))
        gates, held, w_near = run(
            lambda *given: gates_step(*given, True, 0, None), pick_near, w_rows, x_own, near_got
        )
        cut = width * 2 // 3
        far_own = done(far_got)
        far_got = lax.ppermute(far_own, "mp", core_pairs)
        x_pair = done(pair_got)
        relay = [
            lax.ppermute(x_pair[:cut], "mp", chip_pairs),
            lax.ppermute(jnp.concatenate([far_own[cut:], grads_other], axis=0), "dp", pairs),
        ]
        far_got = done(far_got)
        pair_near_got = lax.ppermute(done(x_pair), "mp", core_pairs)
        far_own, far_got, gates, grads_mine = done((far_own, far_got, gates, grads_mine))
        held = done(held)
        hidden_mine, sums_mine, gg, held, w_far = gates_pool(
            pick_far,
            lengths,
            w_rows,
            far_own,
            far_got,
            gates,
            done.token,
            grads_mine,
            held,
            True,
            0,
            (),
        )
        done.token = sums_mine
        gg, held = done((gg, held))
        pair_far_own, grads_pair = run(
            lambda a, b: (jnp.concatenate([a, b[: width - cut]], axis=0), b[width - cut :]), *relay
        )
        pair_far_got = lax.ppermute(pair_far_own, "mp", core_pairs)
        small_pair = lax.ppermute(done(small_other), "dp", pairs)
        kept = {}

        own_shape, wide_type, sent_type = (width, span), jnp.float32, jnp.bfloat16

        def add(left, right):
            return (left + right.astype(jnp.float32),)

        def add_both(left, right):
            total = left + right.astype(jnp.float32)
            return total, total

        def fill_back(window, part):
            keep, give = run(
                lambda *given: back_products(*given, window),
                pick_near,
                (w_near, w_far)[part].reshape(rows, depth // 2),
                gg.reshape(rows, 2 * span),
            )
            kept["keep", window, part] = keep
            kept["core", window, part] = lax.ppermute(give, "mp", core_pairs)

        def fill_core(window, part):
            kind = wide_type if part == 0 else sent_type
            (kept["sum", window, part],) = run(
                lambda *given: whole(add, [(own_shape, kind)], *given),
                kept["keep", window, part],
                kept["core", window, part],
            )

        def fill_cross(window):
            kept["cross", window] = lax.ppermute(done(kept["sum", window, 1]), "mp", chip_pairs)

        pair_gates, held = run(
            lambda *given: gates_step(*given[:4], False, 1, given[4]),
            pick_near,
            w_rows,
            x_pair,
            pair_near_got,
            held,
        )
        small_pair, grads_pair = done((small_pair, grads_pair))
        length_pair = small_pair[0, 5:6].astype(jnp.int32)
        small_pair = jnp.where(lane[:own] < 3, small_mine, small_pair)
        hidden_pair, sums_pair, gg, held = run(
            lambda *given: gates_pool(*given[:9], False, 1, given[9:]),
            pick_far,
            length_pair,
            w_rows,
            pair_far_own,
            pair_far_got,
            pair_gates,
            small_pair,
            grads_pair,
            held,
            gg,
        )

        size = rows // CHUNKS
        per = own // size

        def products():
            return run(
                lambda gg, x: cols_dot(gg.reshape(rows, 2 * span), x).astype(jnp.bfloat16), gg, held
            )

        def fill_send():
            (give,) = run(
                lambda *given: whole(add, [(own_shape, sent_type)], *given),
                kept["sum", 1, 0],
                kept["cross", 1],
            )
            kept["pair"] = lax.ppermute(give, "dp", pairs)

        def unmixed(total, slots):
            return (
                lax.dot_general(
                    total, slots, (((1,), (1,)), ((), ())), preferred_element_type=jnp.float32
                ),
            )

        def send(name, value):
            kept[name] = lax.ppermute(done(value), "dp", pairs)

        def receive(name):
            kept[name] = done(kept[name])

        def fill_input():
            def total(near_sum, cross, pair, slots):
                total = near_sum + cross.astype(jnp.float32) + pair.astype(jnp.float32)
                return unmixed(total.astype(jnp.bfloat16), slots)

            (total,) = run(
                lambda *given: whole(total, [(own_shape, sent_type)], *given),
                kept["sum", 0, 0],
                kept["cross", 0],
                kept["pair"],
                slots,
            )
            kept["input"] = total.T

        def fill_hidden():
            low, high = done((hidden_mine, kept["hidden"]))
            low, high = jnp.where(is_low, low, high), jnp.where(is_low, high, low)

            def both(low, high, slots):
                return unmixed(jnp.concatenate([low, high], axis=0), slots)

            (total,) = run(
                lambda *given: whole(both, [(own_shape, sent_type)], *given), low, high, slots
            )
            kept["hidden out"] = total.T

        position = lax.axis_index("dp") // 2
        inner = (position == 1) | (position == 2)

        def fill_bias(stage):
            def run_stage():
                if stage == 0:
                    kept["bias"] = run(jnp.add, sums_mine, sums_pair)
                    moves = [(0, 1), (1, 0), (2, 3), (3, 2)]
                elif stage == 1:
                    kept["bias"] = run(jnp.add, kept["bias"], kept["bias got"])
                    moves = [(1, 2), (2, 1)]
                elif stage == 2:
                    kept["bias"] = run(jnp.add, kept["bias"], kept["bias got"])
                    moves = [(1, 0), (2, 3), (0, 1), (3, 2)]
                elif stage == 3:
                    kept["bias"] = run(
                        lambda a, b: jnp.where(inner, a, b), kept["bias"], kept["bias got"]
                    )
                if stage < 3:
                    kept["bias got"] = lax.ppermute(kept["bias"], "dp", line_pairs(moves))
                elif stage == 3:
                    kept["bias got"] = lax.ppermute(kept["bias"], "dp", pairs)
                else:
                    kept["bias got"] = done(kept["bias got"])

            return run_stage

        flags = jnp.stack([side, place // 2]).astype(jnp.int32)
        kept["out"] = None

        swapped = {}

        def arrived(k, finals, got):
            swapped[k] = got
            group = k // per
            members = range(group * per, (group + 1) * per)
            if k == members[-1]:
                parts = done(([finals[m] for m in members], [swapped[m] for m in members]))
                kept["out"] = done(write_chunks(flags, *parts, group, kept["out"], (2 * rows, depth)))

        def fill(*steps):
            def run_all():
                for step, *given in steps:
                    step(*given)

            return run_all

        fill_bias(0)()
        fill_bias(0)()
        fill_bias(0)()
        fill_bias(0)()
        send("hidden", hidden_pair)
        fill_back(1, 1)
        fill_back(1, 0)
        fill_core(1, 1)
        fill_cross(1)
        fill_bias(1)()
        fill_back(0, 1)
        fill_core(1, 0)
        fill_back(0, 0)
        fill_bias(2)()
        fill_core(0, 1)
        chunks = products()
        fill_core(0, 0)
        receive("hidden")
        fill_bias(3)()
        fillers = {
            0: fill((receive, ("cross", 1)), (fill_cross, 0), (fill_bias(4),)),
            1: fill((fill_send,)),
            3: fill((receive, ("cross", 0))),
            4: fill((receive, "pair")),
            CHUNKS: fill((send, "sums", sums_pair)),
            CHUNKS + 2: fill((fill_hidden,)),
            CHUNKS + 3: fill((fill_input,)),
            CHUNKS + 4: fill((receive, "sums")),
        }
        piped_sums(done, chunks, pairs, fillers, arrived)
        input_grad, hidden = kept["input"], kept["hidden out"]
        wgrad = kept["out"].reshape(2, 3, width, depth)
        bias_grad = join(is_low, kept["bias"], kept["bias got"], 0)[:, 2:5].T
        sums_mine, sums_other = done.token, kept["sums"]
    else:
        x_own = mix(inputs.T, slots)
        grads = mix(out_grad.T, slots)
        grads_mine, grads_other = half(grads, 0, side), half(grads, 0, other_side)
        grads_pair = lax.ppermute(grads_other, "dp", pairs)
        small_pair = lax.ppermute(small_other, "dp", pairs)
        length_pair = small_pair[0, 5:6].astype(jnp.int32)
        small_pair = jnp.where(lane[:own] < 3, small_mine, small_pair)
        x_all = lax.all_gather(x_own, "mp", axis=0, tiled=True)
        x_pair = lax.all_gather(lax.ppermute(x_own, "dp", pairs), "mp", axis=0, tiled=True)
        w_mine = half(w_rows, 2, side).reshape(rows, depth)
        w_other = half(w_rows, 2, other_side).reshape(rows, depth)
        hidden_mine, sums_mine, gg_mine = pooled(
            times(w_mine, x_all), lengths, small_mine, grads_mine
        )
        _, sums_pair, gg_pair = pooled(times(w_mine, x_pair), length_pair, small_pair, grads_pair)
        hidden_other, sums_other, gg_other = pooled(
            times(w_other, x_all), lengths, small_other, grads_other
        )
        part = cols_dot(gg_mine, x_all) + cols_dot(gg_pair, x_pair)
        total = line_sum(part.astype(jnp.bfloat16), line)
        theirs = lax.ppermute(total, "dp", pairs)
        shape = (2, 3, own, depth)
        wgrad = join(is_low, total.reshape(shape), theirs.reshape(shape), 2).astype(jnp.float32)
        back = rows_dot(w_mine, gg_mine) + rows_dot(w_other, gg_other)
        input_grad = lax.psum_scatter(
            back.astype(jnp.bfloat16), "mp", scatter_dimension=0, tiled=True
        )
        input_grad = mix(input_grad, slots, back=True).T
        hidden = mix(join(is_low, hidden_mine, hidden_other, 0), slots, back=True).T
        bias_mine = line_sum(sums_mine + sums_pair, line)
        bias_pair = lax.ppermute(bias_mine, "dp", pairs)
        bias_grad = join(is_low, bias_mine, bias_pair, 0)[:, 2:5].T

    sums = join(is_low, sums_mine, sums_other, 0)
    return (
        hidden,
        sums[:, 0:1].T,
        input_grad,
        sums[:, 1:2].T,
        jnp.transpose(wgrad, (0, 3, 1, 2)),
        bias_grad,
    )


def solution(mesh):
    in_specs = (
        P("dp", "mp"),
        P("dp"),
        P("dp", "mp"),
        P(None, None, None, "mp"),
        P(None, "mp"),
        P("dp", "mp"),
        P("dp", "mp"),
    )
    out_specs = (
        P("dp", "mp"),
        P("dp", "mp"),
        P("dp", "mp"),
        P("dp", "mp"),
        P(None, None, None, "mp"),
        P(None, "mp"),
    )
    body = functools.partial(on_device, mesh.shape["dp"] // 2, mesh.shape["mp"])
    return jax.shard_map(
        body, mesh=mesh, in_specs=in_specs, out_specs=out_specs, check_vma=False
    )
```
